32 devices in a mesh: ens: 2 (over x), mode: 16 (over z, y, core).
Axes of the slice: x: 2, y: 2, z: 4, core: 2. Of those that a mesh axis runs over, the one named last changes fastest.
Arguments:
- velocity: float32 [6, 512, 2048], P('ens', 'mode'), parts along dimension 0, may hold values from -4 to 4
- log_conf: float32 [12, 512, 2048], P('ens', 'mode'), parts along dimension 0, may hold values from -3 to 3
- orientation: int32 [32], replicated, may hold values from 0 to 7
- wall_speed: float32 [2], P('ens'), parts along dimension 0, may hold values from 0.5 to 2
Outputs:
- vel_next: float32 [6, 512, 2048], P('ens', 'mode'), parts along dimension 0
- logc_next: float32 [12, 512, 2048], P('ens', 'mode'), parts along dimension 0
The draws below stay inside these ranges and needn't reach their ends.
There are 2 independent parts, one for each index of `ens`. The reference program is written for one: setup_inputs(seed, part) draws one part's arguments, and reference() takes and returns one part's arrays. A program takes and returns all parts, laid end to end along the dimension named above; an argument that names none is the same for every part. Nothing has to cross between parts.
Inputs may be any that keep to these rules, and one draw needn't show every extreme that they name: orientation[e] is the storage code of element e as in the reference program; elements take the eight codes independently.
All inputs are finite; a program needn't handle non-finite values.
Results may differ from the reference program's by a relative error of at most 0.0003.
Values sent between devices are 32-bit elements; how exact they have to be, the bound alone decides.
A program may use at most 512 MiB of HBM per device.

```python
import jax
import jax.numpy as jnp
import numpy as np
from jax import lax

NODE_1D = 8
CYCLES = 2
LAYERS_DEV = 1
MODES = 512
ELEMS = 32
NODES = 2048
N_MODE = 16


def touch_ends(entries, own_key, smallest, high):
    shape = entries.shape
    place = [jax.random.randint(jax.random.fold_in(own_key, axis), (), 0, shape[axis]) for axis in range(len(shape))]
    entries = entries.at[tuple(place)].set(smallest)
    longest = shape.index(max(shape))
    place[longest] = (place[longest] + 1) % shape[longest]
    return entries.at[tuple(place)].set(high)


def shard_levels(own_key, dims, shards, smallest, top_value):
    factor_of = 1.0
    for dim, blocks in shards:
        draws = jax.random.uniform(jax.random.fold_in(jax.random.fold_in(own_key, 6), dim), (blocks,), jnp.float32, smallest / len(shards), top_value / len(shards))
        factor_of = factor_of * jnp.repeat(jnp.exp(draws), dims[dim] // blocks).reshape((-1,) + (1,) * (len(dims) - 1 - dim))
    return factor_of


def scatter_about(own_key, extent, scale, most, shards=(), kind=jnp.bfloat16):
    level = shard_levels(own_key, extent, shards, -0.22, 0.18) if shards else 1.0
    entries = jax.random.normal(own_key, extent, jnp.float32) * scale * level
    return jnp.minimum(jnp.maximum(entries, -most), most).astype(kind)


def setup_inputs(seed: int = 0, part: int = 0) -> dict:
    streams_of = jax.random.split(jax.random.key(seed), 5)
    own_keys = jax.random.split(jax.random.fold_in(streams_of[4], part), 5)
    return {
        "velocity": scatter_about(own_keys[0], (3, MODES, NODES), 0.6, 4.0, ((1, 16),), jnp.float32),
        "log_conf": scatter_about(own_keys[1], (6, MODES, NODES), 0.4, 3.0, ((1, 16),), jnp.float32),
        "orientation": touch_ends(jax.random.randint(streams_of[2], (ELEMS,), 0, 8), jax.random.fold_in(streams_of[2], 1), 0, 7).astype(jnp.int32),
        "wall_speed": jnp.clip(jax.random.uniform(own_keys[3], (1,), jnp.float32, 0.5, 2.0), 0.5, 2.0),
    }


STEP_DT = 0.002
RELAX_TIME = 0.02
MOBILITY = 0.3
LAYER_HEIGHT = 0.25
R_INNER = 1.0
HIGHEST = lax.Precision.HIGHEST
PAIRS = ((0, 0), (0, 1), (0, 2), (1, 1), (1, 2), (2, 2))

def cheb_table(points):
    nodes_xi = -np.cos(np.pi * np.arange(points) / (points - 1))
    weights = np.ones(points)
    weights[0] = 2.0
    weights[-1] = 2.0
    weights = weights * (-1.0) ** np.arange(points)
    identity = np.eye(points)
    spacing = nodes_xi[:, None] - nodes_xi[None, :] + identity
    matrix = weights[:, None] / weights[None, :] / spacing
    matrix = matrix * (1.0 - identity)
    matrix = matrix - identity * matrix.sum(axis=1)[:, None]
    return (nodes_xi, matrix)

def cycle_radius(cycle_count, side_pts):
    nodes_xi, matrix = cheb_table(side_pts)
    radius = R_INNER + (np.arange(cycle_count)[:, None] + (nodes_xi[None, :] + 1.0) / 2.0) / cycle_count
    return (jnp.asarray(radius.reshape(-1, 1), dtype=jnp.float32), matrix)

def fourier_basis(planes):
    plane_ids = jnp.arange(planes, dtype=jnp.int32)
    pair_ids = jnp.arange(planes // 2, dtype=jnp.int32)
    phase_ids = plane_ids[:, None] * pair_ids[None, :] % planes
    angles = phase_ids.astype(jnp.float32) * (2.0 * np.pi / planes)
    norm_scale = np.sqrt(2.0 / planes)
    cosine = jnp.cos(angles) * norm_scale
    sine_part = jnp.sin(angles) * norm_scale
    mean_col = jnp.full((planes,), 1.0 / np.sqrt(planes), jnp.float32)
    nyquist = jnp.where(plane_ids % 2 == 0, 1.0, -1.0).astype(jnp.float32) / np.sqrt(planes)
    cosine = cosine.at[:, 0].set(mean_col)
    sine_part = sine_part.at[:, 0].set(nyquist)
    return jnp.stack([cosine, sine_part], axis=2).reshape(planes, planes)

def theta_deriv(coeffs, coef_axis, pair_start):
    shape_in = coeffs.shape
    blocked = coeffs.reshape(shape_in[:coef_axis] + (shape_in[coef_axis] // 2, 2) + shape_in[coef_axis + 1:])
    cos_part = lax.index_in_dim(blocked, 0, coef_axis + 1, keepdims=False)
    sin_part = lax.index_in_dim(blocked, 1, coef_axis + 1, keepdims=False)
    wavenums = (pair_start + jnp.arange(shape_in[coef_axis] // 2, dtype=jnp.int32)).astype(jnp.float32)
    wavenums = wavenums.reshape((-1,) + (1,) * (len(shape_in) - coef_axis - 1))
    return jnp.stack([wavenums * sin_part, -wavenums * cos_part], axis=coef_axis + 1).reshape(shape_in)

def grid_to_stored(orient_block, layers, cycle_count, side_pts):
    layer_ids = jnp.arange(layers, dtype=jnp.int32)[:, None, None, None]
    row_ids = jnp.arange(side_pts, dtype=jnp.int32)[None, :, None, None]
    cycle_ids = jnp.arange(cycle_count, dtype=jnp.int32)[None, None, :, None]
    col_ids = jnp.arange(side_pts, dtype=jnp.int32)[None, None, None, :]
    element = layer_ids * cycle_count + cycle_ids
    orient = orient_block.reshape(layers, cycle_count)[:, None, :, None]
    swapped = orient // 4 % 2 == 1
    leading = jnp.where(swapped, col_ids, row_ids)
    trailing = jnp.where(swapped, row_ids, col_ids)
    leading = jnp.where(orient % 2 == 1, side_pts - 1 - leading, leading)
    trailing = jnp.where(orient // 2 % 2 == 1, side_pts - 1 - trailing, trailing)
    return (element * side_pts * side_pts + leading * side_pts + trailing).reshape(-1)

def stored_coords(orient_block, layers, cycle_count, side_pts):
    layer_ids = jnp.arange(layers, dtype=jnp.int32)[:, None, None, None]
    cycle_ids = jnp.arange(cycle_count, dtype=jnp.int32)[None, :, None, None]
    lead_ids = jnp.arange(side_pts, dtype=jnp.int32)[None, None, :, None]
    trail_ids = jnp.arange(side_pts, dtype=jnp.int32)[None, None, None, :]
    orient = orient_block.reshape(layers, cycle_count)[:, :, None, None]
    lead_ids = jnp.where(orient % 2 == 1, side_pts - 1 - lead_ids, lead_ids)
    trail_ids = jnp.where(orient // 2 % 2 == 1, side_pts - 1 - trail_ids, trail_ids)
    swapped = orient // 4 % 2 == 1
    row_ids = jnp.where(swapped, trail_ids, lead_ids)
    col_ids = jnp.where(swapped, lead_ids, trail_ids)
    position = (layer_ids * side_pts + row_ids) * (cycle_count * side_pts) + cycle_ids * side_pts + col_ids
    inner_wall = jnp.logical_and(cycle_ids == 0, col_ids == 0)
    outer_wall = jnp.logical_and(cycle_ids == cycle_count - 1, col_ids == side_pts - 1)
    full_shape = position.shape
    return (position.reshape(-1), jnp.broadcast_to(inner_wall, full_shape).reshape(-1), jnp.broadcast_to(outer_wall, full_shape).reshape(-1))

def point_sum(blocked, deriv_mat, axis_at, factor):
    axis_pos = axis_at % blocked.ndim
    count = blocked.shape[axis_pos]
    pieces = [lax.index_in_dim(blocked, point, axis_pos, keepdims=False) for point in range(count)]
    rows_out = []
    for target in range(count):
        total = pieces[0] * float(deriv_mat[target][0] * factor)
        for point in range(1, count):
            total = total + pieces[point] * float(deriv_mat[target][point] * factor)
        rows_out.append(total)
    return jnp.stack(rows_out, axis=axis_pos)

def radial_deriv(values, deriv_mat, cycle_count, side_pts):
    shape_in = values.shape
    blocked = values.reshape(shape_in[:-2] + (cycle_count, side_pts, shape_in[-1]))
    return point_sum(blocked, deriv_mat, -2, 2.0 * cycle_count).reshape(shape_in)

def axial_deriv(values, deriv_mat, side_pts):
    shape_in = values.shape
    blocked = values.reshape(shape_in[:-3] + (shape_in[-3] // side_pts, side_pts) + shape_in[-2:])
    return point_sum(blocked, deriv_mat, -3, 2.0 / LAYER_HEIGHT).reshape(shape_in)

def radial_average(values, cycle_count, side_pts):
    shape_in = values.shape
    blocked = values.reshape(shape_in[:-2] + (cycle_count, side_pts, shape_in[-1]))
    left_face = blocked[..., :, 0, :]
    right_face = blocked[..., :, side_pts - 1, :]
    face_mean = 0.5 * (right_face[..., :-1, :] + left_face[..., 1:, :])
    left_face = jnp.concatenate([left_face[..., :1, :], face_mean], axis=-2)
    right_face = jnp.concatenate([face_mean, right_face[..., -1:, :]], axis=-2)
    joined = jnp.concatenate([left_face[..., None, :], blocked[..., 1:side_pts - 1, :], right_face[..., None, :]], axis=-2)
    return joined.reshape(shape_in)

def axial_average(values, below_row, above_row, side_pts):
    shape_in = values.shape
    blocked = values.reshape(shape_in[:-3] + (shape_in[-3] // side_pts, side_pts) + shape_in[-2:])
    bottom = blocked[..., :, 0, :, :]
    top_face = blocked[..., :, side_pts - 1, :, :]
    next_bottom = jnp.concatenate([bottom[..., 1:, :, :], above_row[..., None, :, :]], axis=-3)
    prev_top = jnp.concatenate([below_row[..., None, :, :], top_face[..., :-1, :, :]], axis=-3)
    bottom = 0.5 * (bottom + prev_top)
    top_face = 0.5 * (top_face + next_bottom)
    joined = jnp.concatenate([bottom[..., :, None, :, :], blocked[..., :, 1:side_pts - 1, :, :], top_face[..., :, None, :, :]], axis=-3)
    return joined.reshape(shape_in)

def sym_full(components):
    return [[components[0], components[1], components[2]], [components[1], components[3], components[4]], [components[2], components[4], components[5]]]

def mat_prod(first_mat, second_mat):
    return [[first_mat[row_at][0] * second_mat[0][col_at] + first_mat[row_at][1] * second_mat[1][col_at] + first_mat[row_at][2] * second_mat[2][col_at] for col_at in range(3)] for row_at in range(3)]

def add_diag(matrix, offset):
    return [[matrix[row_at][col_at] + offset if row_at == col_at else matrix[row_at][col_at] for col_at in range(3)] for row_at in range(3)]

def mat_scale(matrix, factor):
    return [[matrix[row_at][col_at] * factor for col_at in range(3)] for row_at in range(3)]

def mat_exp(components):
    scaled = sym_full([member * 0.125 for member in components])
    series = add_diag(mat_scale(scaled, 0.25), 1.0)
    for degree in (3.0, 2.0):
        series = add_diag(mat_scale(mat_prod(scaled, series), 1.0 / degree), 1.0)
    series = add_diag(mat_prod(scaled, series), 1.0)
    for repeat in range(3):
        series = mat_prod(series, series)
    return series

def velocity_grad(velocity, velocity_dth, radius, deriv_mat, cycle_count, side_pts):
    inv_r = 1.0 / radius
    d_radial = radial_deriv(velocity, deriv_mat, cycle_count, side_pts)
    d_axial = axial_deriv(velocity, deriv_mat, side_pts)
    angular = velocity_dth * inv_r
    components = [d_radial[0], angular[0] - velocity[1] * inv_r, d_axial[0], d_radial[1], angular[1] + velocity[0] * inv_r, d_axial[1], d_radial[2], angular[2], d_axial[2]]
    return jnp.stack(components, axis=0)

def tendencies(velocity, logconf, logconf_dth, grad_proj, radius, deriv_mat, cycle_count, side_pts):
    inv_r = 1.0 / radius
    grad_mat = [[grad_proj[3 * row_at + col_at] for col_at in range(3)] for row_at in range(3)]
    members = [logconf[member] for member in range(6)]
    logc_mat = sym_full(members)
    conform = mat_exp(members)
    inverse = mat_exp([-member for member in members])
    d_radial = radial_deriv(logconf, deriv_mat, cycle_count, side_pts)
    d_axial = axial_deriv(logconf, deriv_mat, side_pts)
    hoop_rate = velocity[1] * inv_r
    curvature = [-2.0 * members[1], members[0] - members[3], -members[4], 2.0 * members[1], members[2]]
    spin_mat = [[0.5 * (grad_mat[row_at][col_at] - grad_mat[col_at][row_at]) for col_at in range(3)] for row_at in range(3)]
    rotate_a = mat_prod(spin_mat, logc_mat)
    rotate_b = mat_prod(logc_mat, spin_mat)
    new_logc = []
    stress = []
    for member, (row_at, col_at) in enumerate(PAIRS):
        unit_diag = 1.0 if row_at == col_at else 0.0
        advect = velocity[0] * d_radial[member] + hoop_rate * logconf_dth[member] + velocity[2] * d_axial[member]
        relaxing = -(1.0 / RELAX_TIME) * (unit_diag - inverse[row_at][col_at] + MOBILITY * (conform[row_at][col_at] - 2.0 * unit_diag + inverse[row_at][col_at]))
        tendency = -advect + (rotate_a[row_at][col_at] - rotate_b[row_at][col_at]) + (grad_mat[row_at][col_at] + grad_mat[col_at][row_at]) + relaxing
        if member < 5:
            tendency = tendency - hoop_rate * curvature[member]
        new_logc.append(tendency)
        stress.append(conform[row_at][col_at] - unit_diag)
    stress_arr = jnp.stack(stress, axis=0)
    stress_dr = radial_deriv(stress_arr, deriv_mat, cycle_count, side_pts)
    stress_dz = axial_deriv(stress_arr, deriv_mat, side_pts)
    convect = [grad_mat[row_at][0] * velocity[0] + grad_mat[row_at][1] * velocity[1] + grad_mat[row_at][2] * velocity[2] for row_at in range(3)]
    mom_r = -convect[0] + stress_dr[0] + stress_dz[2] + (stress[0] - stress[3]) * inv_r
    mom_t = -convect[1] + stress_dr[1] + stress_dz[4] + 2.0 * stress[1] * inv_r
    mom_z = -convect[2] + stress_dr[2] + stress_dz[5] + stress[2] * inv_r
    hoop_terms = [stress[1] * inv_r, stress[3] * inv_r, stress[4] * inv_r]
    return jnp.stack([mom_r, mom_t, mom_z] + new_logc + hoop_terms, axis=0)

def to_planes(coeffs, fourier, grid_index, layers, cycle_count, side_pts):
    values = jnp.einsum('fcm,pc->fmp', coeffs, fourier, precision=HIGHEST)
    values = jnp.take(values, grid_index, axis=1)
    return values.reshape(coeffs.shape[0], layers * side_pts, cycle_count * side_pts, coeffs.shape[1])

def to_coeffs(rate_grid, fourier, back_index):
    flattened = jnp.take(rate_grid.reshape(rate_grid.shape[0], -1, rate_grid.shape[-1]), back_index, axis=1)
    coeffs = jnp.einsum('fmp,pc->fcm', flattened, fourier, precision=HIGHEST)
    return jnp.concatenate([coeffs[0:3] + theta_deriv(coeffs[9:12], 1, 0), coeffs[3:9]], axis=0)

def finish_step(velocity, log_conf, rates, orientation, wall_speed, coef_ids, layers_all, cycle_count, side_pts):
    unused, inner_wall, outer_wall = stored_coords(orientation, layers_all, cycle_count, side_pts)
    on_wall = jnp.logical_or(inner_wall, outer_wall)[None, :]
    stepped = velocity + STEP_DT * rates[0:3]
    driven = jnp.where(jnp.logical_and(inner_wall[None, :], (coef_ids == 0)[:, None]), wall_speed[0], 0.0)
    radial_u = jnp.where(on_wall, 0.0, stepped[0])
    azimuth_u = jnp.where(on_wall, driven, stepped[1])
    axial_u = jnp.where(on_wall, 0.0, stepped[2])
    vel_next = jnp.stack([radial_u, azimuth_u, axial_u], axis=0)
    logc_next = log_conf + STEP_DT * rates[3:9]
    return (vel_next, logc_next)

def reference(velocity, log_conf, orientation, wall_speed):
    side_pts = NODE_1D
    cycle_count = CYCLES
    layers = LAYERS_DEV
    blocks = N_MODE
    planes = MODES
    block_nodes = layers * cycle_count * side_pts * side_pts
    radius, deriv_mat = cycle_radius(cycle_count, side_pts)
    fourier = fourier_basis(planes)
    orient_blocks = orientation.reshape(blocks, layers * cycle_count)
    vel_blocks = velocity.reshape(3, planes, blocks, block_nodes).transpose(2, 0, 1, 3)
    logc_blocks = log_conf.reshape(6, planes, blocks, block_nodes).transpose(2, 0, 1, 3)

    def planes_of(vel_c, logc_c, orient):
        grid_index = grid_to_stored(orient, layers, cycle_count, side_pts)
        coeffs = jnp.concatenate([vel_c, theta_deriv(vel_c, 1, 0), logc_c, theta_deriv(logc_c, 1, 0)], axis=0)
        return to_planes(coeffs, fourier, grid_index, layers, cycle_count, side_pts)

    def grad_mean(values):
        raw_grad = velocity_grad(values[0:3], values[3:6], radius, deriv_mat, cycle_count, side_pts)
        return radial_average(raw_grad, cycle_count, side_pts)

    def grad_faces(operands):
        radial_mean = grad_mean(planes_of(operands[0], operands[1], operands[2]))
        return jnp.stack([radial_mean[:, 0], radial_mean[:, -1]], axis=0)
    faces_one = lax.map(grad_faces, (vel_blocks, logc_blocks, orient_blocks))
    below_one = jnp.roll(faces_one[:, 1], 1, axis=0)
    above_one = jnp.roll(faces_one[:, 0], -1, axis=0)

    def combined_rates(operands):
        values = planes_of(operands[0], operands[1], operands[2])
        grad_proj = axial_average(grad_mean(values), operands[3], operands[4], side_pts)
        rate_phys = tendencies(values[0:3], values[6:12], values[12:18], grad_proj, radius, deriv_mat, cycle_count, side_pts)
        return radial_average(rate_phys, cycle_count, side_pts)

    def rate_faces(operands):
        radial_mean = combined_rates(operands)
        return jnp.stack([radial_mean[:, 0], radial_mean[:, -1]], axis=0)
    faces_two = lax.map(rate_faces, (vel_blocks, logc_blocks, orient_blocks, below_one, above_one))
    below_two = jnp.roll(faces_two[:, 1], 1, axis=0)
    above_two = jnp.roll(faces_two[:, 0], -1, axis=0)

    def block_rates(operands):
        rate_grid = axial_average(combined_rates(operands[0:5]), operands[5], operands[6], side_pts)
        back_index = stored_coords(operands[2], layers, cycle_count, side_pts)[0]
        return to_coeffs(rate_grid, fourier, back_index)
    rates_all = lax.map(block_rates, (vel_blocks, logc_blocks, orient_blocks, below_one, above_one, below_two, above_two))
    rates_all = rates_all.transpose(1, 2, 0, 3).reshape(9, planes, blocks * block_nodes)
    coef_ids = jnp.arange(planes, dtype=jnp.int32)
    return finish_step(velocity, log_conf, rates_all, orientation, wall_speed, coef_ids, layers * blocks, cycle_count, side_pts)
```

```python
import functools

import jax
import jax.numpy as jnp
import ml_dtypes
import numpy as np
from jax import lax
from jax.experimental import pallas as pl
from jax.experimental.pallas import tpu as pltpu
from jax.sharding import PartitionSpec as P

NODE_1D = 8
CYCLES = 2
PLANES = 512
CELL = NODE_1D * NODE_1D
LANES = CYCLES * CELL
KEPT = CELL - NODE_1D
SLOT_OF = (0, 1, 2, 4, 5, 6, 7, 8, 3)
STEP_DT = 0.002
RELAX_TIME = 0.02
MOBILITY = 0.3
LAYER_HEIGHT = 0.25
R_INNER = 1.0
ROWS = 16
BF = jnp.bfloat16
F32 = jnp.float32
MESH = pl.DeviceIdType.MESH


def cheb_table(points):
    nodes_xi = -np.cos(np.pi * np.arange(points) / (points - 1))
    weights = np.ones(points)
    weights[0] = 2.0
    weights[-1] = 2.0
    weights = weights * (-1.0) ** np.arange(points)
    identity = np.eye(points)
    spacing = nodes_xi[:, None] - nodes_xi[None, :] + identity
    matrix = weights[:, None] / weights[None, :] / spacing
    matrix = matrix * (1.0 - identity)
    matrix = matrix - identity * matrix.sum(axis=1)[:, None]
    return (nodes_xi, matrix)


def halves(table):
    high = np.asarray(table, np.float32).astype(ml_dtypes.bfloat16)
    low = (np.asarray(table, np.float64) - high.astype(np.float64)).astype(ml_dtypes.bfloat16)
    return high, low


def tables():
    n = np.arange(PLANES)
    k = np.arange(PLANES // 2)
    angle = (n[:, None] * k[None, :] % PLANES) * (2.0 * np.pi / PLANES)
    cosine = np.cos(angle) * np.sqrt(2.0 / PLANES)
    sine = np.sin(angle) * np.sqrt(2.0 / PLANES)
    cosine[:, 0] = PLANES**-0.5
    sine[:, 0] = (-1.0) ** n * PLANES**-0.5
    basis = np.stack([cosine, sine], axis=2).reshape(PLANES, PLANES)
    dbasis = np.stack([-k * sine, k * cosine], axis=2).reshape(PLANES, PLANES)
    forward = np.concatenate([basis, dbasis], axis=0)
    backward = np.concatenate([basis.T, -dbasis.T], axis=1)

    xi, matrix = cheb_table(NODE_1D)
    eye, eyes = np.eye(NODE_1D), np.eye(CYCLES)
    cell_r = np.kron(matrix.T * (2.0 * CYCLES), eye)
    cell_z = np.kron(eye, matrix.T * (2.0 / LAYER_HEIGHT))
    d_r, d_z = np.kron(eyes, cell_r), np.kron(eyes, cell_z)
    mean = np.eye(CYCLES * NODE_1D)
    for c in range(1, CYCLES):
        i = c * NODE_1D
        mean[i - 1 : i + 1, i - 1 : i + 1] = 0.5
    mean = np.kron(mean, eye)
    weight = np.ones(NODE_1D)
    weight[0] = weight[-1] = 0.5
    weight = np.tile(weight, CYCLES * NODE_1D)
    mean_w = mean * weight[None, :]
    both = np.concatenate([d_r, d_z], axis=1)
    grad = np.concatenate([d_r @ mean_w, d_z @ mean_w], axis=1)
    div = np.kron(np.eye(2), np.concatenate([cell_r, cell_z], axis=0))
    return (
        *halves(forward),
        *halves(backward),
        np.concatenate([*halves(both), *halves(grad), mean_w.astype(ml_dtypes.bfloat16)], axis=1),
        np.concatenate(halves(div), axis=1),
    )


def inverse_radius(lane):
    xi, _ = cheb_table(NODE_1D)
    radius = R_INNER + (np.arange(CYCLES)[:, None] + (xi[None, :] + 1.0) / 2.0) / CYCLES
    total = jnp.zeros(lane.shape, F32)
    for i, r in enumerate(radius.reshape(-1)):
        total = jnp.where(lane // NODE_1D == i, float(1.0 / r), total)
    return total


def split(x):
    high = x.astype(BF)
    return high, (x - high.astype(F32)).astype(BF)


def dot(a, b):
    return jnp.dot(a, b, preferred_element_type=F32)


def dot3(ah, al, bh, bl):
    return dot(ah, bh) + (dot(ah, bl) + dot(al, bh))


def stored_of_grid(o, grid):
    side = NODE_1D
    y = grid % side
    x = grid // side % side
    swapped = o // 4 % 2 == 1
    a = jnp.where(swapped, x, y)
    b = jnp.where(swapped, y, x)
    a = jnp.where(o % 2 == 1, side - 1 - a, a)
    b = jnp.where(o // 2 % 2 == 1, side - 1 - b, b)
    return a * side + b


def stored_index(orient_ref, layer, grid):
    cycle = grid // CELL
    place = jnp.zeros_like(grid)
    for c in range(CYCLES):
        o = orient_ref[layer * CYCLES + c]
        place = jnp.where(cycle == c, c * CELL + stored_of_grid(o, grid), place)
    return place


def square(m):
    a, b, c, d, e, f = m
    bb, cc, ee = b * b, c * c, e * e
    return (
        a * a + bb + cc,
        b * (a + d) + c * e,
        c * (a + f) + b * e,
        bb + d * d + ee,
        e * (d + f) + b * c,
        cc + ee + f * f,
    )


def product(m, n):
    a, b, c, d, e, f = m
    p, q, r, s, t, u = n
    return (
        a * p + b * q + c * r,
        a * q + b * s + c * t,
        a * r + b * t + c * u,
        b * q + d * s + e * t,
        b * r + d * t + e * u,
        c * r + e * t + f * u,
    )


def exponentials(psi):
    x = tuple(v * 0.125 for v in psi)
    x2 = square(x)
    x3 = product(x, x2)
    x4 = square(x2)
    even = [x2[i] * 0.5 + x4[i] * (1.0 / 24.0) for i in range(6)]
    for i in (0, 3, 5):
        even[i] = even[i] + 1.0
    odd = [x[i] + x3[i] * (1.0 / 6.0) for i in range(6)]
    plus = tuple(even[i] + odd[i] for i in range(6))
    minus = tuple(even[i] - odd[i] for i in range(6))
    for _ in range(3):
        plus, minus = square(plus), square(minus)
    return plus, minus


def field(ref, f, rows=slice(None)):
    return ref[rows, f * LANES : (f + 1) * LANES]


def main_kernel(
    n_dev, modes, fold,
    vel_ref, logc_ref, orient_ref, fh_in, fl_in, bh_in, bl_in, node_in, div_in,
    out0_ref, out1_ref,
    fh_ref, fl_ref, bh_ref, bl_ref, node_ref, div_ref,
    raw, packed, xv, xp, xh, xl, ph, pw, vv, vp, dp, proj, face_out, face_in, conv, mom, sth, stl, rh, rl,
    kept, back0, back1,
    local_sem, const_sem, vs_sem, vr_sem, ps_sem, pr_sem, fs_sem, fr_sem, bs_sem, br_sem,
):
    me = lax.axis_index("mode")
    up = lax.rem(me + 1, n_dev)
    down = lax.rem(me + n_dev - 1, n_dev)

    barrier = pltpu.get_barrier_semaphore()

    def greet(k, carry):
        pl.semaphore_signal(
            barrier, inc=1, device_id={"mode": lax.rem(me + k, n_dev)}, device_id_type=MESH
        )
        return carry

    lax.fori_loop(1, n_dev, greet, 0)
    load_logc = pltpu.make_async_copy(logc_ref, raw, local_sem.at[0])
    load_logc.start()
    pl.semaphore_wait(barrier, n_dev - 1)

    side = n_dev // 2
    half_of = me // side

    def target(k):
        j = k // 2
        return lax.rem(half_of + lax.rem(k, 2), 2) * side + lax.rem(me + j, side)

    def columns(d):
        return pl.ds(pl.multiple_of(d * LANES, LANES), LANES)

    def every(do):
        def step(k, carry):
            do(k, target(k))
            return carry

        lax.fori_loop(1, n_dev, step, 0)

    def send_v(k, to, slot):
        return pltpu.make_async_remote_copy(
            src_ref=vel_ref.at[:, :, columns(to)],
            dst_ref=xv.at[slot],
            send_sem=vs_sem.at[k],
            recv_sem=vr_sem.at[slot],
            device_id={"mode": to},
            device_id_type=MESH,
        )

    def send_p(c, k, to, slot):
        return pltpu.make_async_remote_copy(
            src_ref=packed.at[c, to],
            dst_ref=xp.at[c, slot],
            send_sem=ps_sem.at[c, k],
            recv_sem=pr_sem.at[c, slot],
            device_id={"mode": to},
            device_id_type=MESH,
        )

    every(lambda k, to: send_v(k, to, me).start())
    own_v = pltpu.make_async_copy(vel_ref.at[:, :, columns(me)], xv.at[me], local_sem.at[1])
    own_v.start()
    loads = [
        pltpu.make_async_copy(a, b, const_sem.at[i])
        for i, (a, b) in enumerate(
            (
                (node_in, node_ref), (fh_in, fh_ref), (fl_in, fl_ref),
                (div_in, div_ref), (bh_in, bh_ref), (bl_in, bl_ref),
            )
        )
    ]
    for load in loads:
        load.start()

    lane = lax.broadcasted_iota(jnp.int32, (1, LANES), 1)
    lo = lane < CELL

    def swap(value):
        return pltpu.roll(value, CELL, 1)

    def pair_up(c, a, b):
        return jnp.where(lo, a, swap(b)) if c == 0 else jnp.where(lo, swap(a), b)

    load_logc.wait()
    own_p = [
        pltpu.make_async_copy(packed.at[c, me], xp.at[c, me], local_sem.at[2 + c]) for c in range(2)
    ]
    for c in range(2):

        def pack_psi(to, carry, c=c):
            at = columns(to)
            for p in range(3):
                packed[c, to, p] = pair_up(c, raw[2 * p, :, at], raw[2 * p + 1, :, at])
            return carry

        lax.fori_loop(0, n_dev, pack_psi, 0)
        every(lambda k, to, c=c: send_p(c, k, to, me).start())
        own_p[c].start()

    stored = lax.broadcasted_iota(jnp.int32, (LANES, LANES), 0)
    grid = lax.broadcasted_iota(jnp.int32, (LANES, LANES), 1)
    to_grid = jnp.where(stored_index(orient_ref, me, grid) == stored, 1.0, 0.0).astype(BF)

    half = PLANES // 2
    inv_r = inverse_radius(lane)
    for load in loads[:3]:
        load.wait()
    wide = 2 * LANES
    both_h, both_l, grad_h, grad_l = [node_ref.at[:, i * wide : (i + 1) * wide] for i in range(4)]
    mean_ref = node_ref.at[:, 4 * wide : 4 * wide + LANES]

    own_v.wait()
    every(lambda k, frm: send_v(k, frm, frm).wait_recv())
    for f in range(3):
        high, low = split(xv[:, f].reshape(PLANES, LANES))
        at = slice(f * LANES, (f + 1) * LANES)
        xh[:, at] = dot(high, to_grid).astype(BF)
        xl[:, at] = dot(low, to_grid).astype(BF)

    def velocity_block(i, carry):
        at = pl.ds(pl.multiple_of(i * half, half), half)
        vv[at, :] = dot3(fh_ref[at, :], fl_ref[at, :], xh[...], xl[...])
        return carry

    lax.fori_loop(0, 4, velocity_block, 0)

    def grad_block(i, carry):
        block = half // 2
        at = pl.ds(pl.multiple_of(i * block, block), block)
        dth_at = pl.ds(pl.multiple_of(PLANES + i * block, block), block)
        u = [field(vv, f, at) for f in range(3)]
        dth = [field(vv, f, dth_at) for f in range(3)]
        hoop = [(dth[0] - u[1]) * inv_r, (dth[1] + u[0]) * inv_r, dth[2] * inv_r]
        for f in range(3):
            uh, ul = split(u[f])
            both = dot3(uh, ul, grad_h[...], grad_l[...])
            hh, hl = split(hoop[f])
            g = (both[:, :LANES], dot(hh, mean_ref[...]) + dot(hl, mean_ref[...]), both[:, LANES:])
            for j in range(3):
                c = 3 * f + j
                proj[at, c * LANES : (c + 1) * LANES] = g[j]
        return carry

    lax.fori_loop(0, 4, grad_block, 0)

    groups = NODE_1D
    short = PLANES // groups

    def rolled(value, shift):
        return pltpu.roll(value, shift % LANES, 1) if shift % LANES else value

    def face_copy(slot, to):
        return pltpu.make_async_remote_copy(
            src_ref=face_out.at[slot],
            dst_ref=face_in.at[slot],
            send_sem=fs_sem.at[slot],
            recv_sem=fr_sem.at[slot],
            device_id={"mode": to},
            device_id_type=MESH,
        )

    faces = (face_copy(0, up), face_copy(1, down))
    for slot, start in ((0, NODE_1D - 1), (1, 0)):

        def pack(i, carry, slot=slot, start=start):
            at = pl.ds(pl.multiple_of(i * 64, 64), 64)
            total = jnp.zeros((64, LANES), F32)
            for c in range(groups):
                total = jnp.where(lane % groups == c, rolled(field(proj, c, at), c - start), total)
            face_out[slot, at, :] = total
            return carry

        lax.fori_loop(0, PLANES // 64, pack, 0)
        total = jnp.zeros((short, LANES), F32)
        for b in range(groups):
            moved = field(proj, 8, slice(b * short, (b + 1) * short))
            total = jnp.where(lane % groups == b, rolled(moved, b - start), total)
        face_out[slot, PLANES:, :] = total
        faces[slot].start()

    for face in faces:
        face.wait()

    top = lane % NODE_1D == NODE_1D - 1
    low_rows = lane % NODE_1D == 0

    def unpacked(from_down, from_up, c):
        below = rolled(from_down, -c)
        above = rolled(from_up, NODE_1D - 1 - c)
        return jnp.where(top, above, jnp.where(low_rows, below, 0.0))

    for b in range(groups):

        def face_block(i, carry, b=b):
            start = pl.multiple_of(b * short + i * ROWS, ROWS)
            at = pl.ds(start, ROWS)
            nine = pl.ds(pl.multiple_of(PLANES + i * ROWS, ROWS), ROWS)
            down_face, up_face = face_in[0, at, :], face_in[1, at, :]
            g = [field(proj, c, at) + unpacked(down_face, up_face, c) for c in range(8)]
            g.append(field(proj, 8, at) + unpacked(face_in[0, nine, :], face_in[1, nine, :], b))
            for c in range(9):
                proj[at, c * LANES : (c + 1) * LANES] = g[c]
            u = [field(vv, f, at) for f in range(3)]
            for f in range(3):
                total = g[3 * f] * u[0] + g[3 * f + 1] * u[1] + g[3 * f + 2] * u[2]
                conv[at, f * LANES : (f + 1) * LANES] = -total
            return carry

        lax.fori_loop(0, short // ROWS, face_block, 0)

    def put_rate(at, f, value):
        high, low = split(value)
        rh[at, f * LANES : (f + 1) * LANES] = high
        rl[at, f * LANES : (f + 1) * LANES] = low

    share = PLANES // 4
    per = share // modes
    quarter = me // per
    backs, outs = (back0, back1), (out0_ref, out1_ref)
    diag = (0, 3, 5)

    def give(c, to, slot):
        return pltpu.make_async_remote_copy(
            src_ref=backs[c].at[to],
            dst_ref=outs[c].at[slot],
            send_sem=bs_sem.at[c, to],
            recv_sem=br_sem.at[c, slot],
            device_id={"mode": to},
            device_id_type=MESH,
        )

    def cycle_part(c):
        in_c = lo if c == 0 else jnp.logical_not(lo)
        o = orient_ref[me * CYCLES + c]
        same = stored // CELL == grid // CELL
        hit = jnp.logical_and(stored_of_grid(o, grid) == stored % CELL, same)
        cell_grid = jnp.where(hit, 1.0, 0.0).astype(BF)

        def conf_half(far):
            which = lax.rem(half_of + far, 2)
            rows = pl.ds(pl.multiple_of(which * half, half), half)
            for p in range(3):
                high, low = split(xp[c, pl.ds(which * side, side), p].reshape(half, LANES))
                at = slice(p * LANES, (p + 1) * LANES)
                ph[rows, at] = dot(high, cell_grid).astype(BF)
                pw[rows, at] = dot(low, cell_grid).astype(BF)

            def conf_block(i, carry):
                at = pl.ds(pl.multiple_of(i * half, half), half)
                total = dot3(fh_ref[at, rows], fl_ref[at, rows], ph[rows, :], pw[rows, :])
                vp[at, :] = vp[at, :] + total if far else total
                return carry

            lax.fori_loop(0, 4, conf_block, 0)

        def recv_half(far):
            def step(k, carry):
                frm = target(2 * k + far)
                send_p(c, 2 * k + far, frm, frm).wait_recv()
                return carry

            lax.fori_loop(1 - far, side, step, 0)

        own_p[c].wait()
        recv_half(0)
        conf_half(0)
        recv_half(1)
        conf_half(1)

        def deriv_block(i, carry):
            at = pl.ds(pl.multiple_of(i * half, half), half)
            for p in range(3):
                high, low = split(field(vp, p, at))
                dp[at, 2 * p * LANES : (2 * p + 2) * LANES] = dot3(high, low, both_h[...], both_l[...])
            return carry

        lax.fori_loop(0, 2, deriv_block, 0)

        def local_block(i, carry):
            at = pl.ds(pl.multiple_of(i * ROWS, ROWS), ROWS)
            dth_at = pl.ds(pl.multiple_of(PLANES + i * ROWS, ROWS), ROWS)
            u_r, u_t, u_z = [field(vv, f, at) for f in range(3)]
            spin = u_t * inv_r
            ur2, spin2, uz2 = [jnp.where(in_c, v, swap(v)) for v in (u_r, spin, u_z)]
            psi, advect = [], []
            for p in range(3):
                value = field(vp, p, at)
                other = swap(value)
                for h in range(2):
                    psi.append(jnp.where(in_c, value if h == c else other, 0.0))
                advect.append(
                    ur2 * field(dp, 2 * p, at) + spin2 * field(vp, p, dth_at) + uz2 * field(dp, 2 * p + 1, at)
                )
            conform, inverse = exponentials(psi)
            g = [field(proj, j, at) for j in range(9)]
            wa, wb, wc = 0.5 * (g[1] - g[3]), 0.5 * (g[2] - g[6]), 0.5 * (g[5] - g[7])
            wa2 = wa + spin
            r0 = [wa2 * psi[1] + wb * psi[2], wa2 * psi[3] + wb * psi[4], wa2 * psi[4] + wb * psi[5]]
            r1 = [wc * psi[2] - wa2 * psi[0], wc * psi[4] - wa2 * psi[1], wc * psi[5] - wa2 * psi[2]]
            r2 = [-(wb * psi[j] + wc * psi[k]) for j, k in ((0, 1), (1, 3), (2, 4))]
            rate = [
                2.0 * (r0[0] + g[0]),
                r0[1] + r1[0] + (g[1] + g[3]),
                r0[2] + r2[0] + (g[2] + g[6]),
                2.0 * (r1[1] + g[4]),
                r1[2] + r2[1] + (g[5] + g[7]),
                2.0 * (r2[2] + g[8]),
            ]
            for m in range(6):
                unit = 1.0 if m in diag else 0.0
                rate[m] = rate[m] - (1.0 / RELAX_TIME) * (
                    unit - inverse[m] + MOBILITY * (conform[m] - 2.0 * unit + inverse[m])
                )
            stress = [conform[m] - 1.0 if m in diag else conform[m] for m in range(6)]
            for f, (m, n) in enumerate(((0, 2), (1, 4), (2, 5))):
                high, low = split(pair_up(c, stress[m], stress[n]))
                sth[at, f * LANES : (f + 1) * LANES] = high
                stl[at, f * LANES : (f + 1) * LANES] = low
            hoop = [stress[m] * inv_r for m in (1, 3, 4)]
            base = [
                field(conv, 0, at) + (stress[0] - stress[3]) * inv_r,
                field(conv, 1, at) + 2.0 * hoop[0],
                field(conv, 2, at) + stress[2] * inv_r,
            ]
            mom[at, :LANES] = pair_up(c, base[0], base[1])
            mom[at, LANES:] = pair_up(c, base[2], rate[5]) - jnp.where(lo, 0.0, advect[2])
            put_rate(at, 2, pair_up(c, rate[0], rate[1]) - advect[0])
            put_rate(at, 3, pair_up(c, rate[2], rate[3]) - advect[1])
            first = rate[4] if c == 0 else swap(rate[4])
            put_rate(at, 4, jnp.where(lo, first - advect[2], 0.0))
            put_rate(at, 5, pair_up(c, hoop[0], hoop[1]))
            last = hoop[2] if c == 0 else swap(hoop[2])
            put_rate(at, 6, jnp.where(lo, last, 0.0))
            return carry

        lax.fori_loop(0, PLANES // ROWS, local_block, 0)
        if c == 0:
            loads[3].wait()

        def div_block(i, carry):
            at = pl.ds(pl.multiple_of(i * half, half), half)
            for f, cols in enumerate((slice(0, wide), slice(wide, 3 * LANES))):
                depth = cols.stop - cols.start
                total = dot3(
                    sth[at, cols], stl[at, cols], div_ref[:depth, :LANES], div_ref[:depth, LANES:]
                )
                put_rate(at, f, field(mom, f, at) + total)
            return carry

        lax.fori_loop(0, 2, div_block, 0)
        if c == 0:
            for load in loads[4:]:
                load.wait()

        def back_block(step, carry):
            pair = lax.rem(quarter // 2 + 1 + step // 2, 2)
            i = pair * 2 + lax.rem(quarter + step + step // 2, 2)
            at = pl.ds(pl.multiple_of(i * share, share), share)
            dst = pl.ds(i * per, per)
            cols, hoops = slice(0, wide), slice(5 * LANES, 7 * LANES)
            total = dot3(bh_ref[at, :PLANES], bl_ref[at, :PLANES], rh[:, cols], rl[:, cols])
            total += dot3(bh_ref[at, PLANES:], bl_ref[at, PLANES:], rh[:, hoops], rl[:, hoops])
            coefs = [total[:, :LANES], total[:, LANES:]]
            cols = slice(wide, 5 * LANES)
            total = dot3(bh_ref[at, :PLANES], bl_ref[at, :PLANES], rh[:, cols], rl[:, cols])
            coefs += [total[:, j * LANES : (j + 1) * LANES] for j in range(3)]
            if c == 0:
                blocks = [None] * 4
                for f in range(9):
                    off = f * KEPT
                    b, inside = off // LANES, off % LANES
                    moved = rolled(coefs[f // 2], inside - f % 2 * CELL)
                    blocks[b] = moved if inside == 0 else jnp.where(lane < inside, blocks[b], moved)
                    if inside + KEPT > LANES:
                        blocks[b + 1] = moved
                for p in range(4):
                    back0[dst, p] = blocks[p].reshape(per, modes, LANES)
                for p in range(5):
                    kept[p, at, :] = coefs[p]
            else:
                for p in range(5):
                    face = rolled(kept[p, at, :], NODE_1D - CELL)
                    coefs[p] = jnp.where(lane % CELL < NODE_1D, 0.5 * (coefs[p] + face), coefs[p])
                for p in range(5):
                    value = coefs[p].reshape(per, modes, LANES)
                    if not fold:
                        back1[dst, p] = value
                    elif p < 4:
                        back1[dst, 2 * p] = value[:, : modes // 2]
                        back1[dst, 2 * p + 1] = value[:, modes // 2 :]
                    else:
                        upper = swap(coefs[p]).reshape(per, modes, LANES)
                        back1[dst, 8] = jnp.where(lo[None], value[:, : modes // 2], upper[:, modes // 2 :])

            def give_start(j, inner):
                to = i * per + lax.rem(me + j, per)

                @pl.when(to != me)
                def _():
                    give(c, to, me).start()

                return inner

            lax.fori_loop(0, per, give_start, 0)
            return carry

        lax.fori_loop(0, 4, back_block, 0)

    cycle_part(0)
    cycle_part(1)
    own = [pltpu.make_async_copy(backs[c].at[me], outs[c].at[me], local_sem.at[c]) for c in range(2)]
    for copy in own:
        copy.start()
    every(lambda k, to: send_v(k, to, me).wait_send())
    for c in range(2):
        every(lambda k, to, c=c: send_p(c, k, to, me).wait_send())
    for copy in own:
        copy.wait()

    def give_wait(k, to):
        for c in range(2):
            give(c, to, to).wait_recv()
            give(c, to, me).wait_send()

    every(give_wait)


def final_kernel(
    n_dev, modes, fold, group,
    orient_ref, wall_ref, below0_ref, below1_ref, first_ref, second_ref, above0_ref, above1_ref, vel_ref, logc_ref,
    vel_out, logc_out,
):
    step = pl.program_id(0)
    me = lax.axis_index("mode")
    lane = lax.broadcasted_iota(jnp.int32, (1, LANES), 1)
    lo = lane < CELL
    top = lane % NODE_1D == NODE_1D - 1
    low_rows = lane % NODE_1D == 0
    grid = lax.broadcasted_iota(jnp.int32, (LANES, LANES), 0)
    stored = lax.broadcasted_iota(jnp.int32, (LANES, LANES), 1)
    mode_ids = me * modes + lax.broadcasted_iota(jnp.int32, (modes, 1), 0)
    speed = jnp.where(mode_ids == 0, wall_ref[0], 0.0)
    cycle = lane // CELL
    lead = lane // NODE_1D % NODE_1D
    trail = lane % NODE_1D

    def rolled(value, shift):
        return pltpu.roll(value, shift % LANES, 1) if shift % LANES else value

    def layer_fields(ref0, ref1, at):
        fields = []
        for f in range(9):
            off = f * KEPT
            b, inside = off // LANES, off % LANES
            zero = rolled(ref0[at, b], -inside)
            if inside + KEPT > LANES:
                zero = jnp.where(lane < LANES - inside, zero, rolled(ref0[at, b + 1], -inside))
            p = f // 2
            if not fold:
                one = rolled(ref1[at, p], (f + 1) % 2 * CELL)
            elif p < 4:
                one = ref1[at, 2 * p : 2 * p + 2].reshape(modes, LANES)
                one = rolled(one, (f + 1) % 2 * CELL)
            else:
                one = jnp.concatenate([rolled(ref1[at, 8], CELL), ref1[at, 8]], axis=0)
            fields.append(jnp.where(lo, zero, one))
        return fields

    layers = [layer_fields(below0_ref, below1_ref, 0)]
    layers += [layer_fields(first_ref, second_ref, g) for g in range(group)]
    layers.append(layer_fields(above0_ref, above1_ref, 0))
    for g in range(group):
        layer = step * group + g
        place = stored_index(orient_ref, layer, grid)
        twin = stored_index(orient_ref, layer, grid - NODE_1D)
        is_face = jnp.logical_and(grid >= CELL, grid < CELL + NODE_1D)
        dropped = jnp.logical_and(grid >= KEPT, grid < CELL)
        hit = jnp.logical_and(place == stored, jnp.logical_not(dropped))
        hit = jnp.logical_or(hit, jnp.logical_and(is_face, twin == stored))
        hot = jnp.where(hit, 1.0, 0.0).astype(BF)
        hot = jnp.concatenate([hot, hot], axis=0)
        code = jnp.zeros_like(lane)
        for c in range(CYCLES):
            code = jnp.where(cycle == c, orient_ref[layer * CYCLES + c], code)
        flipped_a = jnp.where(code % 2 == 1, NODE_1D - 1 - lead, lead)
        flipped_b = jnp.where(code // 2 % 2 == 1, NODE_1D - 1 - trail, trail)
        x = jnp.where(code // 4 % 2 == 1, flipped_a, flipped_b)
        inner = jnp.logical_and(cycle == 0, x == 0)
        outer = jnp.logical_and(cycle == CYCLES - 1, x == NODE_1D - 1)
        on_wall = jnp.logical_or(inner, outer)
        cols = slice(g * LANES, (g + 1) * LANES)
        many = 9 if modes % 8 == 0 else 1
        for start in range(0, 9, many):
            rates = []
            for c in range(start, start + many):
                f = SLOT_OF[c]
                below, rate, above = [layers[g + d][f] for d in range(3)]
                other = jnp.where(low_rows, rolled(below, 1 - NODE_1D), rolled(above, NODE_1D - 1))
                rates.append(jnp.where(jnp.logical_or(top, low_rows), 0.5 * (rate + other), rate))
            rate = jnp.concatenate(rates, axis=0) if many > 1 else rates[0]
            high, low = split(rate)
            rate = STEP_DT * dot(jnp.concatenate([high, low], axis=1), hot)
            for j in range(many):
                c = start + j
                own = rate[j * modes : (j + 1) * modes]
                if c < 3:
                    wall = jnp.where(inner, speed, 0.0) if c == 1 else 0.0
                    vel_out[c, :, cols] = jnp.where(on_wall, wall, vel_ref[c, :, cols] + own)
                else:
                    logc_out[c - 3, :, cols] = logc_ref[c - 3, :, cols] + own


def body(velocity, log_conf, orientation, wall_speed):
    n_dev = lax.axis_size("mode")
    modes = velocity.shape[1]
    fold = modes % 16 == 0
    tail = (9, modes // 2, LANES) if fold else (5, modes, LANES)
    consts = [jnp.asarray(t) for t in tables()]
    hbm = pl.BlockSpec(memory_space=pl.ANY)
    smem = pl.BlockSpec(memory_space=pltpu.SMEM)
    dma = pltpu.SemaphoreType.DMA
    face_rows = PLANES + PLANES * CYCLES * NODE_1D // LANES
    first, second = pl.pallas_call(
        functools.partial(main_kernel, n_dev, modes, fold),
        out_shape=(
            jax.ShapeDtypeStruct((n_dev, 4, modes, LANES), F32),
            jax.ShapeDtypeStruct((n_dev, *tail), F32),
        ),
        in_specs=[hbm, hbm, smem] + [hbm] * len(consts),
        out_specs=(hbm, hbm),
        scratch_shapes=[pltpu.VMEM(t.shape, t.dtype) for t in consts]
        + [
            pltpu.VMEM(log_conf.shape, F32),
            pltpu.VMEM((2, n_dev, 3, modes, LANES), F32),
            pltpu.VMEM((n_dev, 3, modes, LANES), F32),
            pltpu.VMEM((2, n_dev, 3, modes, LANES), F32),
            pltpu.VMEM((PLANES, 3 * LANES), BF),
            pltpu.VMEM((PLANES, 3 * LANES), BF),
            pltpu.VMEM((PLANES, 3 * LANES), BF),
            pltpu.VMEM((PLANES, 3 * LANES), BF),
            pltpu.VMEM((2 * PLANES, 3 * LANES), F32),
            pltpu.VMEM((2 * PLANES, 3 * LANES), F32),
            pltpu.VMEM((PLANES, 6 * LANES), F32),
            pltpu.VMEM((PLANES, 9 * LANES), F32),
            pltpu.VMEM((2, face_rows, LANES), F32),
            pltpu.VMEM((2, face_rows, LANES), F32),
            pltpu.VMEM((PLANES, 3 * LANES), F32),
            pltpu.VMEM((PLANES, 2 * LANES), F32),
            pltpu.VMEM((PLANES, 3 * LANES), BF),
            pltpu.VMEM((PLANES, 3 * LANES), BF),
            pltpu.VMEM((PLANES, 7 * LANES), BF),
            pltpu.VMEM((PLANES, 7 * LANES), BF),
            pltpu.VMEM((5, PLANES, LANES), F32),
            pltpu.VMEM((n_dev, 4, modes, LANES), F32),
            pltpu.VMEM((n_dev, *tail), F32),
            dma((4,)),
            dma((len(consts),)),
            dma((n_dev,)),
            dma((n_dev,)),
            dma((2, n_dev)),
            dma((2, n_dev)),
            dma((2,)),
            dma((2,)),
            dma((2, n_dev)),
            dma((2, n_dev)),
        ],
        compiler_params=pltpu.CompilerParams(
            collective_id=0, has_side_effects=True, vmem_limit_bytes=60 * 2**20
        ),
        name="fields",
    )(velocity, log_conf, orientation, *consts)

    group = 8
    tile = group * LANES

    def below_of(i):
        return (lax.rem(i * group + n_dev - 1, n_dev), 0, 0, 0)

    def above_of(i):
        return (lax.rem(i * group + group, n_dev), 0, 0, 0)

    def here(i):
        return (i, 0, 0, 0)

    return pl.pallas_call(
        functools.partial(final_kernel, n_dev, modes, fold, group),
        grid=(n_dev // group,),
        out_shape=(
            jax.ShapeDtypeStruct(velocity.shape, F32),
            jax.ShapeDtypeStruct(log_conf.shape, F32),
        ),
        in_specs=[
            smem,
            smem,
            pl.BlockSpec((1, 4, modes, LANES), below_of),
            pl.BlockSpec((1, *tail), below_of),
            pl.BlockSpec((group, 4, modes, LANES), here),
            pl.BlockSpec((group, *tail), here),
            pl.BlockSpec((1, 4, modes, LANES), above_of),
            pl.BlockSpec((1, *tail), above_of),
            pl.BlockSpec((3, modes, tile), lambda i: (0, 0, i)),
            pl.BlockSpec((6, modes, tile), lambda i: (0, 0, i)),
        ],
        out_specs=(
            pl.BlockSpec((3, modes, tile), lambda i: (0, 0, i)),
            pl.BlockSpec((6, modes, tile), lambda i: (0, 0, i)),
        ),
        compiler_params=pltpu.CompilerParams(vmem_limit_bytes=60 * 2**20),
        name="finish",
    )(orientation, wall_speed, first, second, first, second, first, second, velocity, log_conf)


def solution(mesh):
    in_specs = (P("ens", "mode", None), P("ens", "mode", None), P(), P("ens"))
    out_specs = (P("ens", "mode", None), P("ens", "mode", None))
    return jax.shard_map(body, mesh=mesh, in_specs=in_specs, out_specs=out_specs, check_vma=False)
```

```python
import functools

import jax
import jax.numpy as jnp
import ml_dtypes
import numpy as np
from jax import lax
from jax.experimental import pallas as pl
from jax.experimental.pallas import tpu as pltpu
from jax.sharding import PartitionSpec as P

NODE_1D = 8
CYCLES = 2
PLANES = 512
CELL = NODE_1D * NODE_1D
LANES = CYCLES * CELL
KEPT = CELL - NODE_1D
INSIDE = LANES - LANES // 4
SLOT_OF = (0, 1, 2, 4, 5, 6, 7, 8, 3)
STEP_DT = 0.002
RELAX_TIME = 0.02
MOBILITY = 0.3
LAYER_HEIGHT = 0.25
R_INNER = 1.0
ROWS = 16
BF = jnp.bfloat16
F32 = jnp.float32
MESH = pl.DeviceIdType.MESH


def cheb_table(points):
    nodes_xi = -np.cos(np.pi * np.arange(points) / (points - 1))
    weights = np.ones(points)
    weights[0] = 2.0
    weights[-1] = 2.0
    weights = weights * (-1.0) ** np.arange(points)
    identity = np.eye(points)
    spacing = nodes_xi[:, None] - nodes_xi[None, :] + identity
    matrix = weights[:, None] / weights[None, :] / spacing
    matrix = matrix * (1.0 - identity)
    matrix = matrix - identity * matrix.sum(axis=1)[:, None]
    return (nodes_xi, matrix)


def halves(table):
    high = np.asarray(table, np.float32).astype(ml_dtypes.bfloat16)
    low = (np.asarray(table, np.float64) - high.astype(np.float64)).astype(ml_dtypes.bfloat16)
    return high, low


def tables():
    n = np.arange(PLANES)
    k = np.arange(PLANES // 2)
    angle = (n[:, None] * k[None, :] % PLANES) * (2.0 * np.pi / PLANES)
    cosine = np.cos(angle) * np.sqrt(2.0 / PLANES)
    sine = np.sin(angle) * np.sqrt(2.0 / PLANES)
    cosine[:, 0] = PLANES**-0.5
    sine[:, 0] = (-1.0) ** n * PLANES**-0.5
    basis = np.stack([cosine, sine], axis=2).reshape(PLANES, PLANES)
    dbasis = np.stack([-k * sine, k * cosine], axis=2).reshape(PLANES, PLANES)
    forward = np.concatenate([basis, dbasis], axis=0)
    backward = np.concatenate([basis.T, -dbasis.T], axis=1)

    xi, matrix = cheb_table(NODE_1D)
    eye, eyes = np.eye(NODE_1D), np.eye(CYCLES)
    cell_r = np.kron(matrix.T * (2.0 * CYCLES), eye)
    cell_z = np.kron(eye, matrix.T * (2.0 / LAYER_HEIGHT))
    d_r, d_z = np.kron(eyes, cell_r), np.kron(eyes, cell_z)
    mean = np.eye(CYCLES * NODE_1D)
    for c in range(1, CYCLES):
        i = c * NODE_1D
        mean[i - 1 : i + 1, i - 1 : i + 1] = 0.5
    mean = np.kron(mean, eye)
    weight = np.ones(NODE_1D)
    weight[0] = weight[-1] = 0.5
    weight = np.tile(weight, CYCLES * NODE_1D)
    mean_w = mean * weight[None, :]
    both = np.concatenate([d_r, d_z], axis=1)
    grad = np.concatenate([d_r @ mean_w, d_z @ mean_w], axis=1)
    div = np.kron(np.eye(2), np.concatenate([cell_r, cell_z], axis=0))
    return (
        *halves(forward),
        *halves(backward),
        np.concatenate([*halves(both), *halves(grad), mean_w.astype(ml_dtypes.bfloat16)], axis=1),
        np.concatenate(halves(div), axis=1),
    )


def inverse_radius(lane):
    xi, _ = cheb_table(NODE_1D)
    radius = R_INNER + (np.arange(CYCLES)[:, None] + (xi[None, :] + 1.0) / 2.0) / CYCLES
    total = jnp.zeros(lane.shape, F32)
    for i, r in enumerate(radius.reshape(-1)):
        total = jnp.where(lane // NODE_1D == i, float(1.0 / r), total)
    return total


def split(x):
    high = x.astype(BF)
    return high, (x - high.astype(F32)).astype(BF)


def dot(a, b):
    return jnp.dot(a, b, preferred_element_type=F32)


def dot3(ah, al, bh, bl):
    return dot(ah, bh) + (dot(ah, bl) + dot(al, bh))


def stored_of_grid(o, grid):
    side = NODE_1D
    y = grid % side
    x = grid // side % side
    swapped = o // 4 % 2 == 1
    a = jnp.where(swapped, x, y)
    b = jnp.where(swapped, y, x)
    a = jnp.where(o % 2 == 1, side - 1 - a, a)
    b = jnp.where(o // 2 % 2 == 1, side - 1 - b, b)
    return a * side + b


def stored_index(orient_ref, layer, grid):
    cycle = grid // CELL
    place = jnp.zeros_like(grid)
    for c in range(CYCLES):
        o = orient_ref[layer * CYCLES + c]
        place = jnp.where(cycle == c, c * CELL + stored_of_grid(o, grid), place)
    return place


def square(m):
    a, b, c, d, e, f = m
    bb, cc, ee = b * b, c * c, e * e
    return (
        a * a + bb + cc,
        b * (a + d) + c * e,
        c * (a + f) + b * e,
        bb + d * d + ee,
        e * (d + f) + b * c,
        cc + ee + f * f,
    )


def product(m, n):
    a, b, c, d, e, f = m
    p, q, r, s, t, u = n
    return (
        a * p + b * q + c * r,
        a * q + b * s + c * t,
        a * r + b * t + c * u,
        b * q + d * s + e * t,
        b * r + d * t + e * u,
        c * r + e * t + f * u,
    )


def exponentials(psi):
    x = tuple(v * 0.125 for v in psi)
    x2 = square(x)
    x3 = product(x, x2)
    x4 = square(x2)
    even = [x2[i] * 0.5 + x4[i] * (1.0 / 24.0) for i in range(6)]
    for i in (0, 3, 5):
        even[i] = even[i] + 1.0
    odd = [x[i] + x3[i] * (1.0 / 6.0) for i in range(6)]
    plus = tuple(even[i] + odd[i] for i in range(6))
    minus = tuple(even[i] - odd[i] for i in range(6))
    for _ in range(3):
        plus, minus = square(plus), square(minus)
    return plus, minus


def first_cycle(f):
    wall = NODE_1D if f < 3 else 0
    start = f * KEPT - min(f, 3) * NODE_1D
    return start // LANES, start % LANES, wall, KEPT - wall


def field(ref, f, rows=slice(None)):
    return ref[rows, f * LANES : (f + 1) * LANES]


def main_kernel(
    n_dev, modes, fold,
    vel_ref, logc_ref, orient_ref, fh_in, fl_in, bh_in, bl_in, node_in, div_in,
    out0_ref, out1_ref,
    fh_ref, fl_ref, bh_ref, bl_ref, node_ref, div_ref,
    raw, packed, xv, xp, xh, xl, ph, pw, vv, vp, dp, proj, face_out, face_in, conv, mom, sth, stl, rh, rl,
    kept, back0, back1,
    local_sem, const_sem, vs_sem, vr_sem, ps_sem, pr_sem, fs_sem, fr_sem, bs_sem, br_sem,
):
    me = lax.axis_index("mode")
    up = lax.rem(me + 1, n_dev)
    down = lax.rem(me + n_dev - 1, n_dev)

    barrier = pltpu.get_barrier_semaphore()

    def greet(k, carry):
        pl.semaphore_signal(
            barrier, inc=1, device_id={"mode": lax.rem(me + k, n_dev)}, device_id_type=MESH
        )
        return carry

    lax.fori_loop(1, n_dev, greet, 0)
    load_logc = pltpu.make_async_copy(logc_ref, raw, local_sem.at[0])
    load_logc.start()
    pl.semaphore_wait(barrier, n_dev - 1)

    side = n_dev // 2
    half_of = me // side

    def target(k):
        j = k // 2
        return lax.rem(half_of + lax.rem(k, 2), 2) * side + lax.rem(me + j, side)

    def columns(d):
        return pl.ds(pl.multiple_of(d * LANES, LANES), LANES)

    def every(do):
        def step(k, carry):
            do(k, target(k))
            return carry

        lax.fori_loop(1, n_dev, step, 0)

    def send_v(k, to, slot):
        return pltpu.make_async_remote_copy(
            src_ref=vel_ref.at[:, :, columns(to)],
            dst_ref=xv.at[slot],
            send_sem=vs_sem.at[k],
            recv_sem=vr_sem.at[slot],
            device_id={"mode": to},
            device_id_type=MESH,
        )

    def send_p(c, k, to, slot):
        return pltpu.make_async_remote_copy(
            src_ref=packed.at[c, to],
            dst_ref=xp.at[c, slot],
            send_sem=ps_sem.at[c, k],
            recv_sem=pr_sem.at[c, slot],
            device_id={"mode": to},
            device_id_type=MESH,
        )

    every(lambda k, to: send_v(k, to, me).start())
    own_v = pltpu.make_async_copy(vel_ref.at[:, :, columns(me)], xv.at[me], local_sem.at[1])
    own_v.start()
    loads = [
        pltpu.make_async_copy(a, b, const_sem.at[i])
        for i, (a, b) in enumerate(
            (
                (node_in, node_ref), (fh_in, fh_ref), (fl_in, fl_ref),
                (div_in, div_ref), (bh_in, bh_ref), (bl_in, bl_ref),
            )
        )
    ]
    for load in loads:
        load.start()

    lane = lax.broadcasted_iota(jnp.int32, (1, LANES), 1)
    lo = lane < CELL

    def swap(value):
        return pltpu.roll(value, CELL, 1)

    def pair_up(c, a, b):
        return jnp.where(lo, a, swap(b)) if c == 0 else jnp.where(lo, swap(a), b)

    load_logc.wait()
    own_p = [
        pltpu.make_async_copy(packed.at[c, me], xp.at[c, me], local_sem.at[2 + c]) for c in range(2)
    ]
    for c in range(2):

        def pack_psi(to, carry, c=c):
            at = columns(to)
            for p in range(3):
                packed[c, to, p] = pair_up(c, raw[2 * p, :, at], raw[2 * p + 1, :, at])
            return carry

        lax.fori_loop(0, n_dev, pack_psi, 0)
        every(lambda k, to, c=c: send_p(c, k, to, me).start())
        own_p[c].start()

    stored = lax.broadcasted_iota(jnp.int32, (LANES, LANES), 0)
    to_grid = jnp.where(stored_index(orient_ref, me, lane) == stored, 1.0, 0.0).astype(BF)

    half = PLANES // 2
    inv_r = inverse_radius(lane)
    for load in loads[:3]:
        load.wait()
    wide = 2 * LANES
    both_h, both_l, grad_h, grad_l = [node_ref.at[:, i * wide : (i + 1) * wide] for i in range(4)]
    mean_ref = node_ref.at[:, 4 * wide : 4 * wide + LANES]

    own_v.wait()
    every(lambda k, frm: send_v(k, frm, frm).wait_recv())
    for f in range(3):
        high, low = split(xv[:, f].reshape(PLANES, LANES))
        at = slice(f * LANES, (f + 1) * LANES)
        xh[:, at] = dot(high, to_grid).astype(BF)
        xl[:, at] = dot(low, to_grid).astype(BF)

    def velocity_block(i, carry):
        at = pl.ds(pl.multiple_of(i * half, half), half)
        vv[at, :] = dot3(fh_ref[at, :], fl_ref[at, :], xh[...], xl[...])
        return carry

    lax.fori_loop(0, 4, velocity_block, 0)

    def grad_block(i, carry):
        block = half // 2
        at = pl.ds(pl.multiple_of(i * block, block), block)
        dth_at = pl.ds(pl.multiple_of(PLANES + i * block, block), block)
        u = [field(vv, f, at) for f in range(3)]
        dth = [field(vv, f, dth_at) for f in range(3)]
        hoop = [(dth[0] - u[1]) * inv_r, (dth[1] + u[0]) * inv_r, dth[2] * inv_r]
        for f in range(3):
            uh, ul = split(u[f])
            both = dot3(uh, ul, grad_h[...], grad_l[...])
            hh, hl = split(hoop[f])
            g = (both[:, :LANES], dot(hh, mean_ref[...]) + dot(hl, mean_ref[...]), both[:, LANES:])
            for j in range(3):
                c = 3 * f + j
                proj[at, c * LANES : (c + 1) * LANES] = g[j]
        return carry

    lax.fori_loop(0, 4, grad_block, 0)

    groups = NODE_1D
    short = PLANES // groups

    def rolled(value, shift):
        return pltpu.roll(value, shift % LANES, 1) if shift % LANES else value

    def face_copy(slot, to):
        return pltpu.make_async_remote_copy(
            src_ref=face_out.at[slot],
            dst_ref=face_in.at[slot],
            send_sem=fs_sem.at[slot],
            recv_sem=fr_sem.at[slot],
            device_id={"mode": to},
            device_id_type=MESH,
        )

    faces = (face_copy(0, up), face_copy(1, down))
    for slot, start in ((0, NODE_1D - 1), (1, 0)):

        def pack(i, carry, slot=slot, start=start):
            at = pl.ds(pl.multiple_of(i * 64, 64), 64)
            total = jnp.zeros((64, LANES), F32)
            for c in range(groups):
                total = jnp.where(lane % groups == c, rolled(field(proj, c, at), c - start), total)
            face_out[slot, at, :] = total
            return carry

        lax.fori_loop(0, PLANES // 64, pack, 0)
        total = jnp.zeros((short, LANES), F32)
        for b in range(groups):
            moved = field(proj, 8, slice(b * short, (b + 1) * short))
            total = jnp.where(lane % groups == b, rolled(moved, b - start), total)
        face_out[slot, PLANES:, :] = total
        faces[slot].start()

    for face in faces:
        face.wait()

    top = lane % NODE_1D == NODE_1D - 1
    low_rows = lane % NODE_1D == 0

    def unpacked(from_down, from_up, c):
        below = rolled(from_down, -c)
        above = rolled(from_up, NODE_1D - 1 - c)
        return jnp.where(top, above, jnp.where(low_rows, below, 0.0))

    for b in range(groups):

        def face_block(i, carry, b=b):
            start = pl.multiple_of(b * short + i * ROWS, ROWS)
            at = pl.ds(start, ROWS)
            nine = pl.ds(pl.multiple_of(PLANES + i * ROWS, ROWS), ROWS)
            down_face, up_face = face_in[0, at, :], face_in[1, at, :]
            g = [field(proj, c, at) + unpacked(down_face, up_face, c) for c in range(8)]
            g.append(field(proj, 8, at) + unpacked(face_in[0, nine, :], face_in[1, nine, :], b))
            for c in range(9):
                proj[at, c * LANES : (c + 1) * LANES] = g[c]
            u = [field(vv, f, at) for f in range(3)]
            for f in range(3):
                total = g[3 * f] * u[0] + g[3 * f + 1] * u[1] + g[3 * f + 2] * u[2]
                conv[at, f * LANES : (f + 1) * LANES] = -total
            return carry

        lax.fori_loop(0, short // ROWS, face_block, 0)

    def put_rate(at, f, value):
        high, low = split(value)
        rh[at, f * LANES : (f + 1) * LANES] = high
        rl[at, f * LANES : (f + 1) * LANES] = low

    share = PLANES // 4
    per = share // modes
    quarter = me // per
    backs, outs = (back0, back1), (out0_ref, out1_ref)
    diag = (0, 3, 5)

    def give(c, to, slot):
        return pltpu.make_async_remote_copy(
            src_ref=backs[c].at[to],
            dst_ref=outs[c].at[slot],
            send_sem=bs_sem.at[c, to],
            recv_sem=br_sem.at[c, slot],
            device_id={"mode": to},
            device_id_type=MESH,
        )

    def quarters(value):
        return value.reshape(per, 4, modes // 4, LANES)

    def cycle_part(c):
        in_c = lo if c == 0 else jnp.logical_not(lo)
        o = orient_ref[me * CYCLES + c]
        place = stored_of_grid(o, lane) + lane // CELL * CELL
        cell_grid = jnp.where(place == stored, 1.0, 0.0).astype(BF)

        def conf_half(far):
            which = lax.rem(half_of + far, 2)
            rows = pl.ds(pl.multiple_of(which * half, half), half)
            for p in range(3):
                high, low = split(xp[c, pl.ds(which * side, side), p].reshape(half, LANES))
                at = slice(p * LANES, (p + 1) * LANES)
                ph[rows, at] = dot(high, cell_grid).astype(BF)
                pw[rows, at] = dot(low, cell_grid).astype(BF)

            def conf_block(i, carry):
                at = pl.ds(pl.multiple_of(i * half, half), half)
                total = dot3(fh_ref[at, rows], fl_ref[at, rows], ph[rows, :], pw[rows, :])
                vp[at, :] = vp[at, :] + total if far else total
                return carry

            lax.fori_loop(0, 4, conf_block, 0)

        def recv_half(far):
            def step(k, carry):
                frm = target(2 * k + far)
                send_p(c, 2 * k + far, frm, frm).wait_recv()
                return carry

            lax.fori_loop(1 - far, side, step, 0)

        own_p[c].wait()
        recv_half(0)
        conf_half(0)
        recv_half(1)
        conf_half(1)

        def deriv_block(i, carry):
            at = pl.ds(pl.multiple_of(i * half, half), half)
            for p in range(3):
                high, low = split(field(vp, p, at))
                dp[at, 2 * p * LANES : (2 * p + 2) * LANES] = dot3(high, low, both_h[...], both_l[...])
            return carry

        lax.fori_loop(0, 2, deriv_block, 0)

        def local_block(i, carry):
            at = pl.ds(pl.multiple_of(i * ROWS, ROWS), ROWS)
            dth_at = pl.ds(pl.multiple_of(PLANES + i * ROWS, ROWS), ROWS)
            u_r, u_t, u_z = [field(vv, f, at) for f in range(3)]
            spin = u_t * inv_r
            ur2, spin2, uz2 = [jnp.where(in_c, v, swap(v)) for v in (u_r, spin, u_z)]
            psi, advect = [], []
            for p in range(3):
                value = field(vp, p, at)
                other = swap(value)
                for h in range(2):
                    psi.append(jnp.where(in_c, value if h == c else other, 0.0))
                advect.append(
                    ur2 * field(dp, 2 * p, at) + spin2 * field(vp, p, dth_at) + uz2 * field(dp, 2 * p + 1, at)
                )
            conform, inverse = exponentials(psi)
            g = [field(proj, j, at) for j in range(9)]
            wa, wb, wc = 0.5 * (g[1] - g[3]), 0.5 * (g[2] - g[6]), 0.5 * (g[5] - g[7])
            wa2 = wa + spin
            r0 = [wa2 * psi[1] + wb * psi[2], wa2 * psi[3] + wb * psi[4], wa2 * psi[4] + wb * psi[5]]
            r1 = [wc * psi[2] - wa2 * psi[0], wc * psi[4] - wa2 * psi[1], wc * psi[5] - wa2 * psi[2]]
            r2 = [-(wb * psi[j] + wc * psi[k]) for j, k in ((0, 1), (1, 3), (2, 4))]
            rate = [
                2.0 * (r0[0] + g[0]),
                r0[1] + r1[0] + (g[1] + g[3]),
                r0[2] + r2[0] + (g[2] + g[6]),
                2.0 * (r1[1] + g[4]),
                r1[2] + r2[1] + (g[5] + g[7]),
                2.0 * (r2[2] + g[8]),
            ]
            for m in range(6):
                unit = 1.0 if m in diag else 0.0
                rate[m] = rate[m] - (1.0 / RELAX_TIME) * (
                    unit - inverse[m] + MOBILITY * (conform[m] - 2.0 * unit + inverse[m])
                )
            stress = [conform[m] - 1.0 if m in diag else conform[m] for m in range(6)]
            for f, (m, n) in enumerate(((0, 2), (1, 4), (2, 5))):
                high, low = split(pair_up(c, stress[m], stress[n]))
                sth[at, f * LANES : (f + 1) * LANES] = high
                stl[at, f * LANES : (f + 1) * LANES] = low
            hoop = [stress[m] * inv_r for m in (1, 3, 4)]
            base = [
                field(conv, 0, at) + (stress[0] - stress[3]) * inv_r,
                field(conv, 1, at) + 2.0 * hoop[0],
                field(conv, 2, at) + stress[2] * inv_r,
            ]
            mom[at, :LANES] = pair_up(c, base[0], base[1])
            mom[at, LANES:] = pair_up(c, base[2], rate[5]) - jnp.where(lo, 0.0, advect[2])
            put_rate(at, 2, pair_up(c, rate[0], rate[1]) - advect[0])
            put_rate(at, 3, pair_up(c, rate[2], rate[3]) - advect[1])
            first = rate[4] if c == 0 else swap(rate[4])
            put_rate(at, 4, jnp.where(lo, first - advect[2], 0.0))
            put_rate(at, 5, pair_up(c, hoop[0], hoop[1]))
            last = hoop[2] if c == 0 else swap(hoop[2])
            put_rate(at, 6, jnp.where(lo, last, 0.0))
            return carry

        lax.fori_loop(0, PLANES // ROWS, local_block, 0)
        if c == 0:
            loads[3].wait()

        def div_block(i, carry):
            at = pl.ds(pl.multiple_of(i * half, half), half)
            for f, cols in enumerate((slice(0, wide), slice(wide, 3 * LANES))):
                depth = cols.stop - cols.start
                total = dot3(
                    sth[at, cols], stl[at, cols], div_ref[:depth, :LANES], div_ref[:depth, LANES:]
                )
                put_rate(at, f, field(mom, f, at) + total)
            return carry

        lax.fori_loop(0, 2, div_block, 0)
        if c == 0:
            for load in loads[4:]:
                load.wait()

        def back_block(step, carry):
            pair = lax.rem(quarter // 2 + 1 + step // 2, 2)
            i = pair * 2 + lax.rem(quarter + step + step // 2, 2)
            at = pl.ds(pl.multiple_of(i * share, share), share)
            dst = pl.ds(i * per, per)
            cols, hoops = slice(0, wide), slice(5 * LANES, 7 * LANES)
            total = dot3(bh_ref[at, :PLANES], bl_ref[at, :PLANES], rh[:, cols], rl[:, cols])
            total += dot3(bh_ref[at, PLANES:], bl_ref[at, PLANES:], rh[:, hoops], rl[:, hoops])
            coefs = [total[:, :LANES], total[:, LANES:]]
            cols = slice(wide, 5 * LANES)
            total = dot3(bh_ref[at, :PLANES], bl_ref[at, :PLANES], rh[:, cols], rl[:, cols])
            coefs += [total[:, j * LANES : (j + 1) * LANES] for j in range(3)]
            if c == 0:
                blocks = [None] * 4
                for f in range(9):
                    b, inside, wall, width = first_cycle(f)
                    moved = rolled(coefs[f // 2], inside - wall - f % 2 * CELL)
                    blocks[b] = moved if inside == 0 else jnp.where(lane < inside, blocks[b], moved)
                    if inside + width > LANES:
                        blocks[b + 1] = moved
                for p in range(4):
                    if not fold:
                        back0[dst, p] = blocks[p].reshape(per, modes, LANES)
                    elif p < 3:
                        back0[dst, 4 * p : 4 * p + 4] = quarters(blocks[p])
                    else:
                        value = quarters(blocks[p])
                        for j in range(3):
                            extra = quarters(rolled(blocks[p], INSIDE - j * (LANES // 4)))[:, 3]
                            back0[dst, 12 + j] = jnp.where(lane < INSIDE, value[:, j], extra)
                for p in range(5):
                    kept[p, at, :] = coefs[p]
            else:
                for p in range(5):
                    face = rolled(kept[p, at, :], NODE_1D - CELL)
                    coefs[p] = jnp.where(lane % CELL < NODE_1D, 0.5 * (coefs[p] + face), coefs[p])
                for p in range(5):
                    if not fold:
                        back1[dst, p] = coefs[p].reshape(per, modes, LANES)
                    elif p < 4:
                        back1[dst, 4 * p : 4 * p + 4] = quarters(coefs[p])
                    else:
                        value, upper = quarters(coefs[p]), quarters(swap(coefs[p]))
                        for j in range(2):
                            back1[dst, 16 + j] = jnp.where(lo, value[:, j], upper[:, 2 + j])

            def give_start(j, inner):
                to = i * per + lax.rem(me + j, per)

                @pl.when(to != me)
                def _():
                    give(c, to, me).start()

                return inner

            lax.fori_loop(0, per, give_start, 0)
            return carry

        lax.fori_loop(0, 4, back_block, 0)

    cycle_part(0)
    cycle_part(1)
    own = [pltpu.make_async_copy(backs[c].at[me], outs[c].at[me], local_sem.at[c]) for c in range(2)]
    for copy in own:
        copy.start()
    every(lambda k, to: send_v(k, to, me).wait_send())
    for c in range(2):
        every(lambda k, to, c=c: send_p(c, k, to, me).wait_send())
    for copy in own:
        copy.wait()

    def give_wait(k, to):
        for c in range(2):
            give(c, to, to).wait_recv()
            give(c, to, me).wait_send()

    every(give_wait)


def final_kernel(
    n_dev, modes, fold, group,
    orient_ref, wall_ref, first_ref, second_ref, vel_ref, logc_ref,
    vel_out, logc_out,
):
    step = pl.program_id(0)
    me = lax.axis_index("mode")
    lane = lax.broadcasted_iota(jnp.int32, (1, LANES), 1)
    lo = lane < CELL
    top = lane % NODE_1D == NODE_1D - 1
    low_rows = lane % NODE_1D == 0
    stored = lax.broadcasted_iota(jnp.int32, (LANES, LANES), 0)
    is_face = jnp.logical_and(lane >= CELL, lane < CELL + NODE_1D)
    dropped = jnp.logical_and(lane >= KEPT, lane < CELL)
    mode_ids = me * modes + lax.broadcasted_iota(jnp.int32, (modes, 1), 0)
    speed = jnp.where(mode_ids == 0, wall_ref[0], 0.0)
    cycle = lane // CELL
    lead = lane // NODE_1D % NODE_1D
    trail = lane % NODE_1D

    def rolled(value, shift):
        return pltpu.roll(value, shift % LANES, 1) if shift % LANES else value

    def layer_fields(g):
        at = lax.rem(step * group + g + n_dev, n_dev)
        ref0, ref1 = first_ref, second_ref
        fields = []
        blocks = [ref0[at, p] if not fold else ref0[at, 4 * p : 4 * p + 4].reshape(modes, LANES) for p in range(3)]
        if not fold:
            blocks.append(ref0[at, 3])
        else:
            units = [ref0[at, 12 + j] for j in range(3)]
            piece = lane // (LANES // 4)
            outer = [rolled(units[j], (j + 1) * (LANES // 4)) for j in range(3)]
            units.append(jnp.where(piece == 0, outer[0], jnp.where(piece == 1, outer[1], outer[2])))
            blocks.append(jnp.concatenate(units, axis=0))
        for f in range(9):
            b, inside, wall, width = first_cycle(f)
            zero = rolled(blocks[b], wall - inside)
            if inside + width > LANES:
                zero = jnp.where(lane < wall + LANES - inside, zero, rolled(blocks[b + 1], wall - inside))
            p = f // 2
            if not fold:
                one = rolled(ref1[at, p], (f + 1) % 2 * CELL)
            elif p < 4:
                one = ref1[at, 4 * p : 4 * p + 4].reshape(modes, LANES)
                one = rolled(one, (f + 1) % 2 * CELL)
            else:
                one = ref1[at, 16:18].reshape(modes // 2, LANES)
                one = jnp.concatenate([rolled(one, CELL), one], axis=0)
            fields.append(jnp.where(lo, zero, one))
        return fields

    layers = [layer_fields(g) for g in range(-1, group + 1)]
    for g in range(group):
        layer = step * group + g
        place = jnp.where(dropped, -1, stored_index(orient_ref, layer, lane))
        twin = jnp.where(is_face, stored_index(orient_ref, layer, lane - NODE_1D), -1)
        hot = jnp.where(jnp.logical_or(place == stored, twin == stored), 1.0, 0.0).astype(BF)
        hot = jnp.concatenate([hot, hot], axis=1)
        code = jnp.zeros_like(lane)
        for c in range(CYCLES):
            code = jnp.where(cycle == c, orient_ref[layer * CYCLES + c], code)
        flipped_a = jnp.where(code % 2 == 1, NODE_1D - 1 - lead, lead)
        flipped_b = jnp.where(code // 2 % 2 == 1, NODE_1D - 1 - trail, trail)
        x = jnp.where(code // 4 % 2 == 1, flipped_a, flipped_b)
        inner = jnp.logical_and(cycle == 0, x == 0)
        outer = jnp.logical_and(cycle == CYCLES - 1, x == NODE_1D - 1)
        on_wall = jnp.logical_or(inner, outer)
        cols = slice(g * LANES, (g + 1) * LANES)
        held = pl.ds(pl.multiple_of(layer * LANES, LANES), LANES)
        many = 9 if modes % 8 == 0 else 1
        for start in range(0, 9, many):
            rates = []
            for c in range(start, start + many):
                f = SLOT_OF[c]
                below, rate, above = [layers[g + d][f] for d in range(3)]
                other = jnp.where(low_rows, rolled(below, 1 - NODE_1D), rolled(above, NODE_1D - 1))
                rates.append(jnp.where(jnp.logical_or(top, low_rows), 0.5 * (rate + other), rate))
            rate = jnp.concatenate(rates, axis=0) if many > 1 else rates[0]
            high, low = split(rate)
            rate = STEP_DT * lax.dot_general(
                jnp.concatenate([high, low], axis=1),
                hot,
                (((1,), (1,)), ((), ())),
                preferred_element_type=F32,
            )
            for j in range(many):
                c = start + j
                own = rate[j * modes : (j + 1) * modes]
                if c < 3:
                    wall = jnp.where(inner, speed, 0.0) if c == 1 else 0.0
                    vel_out[c, :, cols] = jnp.where(on_wall, wall, vel_ref[c, :, held] + own)
                else:
                    logc_out[c - 3, :, cols] = logc_ref[c - 3, :, held] + own


def body(velocity, log_conf, orientation, wall_speed):
    n_dev = lax.axis_size("mode")
    modes = velocity.shape[1]
    fold = modes % 32 == 0
    head = (15, modes // 4, LANES) if fold else (4, modes, LANES)
    tail = (18, modes // 4, LANES) if fold else (5, modes, LANES)
    consts = [jnp.asarray(t) for t in tables()]
    hbm = pl.BlockSpec(memory_space=pltpu.HBM)
    free = pl.BlockSpec(memory_space=pl.ANY)
    smem = pl.BlockSpec(memory_space=pltpu.SMEM)
    dma = pltpu.SemaphoreType.DMA
    face_rows = PLANES + PLANES * CYCLES * NODE_1D // LANES
    first, second = pl.pallas_call(
        functools.partial(main_kernel, n_dev, modes, fold),
        out_shape=(
            jax.ShapeDtypeStruct((n_dev, *head), F32),
            jax.ShapeDtypeStruct((n_dev, *tail), F32),
        ),
        in_specs=[hbm, hbm, smem] + [hbm] * len(consts),
        out_specs=(free, free),
        scratch_shapes=[pltpu.VMEM(t.shape, t.dtype) for t in consts]
        + [
            pltpu.VMEM(log_conf.shape, F32),
            pltpu.VMEM((2, n_dev, 3, modes, LANES), F32),
            pltpu.VMEM((n_dev, 3, modes, LANES), F32),
            pltpu.VMEM((2, n_dev, 3, modes, LANES), F32),
            pltpu.VMEM((PLANES, 3 * LANES), BF),
            pltpu.VMEM((PLANES, 3 * LANES), BF),
            pltpu.VMEM((PLANES, 3 * LANES), BF),
            pltpu.VMEM((PLANES, 3 * LANES), BF),
            pltpu.VMEM((2 * PLANES, 3 * LANES), F32),
            pltpu.VMEM((2 * PLANES, 3 * LANES), F32),
            pltpu.VMEM((PLANES, 6 * LANES), F32),
            pltpu.VMEM((PLANES, 9 * LANES), F32),
            pltpu.VMEM((2, face_rows, LANES), F32),
            pltpu.VMEM((2, face_rows, LANES), F32),
            pltpu.VMEM((PLANES, 3 * LANES), F32),
            pltpu.VMEM((PLANES, 2 * LANES), F32),
            pltpu.VMEM((PLANES, 3 * LANES), BF),
            pltpu.VMEM((PLANES, 3 * LANES), BF),
            pltpu.VMEM((PLANES, 7 * LANES), BF),
            pltpu.VMEM((PLANES, 7 * LANES), BF),
            pltpu.VMEM((5, PLANES, LANES), F32),
            pltpu.VMEM((n_dev, *head), F32),
            pltpu.VMEM((n_dev, *tail), F32),
            dma((4,)),
            dma((len(consts),)),
            dma((n_dev,)),
            dma((n_dev,)),
            dma((2, n_dev)),
            dma((2, n_dev)),
            dma((2,)),
            dma((2,)),
            dma((2, n_dev)),
            dma((2, n_dev)),
        ],
        compiler_params=pltpu.CompilerParams(
            collective_id=0, has_side_effects=True, vmem_limit_bytes=36 * 2**20
        ),
        name="fields",
    )(*[pltpu.with_memory_space_constraint(v, pltpu.HBM) for v in (velocity, log_conf, orientation, *consts)])

    group = 8
    tile = group * LANES

    vmem = pl.BlockSpec(memory_space=pltpu.VMEM)
    return pl.pallas_call(
        functools.partial(final_kernel, n_dev, modes, fold, group),
        grid=(n_dev // group,),
        out_shape=(
            jax.ShapeDtypeStruct(velocity.shape, F32),
            jax.ShapeDtypeStruct(log_conf.shape, F32),
        ),
        in_specs=[
            smem,
            smem,
            vmem,
            vmem,
            vmem,
            vmem,
        ],
        out_specs=(
            pl.BlockSpec((3, modes, tile), lambda i: (0, 0, i)),
            pl.BlockSpec((6, modes, tile), lambda i: (0, 0, i)),
        ),
        compiler_params=pltpu.CompilerParams(vmem_limit_bytes=24 * 2**20),
        name="finish",
    )(pltpu.with_memory_space_constraint(orientation, pltpu.HBM), wall_speed, first, second, velocity, log_conf)


def solution(mesh):
    in_specs = (P("ens", "mode", None), P("ens", "mode", None), P(), P("ens"))
    out_specs = (P("ens", "mode", None), P("ens", "mode", None))
    return jax.shard_map(body, mesh=mesh, in_specs=in_specs, out_specs=out_specs, check_vma=False)
```

```python
import functools

import jax
import jax.numpy as jnp
import ml_dtypes
import numpy as np
from jax import lax
from jax.experimental import pallas as pl
from jax.experimental.pallas import tpu as pltpu
from jax.sharding import PartitionSpec as P

NODE_1D = 8
CYCLES = 2
PLANES = 512
CELL = NODE_1D * NODE_1D
LANES = CYCLES * CELL
KEPT = CELL - NODE_1D
INSIDE = LANES - LANES // 4
CHANNEL_OF = (0, 1, 2, 8, 3, 4, 5, 6, 7)
STEP_DT = 0.002
RELAX_TIME = 0.02
MOBILITY = 0.3
LAYER_HEIGHT = 0.25
R_INNER = 1.0
ROWS = 16
BF = jnp.bfloat16
F32 = jnp.float32
MESH = pl.DeviceIdType.MESH


def cheb_table(points):
    nodes_xi = -np.cos(np.pi * np.arange(points) / (points - 1))
    weights = np.ones(points)
    weights[0] = 2.0
    weights[-1] = 2.0
    weights = weights * (-1.0) ** np.arange(points)
    identity = np.eye(points)
    spacing = nodes_xi[:, None] - nodes_xi[None, :] + identity
    matrix = weights[:, None] / weights[None, :] / spacing
    matrix = matrix * (1.0 - identity)
    matrix = matrix - identity * matrix.sum(axis=1)[:, None]
    return (nodes_xi, matrix)


def halves(table):
    high = np.asarray(table, np.float32).astype(ml_dtypes.bfloat16)
    low = (np.asarray(table, np.float64) - high.astype(np.float64)).astype(ml_dtypes.bfloat16)
    return high, low


def tables():
    n = np.arange(PLANES)
    k = np.arange(PLANES // 2)
    angle = (n[:, None] * k[None, :] % PLANES) * (2.0 * np.pi / PLANES)
    cosine = np.cos(angle) * np.sqrt(2.0 / PLANES)
    sine = np.sin(angle) * np.sqrt(2.0 / PLANES)
    cosine[:, 0] = PLANES**-0.5
    sine[:, 0] = (-1.0) ** n * PLANES**-0.5
    basis = np.stack([cosine, sine], axis=2).reshape(PLANES, PLANES)
    dbasis = np.stack([-k * sine, k * cosine], axis=2).reshape(PLANES, PLANES)
    forward = np.concatenate([basis, dbasis], axis=0)
    backward = np.concatenate([basis.T, -dbasis.T], axis=1)

    xi, matrix = cheb_table(NODE_1D)
    eye, eyes = np.eye(NODE_1D), np.eye(CYCLES)
    cell_r = np.kron(matrix.T * (2.0 * CYCLES), eye)
    cell_z = np.kron(eye, matrix.T * (2.0 / LAYER_HEIGHT))
    d_r, d_z = np.kron(eyes, cell_r), np.kron(eyes, cell_z)
    mean = np.eye(CYCLES * NODE_1D)
    for c in range(1, CYCLES):
        i = c * NODE_1D
        mean[i - 1 : i + 1, i - 1 : i + 1] = 0.5
    mean = np.kron(mean, eye)
    weight = np.ones(NODE_1D)
    weight[0] = weight[-1] = 0.5
    weight = np.tile(weight, CYCLES * NODE_1D)
    mean_w = mean * weight[None, :]
    both = np.concatenate([d_r, d_z], axis=1)
    grad = np.concatenate([d_r @ mean_w, d_z @ mean_w], axis=1)
    div = np.kron(np.eye(2), np.concatenate([cell_r, cell_z], axis=0))
    return (
        *halves(forward),
        *halves(backward),
        np.concatenate([*halves(both), *halves(grad), mean_w.astype(ml_dtypes.bfloat16)], axis=1),
        np.concatenate(halves(div), axis=1),
    )


def inverse_radius(lane):
    xi, _ = cheb_table(NODE_1D)
    radius = R_INNER + (np.arange(CYCLES)[:, None] + (xi[None, :] + 1.0) / 2.0) / CYCLES
    total = jnp.zeros(lane.shape, F32)
    for i, r in enumerate(radius.reshape(-1)):
        total = jnp.where(lane // NODE_1D == i, float(1.0 / r), total)
    return total


def split(x):
    high = x.astype(BF)
    return high, (x - high.astype(F32)).astype(BF)


def dot(a, b):
    return jnp.dot(a, b, preferred_element_type=F32)


def dot3(ah, al, bh, bl):
    return dot(ah, bh) + (dot(ah, bl) + dot(al, bh))


def stored_of_grid(o, grid):
    side = NODE_1D
    y = grid % side
    x = grid // side % side
    swapped = o // 4 % 2 == 1
    a = jnp.where(swapped, x, y)
    b = jnp.where(swapped, y, x)
    a = jnp.where(o % 2 == 1, side - 1 - a, a)
    b = jnp.where(o // 2 % 2 == 1, side - 1 - b, b)
    return a * side + b


def stored_index(orient_ref, layer, grid):
    cycle = grid // CELL
    place = jnp.zeros_like(grid)
    for c in range(CYCLES):
        o = orient_ref[layer * CYCLES + c]
        place = jnp.where(cycle == c, c * CELL + stored_of_grid(o, grid), place)
    return place


def square(m):
    a, b, c, d, e, f = m
    bb, cc, ee = b * b, c * c, e * e
    return (
        a * a + bb + cc,
        b * (a + d) + c * e,
        c * (a + f) + b * e,
        bb + d * d + ee,
        e * (d + f) + b * c,
        cc + ee + f * f,
    )


def product(m, n):
    a, b, c, d, e, f = m
    p, q, r, s, t, u = n
    return (
        a * p + b * q + c * r,
        a * q + b * s + c * t,
        a * r + b * t + c * u,
        b * q + d * s + e * t,
        b * r + d * t + e * u,
        c * r + e * t + f * u,
    )


def exponentials(psi):
    x = tuple(v * 0.125 for v in psi)
    x2 = square(x)
    x3 = product(x, x2)
    x4 = square(x2)
    even = [x2[i] * 0.5 + x4[i] * (1.0 / 24.0) for i in range(6)]
    for i in (0, 3, 5):
        even[i] = even[i] + 1.0
    odd = [x[i] + x3[i] * (1.0 / 6.0) for i in range(6)]
    plus = tuple(even[i] + odd[i] for i in range(6))
    minus = tuple(even[i] - odd[i] for i in range(6))
    for _ in range(3):
        plus, minus = square(plus), square(minus)
    return plus, minus


def first_cycle(f):
    wall = NODE_1D if f < 3 else 0
    start = f * KEPT - min(f, 3) * NODE_1D
    return start // LANES, start % LANES, wall, KEPT - wall


def field(ref, f, rows=slice(None)):
    return ref[rows, f * LANES : (f + 1) * LANES]


def main_kernel(
    n_dev, modes, fold,
    vel_ref, logc_ref, orient_ref, fh_in, fl_in, bh_in, bl_in, node_in, div_in,
    out0_ref, out1_ref,
    fh_ref, fl_ref, bh_ref, bl_ref, node_ref, div_ref,
    raw, packed, xv, xp, xh, xl, ph, pw, vv, vp, dp, proj, face_out, face_in, conv, mom, sth, stl, rh, rl,
    kept, back0, back1,
    local_sem, const_sem, vs_sem, vr_sem, ps_sem, pr_sem, fs_sem, fr_sem, bs_sem, br_sem,
):
    me = lax.axis_index("mode")
    up = lax.rem(me + 1, n_dev)
    down = lax.rem(me + n_dev - 1, n_dev)

    barrier = pltpu.get_barrier_semaphore()

    def greet(k, carry):
        pl.semaphore_signal(
            barrier, inc=1, device_id={"mode": lax.rem(me + k, n_dev)}, device_id_type=MESH
        )
        return carry

    lax.fori_loop(1, n_dev, greet, 0)
    load_logc = pltpu.make_async_copy(logc_ref, raw, local_sem.at[0])
    load_logc.start()
    pl.semaphore_wait(barrier, n_dev - 1)

    side = n_dev // 2
    half_of = me // side

    def target(k):
        j = k // 2
        return lax.rem(half_of + lax.rem(k, 2), 2) * side + lax.rem(me + j, side)

    def columns(d):
        return pl.ds(pl.multiple_of(d * LANES, LANES), LANES)

    def every(do):
        def step(k, carry):
            do(k, target(k))
            return carry

        lax.fori_loop(1, n_dev, step, 0)

    def send_v(k, to, slot):
        return pltpu.make_async_remote_copy(
            src_ref=vel_ref.at[:, :, columns(to)],
            dst_ref=xv.at[slot],
            send_sem=vs_sem.at[k],
            recv_sem=vr_sem.at[slot],
            device_id={"mode": to},
            device_id_type=MESH,
        )

    def send_p(c, k, to, slot):
        return pltpu.make_async_remote_copy(
            src_ref=packed.at[c, to],
            dst_ref=xp.at[c, slot],
            send_sem=ps_sem.at[c, k],
            recv_sem=pr_sem.at[c, slot],
            device_id={"mode": to},
            device_id_type=MESH,
        )

    every(lambda k, to: send_v(k, to, me).start())
    own_v = pltpu.make_async_copy(vel_ref.at[:, :, columns(me)], xv.at[me], local_sem.at[1])
    own_v.start()
    loads = [
        pltpu.make_async_copy(a, b, const_sem.at[i])
        for i, (a, b) in enumerate(
            (
                (node_in, node_ref), (fh_in, fh_ref), (fl_in, fl_ref),
                (div_in, div_ref), (bh_in, bh_ref), (bl_in, bl_ref),
            )
        )
    ]
    for load in loads:
        load.start()

    lane = lax.broadcasted_iota(jnp.int32, (1, LANES), 1)
    lo = lane < CELL

    def swap(value):
        return pltpu.roll(value, CELL, 1)

    def pair_up(c, a, b):
        return jnp.where(lo, a, swap(b)) if c == 0 else jnp.where(lo, swap(a), b)

    load_logc.wait()
    own_p = [
        pltpu.make_async_copy(packed.at[c, me], xp.at[c, me], local_sem.at[2 + c]) for c in range(2)
    ]
    for c in range(2):

        def pack_psi(to, carry, c=c):
            at = columns(to)
            for p in range(3):
                packed[c, to, p] = pair_up(c, raw[2 * p, :, at], raw[2 * p + 1, :, at])
            return carry

        lax.fori_loop(0, n_dev, pack_psi, 0)
        if c == 0:
            every(lambda k, to: send_p(0, k, to, me).start())
        own_p[c].start()

    stored = lax.broadcasted_iota(jnp.int32, (LANES, LANES), 0)
    to_grid = jnp.where(stored_index(orient_ref, me, lane) == stored, 1.0, 0.0).astype(BF)

    half = PLANES // 2
    inv_r = inverse_radius(lane)
    for load in loads[:3]:
        load.wait()
    wide = 2 * LANES
    both_h, both_l, grad_h, grad_l = [node_ref.at[:, i * wide : (i + 1) * wide] for i in range(4)]
    mean_ref = node_ref.at[:, 4 * wide : 4 * wide + LANES]

    def vel_half(far):
        def step(k, carry):
            frm = target(2 * k + far)
            send_v(2 * k + far, frm, frm).wait_recv()
            return carry

        lax.fori_loop(1 - far, side, step, 0)
        which = lax.rem(half_of + far, 2)
        rows = pl.ds(pl.multiple_of(which * half, half), half)
        for f in range(3):
            high, low = split(xv[pl.ds(which * side, side), f].reshape(half, LANES))
            at = slice(f * LANES, (f + 1) * LANES)
            xh[rows, at] = dot(high, to_grid).astype(BF)
            xl[rows, at] = dot(low, to_grid).astype(BF)

        def velocity_block(i, carry):
            at = pl.ds(pl.multiple_of(i * half, half), half)
            total = dot3(fh_ref[at, rows], fl_ref[at, rows], xh[rows, :], xl[rows, :])
            vv[at, :] = vv[at, :] + total if far else total
            return carry

        lax.fori_loop(0, 4, velocity_block, 0)

    own_v.wait()
    vel_half(0)
    vel_half(1)

    def grad_block(i, carry):
        block = half // 2
        at = pl.ds(pl.multiple_of(i * block, block), block)
        dth_at = pl.ds(pl.multiple_of(PLANES + i * block, block), block)
        u = [field(vv, f, at) for f in range(3)]
        dth = [field(vv, f, dth_at) for f in range(3)]
        hoop = [(dth[0] - u[1]) * inv_r, (dth[1] + u[0]) * inv_r, dth[2] * inv_r]
        for f in range(3):
            uh, ul = split(u[f])
            both = dot3(uh, ul, grad_h[...], grad_l[...])
            hh, hl = split(hoop[f])
            g = (both[:, :LANES], dot(hh, mean_ref[...]) + dot(hl, mean_ref[...]), both[:, LANES:])
            for j in range(3):
                c = 3 * f + j
                proj[at, c * LANES : (c + 1) * LANES] = g[j]
        return carry

    lax.fori_loop(0, 4, grad_block, 0)

    groups = NODE_1D
    short = PLANES // groups

    def rolled(value, shift):
        return pltpu.roll(value, shift % LANES, 1) if shift % LANES else value

    def face_copy(slot, to):
        return pltpu.make_async_remote_copy(
            src_ref=face_out.at[slot],
            dst_ref=face_in.at[slot],
            send_sem=fs_sem.at[slot],
            recv_sem=fr_sem.at[slot],
            device_id={"mode": to},
            device_id_type=MESH,
        )

    faces = (face_copy(0, up), face_copy(1, down))
    for slot, start in ((0, NODE_1D - 1), (1, 0)):

        def pack(i, carry, slot=slot, start=start):
            at = pl.ds(pl.multiple_of(i * 64, 64), 64)
            total = jnp.zeros((64, LANES), F32)
            for c in range(groups):
                total = jnp.where(lane % groups == c, rolled(field(proj, c, at), c - start), total)
            face_out[slot, at, :] = total
            return carry

        lax.fori_loop(0, PLANES // 64, pack, 0)
        total = jnp.zeros((short, LANES), F32)
        for b in range(groups):
            moved = field(proj, 8, slice(b * short, (b + 1) * short))
            total = jnp.where(lane % groups == b, rolled(moved, b - start), total)
        face_out[slot, PLANES:, :] = total
        faces[slot].start()

    for face in faces:
        face.wait()
    every(lambda k, to: send_p(1, k, to, me).start())

    top = lane % NODE_1D == NODE_1D - 1
    low_rows = lane % NODE_1D == 0

    def unpacked(from_down, from_up, c):
        below = rolled(from_down, -c)
        above = rolled(from_up, NODE_1D - 1 - c)
        return jnp.where(top, above, jnp.where(low_rows, below, 0.0))

    for b in range(groups):

        def face_block(i, carry, b=b):
            start = pl.multiple_of(b * short + i * ROWS, ROWS)
            at = pl.ds(start, ROWS)
            nine = pl.ds(pl.multiple_of(PLANES + i * ROWS, ROWS), ROWS)
            down_face, up_face = face_in[0, at, :], face_in[1, at, :]
            g = [field(proj, c, at) + unpacked(down_face, up_face, c) for c in range(8)]
            g.append(field(proj, 8, at) + unpacked(face_in[0, nine, :], face_in[1, nine, :], b))
            for c in range(9):
                proj[at, c * LANES : (c + 1) * LANES] = g[c]
            u = [field(vv, f, at) for f in range(3)]
            for f in range(3):
                total = g[3 * f] * u[0] + g[3 * f + 1] * u[1] + g[3 * f + 2] * u[2]
                conv[at, f * LANES : (f + 1) * LANES] = -total
            return carry

        lax.fori_loop(0, short // ROWS, face_block, 0)

    def put_rate(at, f, value):
        high, low = split(value)
        rh[at, f * LANES : (f + 1) * LANES] = high
        rl[at, f * LANES : (f + 1) * LANES] = low

    share = PLANES // 4
    per = share // modes
    quarter = me // per
    backs, outs = (back0, back1), (out0_ref, out1_ref)
    diag = (0, 3, 5)

    def give(c, to, slot):
        return pltpu.make_async_remote_copy(
            src_ref=backs[c].at[to],
            dst_ref=outs[c].at[slot],
            send_sem=bs_sem.at[c, to],
            recv_sem=br_sem.at[c, slot],
            device_id={"mode": to},
            device_id_type=MESH,
        )

    def quarters(value):
        return value.reshape(per, 4, modes // 4, LANES)

    def cycle_part(c):
        in_c = lo if c == 0 else jnp.logical_not(lo)
        o = orient_ref[me * CYCLES + c]
        place = stored_of_grid(o, lane) + lane // CELL * CELL
        cell_grid = jnp.where(place == stored, 1.0, 0.0).astype(BF)

        def conf_half(far):
            which = lax.rem(half_of + far, 2)
            rows = pl.ds(pl.multiple_of(which * half, half), half)
            for p in range(3):
                high, low = split(xp[c, pl.ds(which * side, side), p].reshape(half, LANES))
                at = slice(p * LANES, (p + 1) * LANES)
                ph[rows, at] = dot(high, cell_grid).astype(BF)
                pw[rows, at] = dot(low, cell_grid).astype(BF)

            def conf_block(i, carry):
                at = pl.ds(pl.multiple_of(i * half, half), half)
                total = dot3(fh_ref[at, rows], fl_ref[at, rows], ph[rows, :], pw[rows, :])
                vp[at, :] = vp[at, :] + total if far else total
                return carry

            lax.fori_loop(0, 4, conf_block, 0)

        def recv_half(far):
            def step(k, carry):
                frm = target(2 * k + far)
                send_p(c, 2 * k + far, frm, frm).wait_recv()
                return carry

            lax.fori_loop(1 - far, side, step, 0)

        own_p[c].wait()
        recv_half(0)
        conf_half(0)
        recv_half(1)
        conf_half(1)

        def deriv_block(i, carry):
            at = pl.ds(pl.multiple_of(i * half, half), half)
            for p in range(3):
                high, low = split(field(vp, p, at))
                dp[at, 2 * p * LANES : (2 * p + 2) * LANES] = dot3(high, low, both_h[...], both_l[...])
            return carry

        lax.fori_loop(0, 2, deriv_block, 0)

        def local_block(i, carry):
            at = pl.ds(pl.multiple_of(i * ROWS, ROWS), ROWS)
            dth_at = pl.ds(pl.multiple_of(PLANES + i * ROWS, ROWS), ROWS)
            u_r, u_t, u_z = [field(vv, f, at) for f in range(3)]
            spin = u_t * inv_r
            ur2, spin2, uz2 = [jnp.where(in_c, v, swap(v)) for v in (u_r, spin, u_z)]
            psi, advect = [], []
            for p in range(3):
                value = field(vp, p, at)
                other = swap(value)
                for h in range(2):
                    psi.append(jnp.where(in_c, value if h == c else other, 0.0))
                advect.append(
                    ur2 * field(dp, 2 * p, at) + spin2 * field(vp, p, dth_at) + uz2 * field(dp, 2 * p + 1, at)
                )
            conform, inverse = exponentials(psi)
            g = [field(proj, j, at) for j in range(9)]
            wa, wb, wc = 0.5 * (g[1] - g[3]), 0.5 * (g[2] - g[6]), 0.5 * (g[5] - g[7])
            wa2 = wa + spin
            r0 = [wa2 * psi[1] + wb * psi[2], wa2 * psi[3] + wb * psi[4], wa2 * psi[4] + wb * psi[5]]
            r1 = [wc * psi[2] - wa2 * psi[0], wc * psi[4] - wa2 * psi[1], wc * psi[5] - wa2 * psi[2]]
            r2 = [-(wb * psi[j] + wc * psi[k]) for j, k in ((0, 1), (1, 3), (2, 4))]
            rate = [
                2.0 * (r0[0] + g[0]),
                r0[1] + r1[0] + (g[1] + g[3]),
                r0[2] + r2[0] + (g[2] + g[6]),
                2.0 * (r1[1] + g[4]),
                r1[2] + r2[1] + (g[5] + g[7]),
                2.0 * (r2[2] + g[8]),
            ]
            for m in range(6):
                unit = 1.0 if m in diag else 0.0
                rate[m] = rate[m] - (1.0 / RELAX_TIME) * (
                    unit - inverse[m] + MOBILITY * (conform[m] - 2.0 * unit + inverse[m])
                )
            stress = [conform[m] - 1.0 if m in diag else conform[m] for m in range(6)]
            for f, (m, n) in enumerate(((0, 2), (1, 4), (2, 5))):
                high, low = split(pair_up(c, stress[m], stress[n]))
                sth[at, f * LANES : (f + 1) * LANES] = high
                stl[at, f * LANES : (f + 1) * LANES] = low
            hoop = [stress[m] * inv_r for m in (1, 3, 4)]
            base = [
                field(conv, 0, at) + (stress[0] - stress[3]) * inv_r,
                field(conv, 1, at) + 2.0 * hoop[0],
                field(conv, 2, at) + stress[2] * inv_r,
            ]
            mom[at, :LANES] = pair_up(c, base[0], base[1])
            mom[at, LANES:] = pair_up(c, base[2], rate[5]) - jnp.where(lo, 0.0, advect[2])
            put_rate(at, 2, pair_up(c, rate[0], rate[1]) - advect[0])
            put_rate(at, 3, pair_up(c, rate[2], rate[3]) - advect[1])
            first = rate[4] if c == 0 else swap(rate[4])
            put_rate(at, 4, jnp.where(lo, first - advect[2], 0.0))
            put_rate(at, 5, pair_up(c, hoop[0], hoop[1]))
            last = hoop[2] if c == 0 else swap(hoop[2])
            put_rate(at, 6, jnp.where(lo, last, 0.0))
            return carry

        lax.fori_loop(0, PLANES // ROWS, local_block, 0)
        if c == 0:
            loads[3].wait()

        def div_block(i, carry):
            at = pl.ds(pl.multiple_of(i * half, half), half)
            for f, cols in enumerate((slice(0, wide), slice(wide, 3 * LANES))):
                depth = cols.stop - cols.start
                total = dot3(
                    sth[at, cols], stl[at, cols], div_ref[:depth, :LANES], div_ref[:depth, LANES:]
                )
                put_rate(at, f, field(mom, f, at) + total)
            return carry

        lax.fori_loop(0, 2, div_block, 0)
        if c == 0:
            for load in loads[4:]:
                load.wait()

        def back_block(step, carry):
            pair = lax.rem(quarter // 2 + 1 + step // 2, 2)
            i = pair * 2 + lax.rem(quarter + step + step // 2, 2)
            at = pl.ds(pl.multiple_of(i * share, share), share)
            dst = pl.ds(i * per, per)
            cols, hoops = slice(0, wide), slice(5 * LANES, 7 * LANES)
            total = dot3(bh_ref[at, :PLANES], bl_ref[at, :PLANES], rh[:, cols], rl[:, cols])
            total += dot3(bh_ref[at, PLANES:], bl_ref[at, PLANES:], rh[:, hoops], rl[:, hoops])
            coefs = [total[:, :LANES], total[:, LANES:]]
            cols = slice(wide, 5 * LANES)
            total = dot3(bh_ref[at, :PLANES], bl_ref[at, :PLANES], rh[:, cols], rl[:, cols])
            coefs += [total[:, j * LANES : (j + 1) * LANES] for j in range(3)]
            if c == 0:
                blocks = [None] * 4
                for f in range(9):
                    b, inside, wall, width = first_cycle(f)
                    moved = rolled(coefs[f // 2], inside - wall - f % 2 * CELL)
                    blocks[b] = moved if inside == 0 else jnp.where(lane < inside, blocks[b], moved)
                    if inside + width > LANES:
                        blocks[b + 1] = moved
                for p in range(4):
                    if not fold:
                        back0[dst, p] = blocks[p].reshape(per, modes, LANES)
                    elif p < 3:
                        back0[dst, 4 * p : 4 * p + 4] = quarters(blocks[p])
                    else:
                        value = quarters(blocks[p])
                        for j in range(3):
                            extra = quarters(rolled(blocks[p], INSIDE - j * (LANES // 4)))[:, 3]
                            back0[dst, 12 + j] = jnp.where(lane < INSIDE, value[:, j], extra)
                for p in range(5):
                    kept[p, at, :] = coefs[p]
            else:
                for p in range(5):
                    face = rolled(kept[p, at, :], NODE_1D - CELL)
                    coefs[p] = jnp.where(lane % CELL < NODE_1D, 0.5 * (coefs[p] + face), coefs[p])
                for p in range(5):
                    if not fold:
                        back1[dst, p] = coefs[p].reshape(per, modes, LANES)
                    elif p < 4:
                        back1[dst, 4 * p : 4 * p + 4] = quarters(coefs[p])
                    else:
                        value, upper = quarters(coefs[p]), quarters(swap(coefs[p]))
                        for j in range(2):
                            back1[dst, 16 + j] = jnp.where(lo, value[:, j], upper[:, 2 + j])

            def give_start(j, inner):
                to = i * per + lax.rem(me + j, per)

                @pl.when(to != me)
                def _():
                    give(c, to, me).start()

                return inner

            lax.fori_loop(0, per, give_start, 0)
            return carry

        lax.fori_loop(0, 4, back_block, 0)

    cycle_part(0)
    cycle_part(1)
    own = [pltpu.make_async_copy(backs[c].at[me], outs[c].at[me], local_sem.at[c]) for c in range(2)]
    for copy in own:
        copy.start()
    every(lambda k, to: send_v(k, to, me).wait_send())
    for c in range(2):
        every(lambda k, to, c=c: send_p(c, k, to, me).wait_send())
    for copy in own:
        copy.wait()

    def give_wait(k, to):
        for c in range(2):
            give(c, to, to).wait_recv()
            give(c, to, me).wait_send()

    every(give_wait)


def final_kernel(
    n_dev, modes, fold, group,
    orient_ref, wall_ref, first_ref, second_ref, vel_ref, logc_ref,
    vel_out, logc_out,
):
    step = pl.program_id(0)
    me = lax.axis_index("mode")
    lane = lax.broadcasted_iota(jnp.int32, (1, LANES), 1)
    lo = lane < CELL
    top = lane % NODE_1D == NODE_1D - 1
    low_rows = lane % NODE_1D == 0
    stored = lax.broadcasted_iota(jnp.int32, (LANES, LANES), 0)
    edge = jnp.logical_or(top, low_rows)
    jump = jnp.where(low_rows, NODE_1D - 1, jnp.where(top, 1 - NODE_1D, 0))
    weight = jnp.where(edge, 0.5 * STEP_DT, STEP_DT)
    mode_ids = me * modes + lax.broadcasted_iota(jnp.int32, (modes, 1), 0)
    speed = jnp.where(mode_ids == 0, wall_ref[0], 0.0)
    cycle = lane // CELL
    lead = lane // NODE_1D % NODE_1D
    trail = lane % NODE_1D

    def rolled(value, shift):
        return pltpu.roll(value, shift % LANES, 1) if shift % LANES else value

    def layer_fields(g):
        at = lax.rem(step * group + g + n_dev, n_dev)
        ref0, ref1 = first_ref, second_ref
        fields = []
        blocks = [ref0[at, p] if not fold else ref0[at, 4 * p : 4 * p + 4].reshape(modes, LANES) for p in range(3)]
        if not fold:
            blocks.append(ref0[at, 3])
        else:
            units = [ref0[at, 12 + j] for j in range(3)]
            piece = lane // (LANES // 4)
            outer = [rolled(units[j], (j + 1) * (LANES // 4)) for j in range(3)]
            units.append(jnp.where(piece == 0, outer[0], jnp.where(piece == 1, outer[1], outer[2])))
            blocks.append(jnp.concatenate(units, axis=0))
        for f in range(9):
            b, inside, wall, width = first_cycle(f)
            shift = wall - inside + (f + 1) % 2 * CELL
            zero = rolled(blocks[b], shift)
            if inside + width > LANES:
                zero = jnp.where(lane < shift + LANES, zero, rolled(blocks[b + 1], shift))
            p = f // 2
            if not fold:
                one = ref1[at, p]
            elif p < 4:
                one = ref1[at, 4 * p : 4 * p + 4].reshape(modes, LANES)
            else:
                one = ref1[at, 16:18].reshape(modes // 2, LANES)
                one = jnp.concatenate([one, rolled(one, CELL)], axis=0)
            fields.append(jnp.where(lo, zero, one) if f % 2 else jnp.where(lo, one, zero))
        return fields

    layers = [layer_fields(g) for g in range(-1, group + 1)]
    for g in range(group):
        layer = step * group + g
        hots = []
        for nat in ((lane + CELL) % LANES, lane):
            parts = []
            for to in (nat, nat + jump):
                here = jnp.logical_or(nat < KEPT, nat >= CELL)
                face = jnp.logical_and(nat >= CELL, nat < CELL + NODE_1D)
                if parts:
                    here, face = jnp.logical_and(here, edge), jnp.logical_and(face, edge)
                place = jnp.where(here, stored_index(orient_ref, layer, to), -1)
                twin = jnp.where(face, stored_index(orient_ref, layer, to - NODE_1D), -1)
                hit = jnp.logical_or(place == stored, twin == stored)
                parts += [jnp.where(hit, 1.0, 0.0).astype(BF)] * 2
            hots.append(jnp.concatenate(parts, axis=1))
        code = jnp.zeros_like(lane)
        for c in range(CYCLES):
            code = jnp.where(cycle == c, orient_ref[layer * CYCLES + c], code)
        flipped_a = jnp.where(code % 2 == 1, NODE_1D - 1 - lead, lead)
        flipped_b = jnp.where(code // 2 % 2 == 1, NODE_1D - 1 - trail, trail)
        x = jnp.where(code // 4 % 2 == 1, flipped_a, flipped_b)
        inner = jnp.logical_and(cycle == 0, x == 0)
        outer = jnp.logical_and(cycle == CYCLES - 1, x == NODE_1D - 1)
        on_wall = jnp.logical_or(inner, outer)
        cols = slice(g * LANES, (g + 1) * LANES)
        held = pl.ds(pl.multiple_of(layer * LANES, LANES), LANES)
        many = modes % 8 == 0
        for fields in ((0, 2, 4, 6, 8), (1, 3, 5, 7)) if many else [(f,) for f in range(9)]:
            rates, others = [], []
            for f in fields:
                below, rate, above = [layers[g + d][f] for d in range(3)]
                rates.append(weight * rate)
                others.append((0.5 * STEP_DT) * jnp.where(top, below, above))
            pieces = []
            for part in (rates, others):
                pieces += split(jnp.concatenate(part, axis=0) if many else part[0])
            total = lax.dot_general(
                jnp.concatenate(pieces, axis=1),
                hots[fields[0] % 2],
                (((1,), (1,)), ((), ())),
                preferred_element_type=F32,
            )
            for j, f in enumerate(fields):
                c = CHANNEL_OF[f]
                own = total[j * modes : (j + 1) * modes]
                if c < 3:
                    wall = jnp.where(inner, speed, 0.0) if c == 1 else 0.0
                    vel_out[c, :, cols] = jnp.where(on_wall, wall, vel_ref[c, :, held] + own)
                else:
                    logc_out[c - 3, :, cols] = logc_ref[c - 3, :, held] + own


def body(velocity, log_conf, orientation, wall_speed):
    n_dev = lax.axis_size("mode")
    modes = velocity.shape[1]
    fold = modes % 32 == 0
    head = (15, modes // 4, LANES) if fold else (4, modes, LANES)
    tail = (18, modes // 4, LANES) if fold else (5, modes, LANES)
    consts = [jnp.asarray(t) for t in tables()]
    hbm = pl.BlockSpec(memory_space=pltpu.HBM)
    free = pl.BlockSpec(memory_space=pl.ANY)
    smem = pl.BlockSpec(memory_space=pltpu.SMEM)
    dma = pltpu.SemaphoreType.DMA
    face_rows = PLANES + PLANES * CYCLES * NODE_1D // LANES
    first, second = pl.pallas_call(
        functools.partial(main_kernel, n_dev, modes, fold),
        out_shape=(
            jax.ShapeDtypeStruct((n_dev, *head), F32),
            jax.ShapeDtypeStruct((n_dev, *tail), F32),
        ),
        in_specs=[hbm, hbm, smem] + [hbm] * len(consts),
        out_specs=(free, free),
        scratch_shapes=[pltpu.VMEM(t.shape, t.dtype) for t in consts]
        + [
            pltpu.VMEM(log_conf.shape, F32),
            pltpu.VMEM((2, n_dev, 3, modes, LANES), F32),
            pltpu.VMEM((n_dev, 3, modes, LANES), F32),
            pltpu.VMEM((2, n_dev, 3, modes, LANES), F32),
            pltpu.VMEM((PLANES, 3 * LANES), BF),
            pltpu.VMEM((PLANES, 3 * LANES), BF),
            pltpu.VMEM((PLANES, 3 * LANES), BF),
            pltpu.VMEM((PLANES, 3 * LANES), BF),
            pltpu.VMEM((2 * PLANES, 3 * LANES), F32),
            pltpu.VMEM((2 * PLANES, 3 * LANES), F32),
            pltpu.VMEM((PLANES, 6 * LANES), F32),
            pltpu.VMEM((PLANES, 9 * LANES), F32),
            pltpu.VMEM((2, face_rows, LANES), F32),
            pltpu.VMEM((2, face_rows, LANES), F32),
            pltpu.VMEM((PLANES, 3 * LANES), F32),
            pltpu.VMEM((PLANES, 2 * LANES), F32),
            pltpu.VMEM((PLANES, 3 * LANES), BF),
            pltpu.VMEM((PLANES, 3 * LANES), BF),
            pltpu.VMEM((PLANES, 7 * LANES), BF),
            pltpu.VMEM((PLANES, 7 * LANES), BF),
            pltpu.VMEM((5, PLANES, LANES), F32),
            pltpu.VMEM((n_dev, *head), F32),
            pltpu.VMEM((n_dev, *tail), F32),
            dma((4,)),
            dma((len(consts),)),
            dma((n_dev,)),
            dma((n_dev,)),
            dma((2, n_dev)),
            dma((2, n_dev)),
            dma((2,)),
            dma((2,)),
            dma((2, n_dev)),
            dma((2, n_dev)),
        ],
        compiler_params=pltpu.CompilerParams(
            collective_id=0, has_side_effects=True, vmem_limit_bytes=36 * 2**20
        ),
        name="fields",
    )(*[pltpu.with_memory_space_constraint(v, pltpu.HBM) for v in (velocity, log_conf, orientation, *consts)])

    group = 8
    tile = group * LANES

    vmem = pl.BlockSpec(memory_space=pltpu.VMEM)
    return pl.pallas_call(
        functools.partial(final_kernel, n_dev, modes, fold, group),
        grid=(n_dev // group,),
        out_shape=(
            jax.ShapeDtypeStruct(velocity.shape, F32),
            jax.ShapeDtypeStruct(log_conf.shape, F32),
        ),
        in_specs=[
            smem,
            smem,
            vmem,
            vmem,
            vmem,
            vmem,
        ],
        out_specs=(
            pl.BlockSpec((3, modes, tile), lambda i: (0, 0, i)),
            pl.BlockSpec((6, modes, tile), lambda i: (0, 0, i)),
        ),
        compiler_params=pltpu.CompilerParams(vmem_limit_bytes=24 * 2**20),
        name="finish",
    )(pltpu.with_memory_space_constraint(orientation, pltpu.HBM), wall_speed, first, second, velocity, log_conf)


def solution(mesh):
    in_specs = (P("ens", "mode", None), P("ens", "mode", None), P(), P("ens"))
    out_specs = (P("ens", "mode", None), P("ens", "mode", None))
    return jax.shard_map(body, mesh=mesh, in_specs=in_specs, out_specs=out_specs, check_vma=False)
```

```python
import functools

import jax
import jax.numpy as jnp
import ml_dtypes
import numpy as np
from jax import lax
from jax.experimental import pallas as pl
from jax.experimental.pallas import tpu as pltpu
from jax.sharding import PartitionSpec as P

NODE_1D = 8
CYCLES = 2
PLANES = 512
CELL = NODE_1D * NODE_1D
LANES = CYCLES * CELL
KEPT = CELL - NODE_1D
INSIDE = LANES - LANES // 4
CHANNEL_OF = (0, 1, 2, 8, 3, 4, 5, 6, 7)
STEP_DT = 0.002
RELAX_TIME = 0.02
MOBILITY = 0.3
LAYER_HEIGHT = 0.25
R_INNER = 1.0
ROWS = 16
BF = jnp.bfloat16
F32 = jnp.float32
MESH = pl.DeviceIdType.MESH


def cheb_table(points):
    nodes_xi = -np.cos(np.pi * np.arange(points) / (points - 1))
    weights = np.ones(points)
    weights[0] = 2.0
    weights[-1] = 2.0
    weights = weights * (-1.0) ** np.arange(points)
    identity = np.eye(points)
    spacing = nodes_xi[:, None] - nodes_xi[None, :] + identity
    matrix = weights[:, None] / weights[None, :] / spacing
    matrix = matrix * (1.0 - identity)
    matrix = matrix - identity * matrix.sum(axis=1)[:, None]
    return (nodes_xi, matrix)


def halves(table):
    high = np.asarray(table, np.float32).astype(ml_dtypes.bfloat16)
    low = (np.asarray(table, np.float64) - high.astype(np.float64)).astype(ml_dtypes.bfloat16)
    return high, low


def tables():
    n = np.arange(PLANES)
    k = np.arange(PLANES // 2)
    angle = (n[:, None] * k[None, :] % PLANES) * (2.0 * np.pi / PLANES)
    cosine = np.cos(angle) * np.sqrt(2.0 / PLANES)
    sine = np.sin(angle) * np.sqrt(2.0 / PLANES)
    cosine[:, 0] = PLANES**-0.5
    sine[:, 0] = (-1.0) ** n * PLANES**-0.5
    basis = np.stack([cosine, sine], axis=2).reshape(PLANES, PLANES)
    dbasis = np.stack([-k * sine, k * cosine], axis=2).reshape(PLANES, PLANES)
    forward = np.concatenate([basis, dbasis], axis=0)
    backward = np.concatenate([basis.T, -dbasis.T], axis=1)

    xi, matrix = cheb_table(NODE_1D)
    eye, eyes = np.eye(NODE_1D), np.eye(CYCLES)
    cell_r = np.kron(matrix.T * (2.0 * CYCLES), eye)
    cell_z = np.kron(eye, matrix.T * (2.0 / LAYER_HEIGHT))
    d_r, d_z = np.kron(eyes, cell_r), np.kron(eyes, cell_z)
    mean = np.eye(CYCLES * NODE_1D)
    for c in range(1, CYCLES):
        i = c * NODE_1D
        mean[i - 1 : i + 1, i - 1 : i + 1] = 0.5
    mean = np.kron(mean, eye)
    weight = np.ones(NODE_1D)
    weight[0] = weight[-1] = 0.5
    weight = np.tile(weight, CYCLES * NODE_1D)
    mean_w = mean * weight[None, :]
    both = np.concatenate([d_r, d_z], axis=1)
    grad = np.concatenate([d_r @ mean_w, d_z @ mean_w], axis=1)
    div = np.kron(np.eye(2), np.concatenate([cell_r, cell_z], axis=0))
    return (
        *halves(forward),
        *halves(backward),
        np.concatenate([*halves(both), *halves(grad), mean_w.astype(ml_dtypes.bfloat16)], axis=1),
        np.concatenate(halves(div), axis=1),
    )


def inverse_radius(lane):
    xi, _ = cheb_table(NODE_1D)
    radius = R_INNER + (np.arange(CYCLES)[:, None] + (xi[None, :] + 1.0) / 2.0) / CYCLES
    total = jnp.zeros(lane.shape, F32)
    for i, r in enumerate(radius.reshape(-1)):
        total = jnp.where(lane // NODE_1D == i, float(1.0 / r), total)
    return total


def split(x):
    high = x.astype(BF)
    return high, (x - high.astype(F32)).astype(BF)


def dot(a, b):
    return jnp.dot(a, b, preferred_element_type=F32)


def dot3(ah, al, bh, bl):
    return dot(ah, bh) + (dot(ah, bl) + dot(al, bh))


def stored_of_grid(o, grid):
    side = NODE_1D
    y = grid % side
    x = grid // side % side
    swapped = o // 4 % 2 == 1
    a = jnp.where(swapped, x, y)
    b = jnp.where(swapped, y, x)
    a = jnp.where(o % 2 == 1, side - 1 - a, a)
    b = jnp.where(o // 2 % 2 == 1, side - 1 - b, b)
    return a * side + b


def stored_index(orient_ref, layer, grid):
    cycle = grid // CELL
    place = jnp.zeros_like(grid)
    for c in range(CYCLES):
        o = orient_ref[layer * CYCLES + c]
        place = jnp.where(cycle == c, c * CELL + stored_of_grid(o, grid), place)
    return place


def square(m):
    a, b, c, d, e, f = m
    bb, cc, ee = b * b, c * c, e * e
    return (
        a * a + bb + cc,
        b * (a + d) + c * e,
        c * (a + f) + b * e,
        bb + d * d + ee,
        e * (d + f) + b * c,
        cc + ee + f * f,
    )


def product(m, n):
    a, b, c, d, e, f = m
    p, q, r, s, t, u = n
    return (
        a * p + b * q + c * r,
        a * q + b * s + c * t,
        a * r + b * t + c * u,
        b * q + d * s + e * t,
        b * r + d * t + e * u,
        c * r + e * t + f * u,
    )


def exponentials(psi):
    x = tuple(v * 0.125 for v in psi)
    x2 = square(x)
    x3 = product(x, x2)
    x4 = square(x2)
    even = [x2[i] * 0.5 + x4[i] * (1.0 / 24.0) for i in range(6)]
    for i in (0, 3, 5):
        even[i] = even[i] + 1.0
    odd = [x[i] + x3[i] * (1.0 / 6.0) for i in range(6)]
    plus = tuple(even[i] + odd[i] for i in range(6))
    minus = tuple(even[i] - odd[i] for i in range(6))
    for _ in range(3):
        plus, minus = square(plus), square(minus)
    return plus, minus


def first_cycle(f):
    wall = NODE_1D if f < 3 else 0
    start = f * KEPT - min(f, 3) * NODE_1D
    return start // LANES, start % LANES, wall, KEPT - wall


def field(ref, f, rows=slice(None)):
    return ref[rows, f * LANES : (f + 1) * LANES]


def main_kernel(
    n_dev, modes, fold,
    vel_ref, logc_ref, orient_in, wall_ref, fh_in, fl_in, bh_in, bl_in, node_in, div_in,
    vel_out, logc_out,
    fh_ref, fl_ref, bh_ref, bl_ref, node_ref, div_ref,
    orient_ref, out0_ref, out1_ref, packed, xv, xp, xh, xl, ph, pw, vv, vp, dp, proj, face_out, face_in, conv, mom, sth, stl, rh, rl,
    kept, back0, back1,
    local_sem, const_sem, vs_sem, vr_sem, ps_sem, pr_sem, fs_sem, fr_sem, bs_sem, br_sem,
):
    me = lax.axis_index("mode")
    up = lax.rem(me + 1, n_dev)
    down = lax.rem(me + n_dev - 1, n_dev)

    barrier = pltpu.get_barrier_semaphore()

    def greet(k, carry):
        pl.semaphore_signal(
            barrier, inc=1, device_id={"mode": lax.rem(me + k, n_dev)}, device_id_type=MESH
        )
        return carry

    lax.fori_loop(1, n_dev, greet, 0)
    early = [
        pltpu.make_async_copy(a, b, local_sem.at[i])
        for i, (a, b) in ((0, (logc_ref, logc_out)), (4, (orient_in, orient_ref)))
    ]
    for copy in early:
        copy.start()
    pl.semaphore_wait(barrier, n_dev - 1)

    side = n_dev // 2
    half_of = me // side

    def target(k):
        j = k // 2
        return lax.rem(half_of + lax.rem(k, 2), 2) * side + lax.rem(me + j, side)

    def columns(d):
        return pl.ds(pl.multiple_of(d * LANES, LANES), LANES)

    def every(do):
        def step(k, carry):
            do(k, target(k))
            return carry

        lax.fori_loop(1, n_dev, step, 0)

    def send_v(k, to, slot):
        return pltpu.make_async_remote_copy(
            src_ref=vel_ref.at[:, :, columns(to)],
            dst_ref=xv.at[slot],
            send_sem=vs_sem.at[k],
            recv_sem=vr_sem.at[slot],
            device_id={"mode": to},
            device_id_type=MESH,
        )

    def send_p(c, k, to, slot):
        return pltpu.make_async_remote_copy(
            src_ref=packed.at[c, to],
            dst_ref=xp.at[c, slot],
            send_sem=ps_sem.at[c, k],
            recv_sem=pr_sem.at[c, slot],
            device_id={"mode": to},
            device_id_type=MESH,
        )

    every(lambda k, to: send_v(k, to, me).start())
    own_v = pltpu.make_async_copy(vel_ref.at[:, :, columns(me)], xv.at[me], local_sem.at[1])
    own_v.start()
    load_v = pltpu.make_async_copy(vel_ref, vel_out, local_sem.at[5])
    load_v.start()
    loads = [
        pltpu.make_async_copy(a, b, const_sem.at[i])
        for i, (a, b) in enumerate(
            (
                (node_in, node_ref), (fh_in, fh_ref), (fl_in, fl_ref),
                (div_in, div_ref), (bh_in, bh_ref), (bl_in, bl_ref),
            )
        )
    ]
    for load in loads:
        load.start()

    lane = lax.broadcasted_iota(jnp.int32, (1, LANES), 1)
    lo = lane < CELL

    def swap(value):
        return pltpu.roll(value, CELL, 1)

    def pair_up(c, a, b):
        return jnp.where(lo, a, swap(b)) if c == 0 else jnp.where(lo, swap(a), b)

    for copy in early:
        copy.wait()
    own_p = [
        pltpu.make_async_copy(packed.at[c, me], xp.at[c, me], local_sem.at[2 + c]) for c in range(2)
    ]
    for c in range(2):

        def pack_psi(to, carry, c=c):
            at = columns(to)
            for p in range(3):
                packed[c, to, p] = pair_up(c, logc_out[2 * p, :, at], logc_out[2 * p + 1, :, at])
            return carry

        lax.fori_loop(0, n_dev, pack_psi, 0)
        if c == 0:
            every(lambda k, to: send_p(0, k, to, me).start())
        own_p[c].start()

    stored = lax.broadcasted_iota(jnp.int32, (LANES, LANES), 0)
    to_grid = jnp.where(stored_index(orient_ref, me, lane) == stored, 1.0, 0.0).astype(BF)

    half = PLANES // 2
    inv_r = inverse_radius(lane)
    for load in loads[:3]:
        load.wait()
    wide = 2 * LANES
    both_h, both_l, grad_h, grad_l = [node_ref.at[:, i * wide : (i + 1) * wide] for i in range(4)]
    mean_ref = node_ref.at[:, 4 * wide : 4 * wide + LANES]

    def vel_half(far):
        def step(k, carry):
            frm = target(2 * k + far)
            send_v(2 * k + far, frm, frm).wait_recv()
            return carry

        lax.fori_loop(1 - far, side, step, 0)
        which = lax.rem(half_of + far, 2)
        rows = pl.ds(pl.multiple_of(which * half, half), half)
        for f in range(3):
            high, low = split(xv[pl.ds(which * side, side), f].reshape(half, LANES))
            at = slice(f * LANES, (f + 1) * LANES)
            xh[rows, at] = dot(high, to_grid).astype(BF)
            xl[rows, at] = dot(low, to_grid).astype(BF)

        def velocity_block(i, carry):
            at = pl.ds(pl.multiple_of(i * half, half), half)
            total = dot3(fh_ref[at, rows], fl_ref[at, rows], xh[rows, :], xl[rows, :])
            vv[at, :] = vv[at, :] + total if far else total
            return carry

        lax.fori_loop(0, 4, velocity_block, 0)

    own_v.wait()
    vel_half(0)
    vel_half(1)

    def grad_block(i, carry):
        block = half // 2
        at = pl.ds(pl.multiple_of(i * block, block), block)
        dth_at = pl.ds(pl.multiple_of(PLANES + i * block, block), block)
        u = [field(vv, f, at) for f in range(3)]
        dth = [field(vv, f, dth_at) for f in range(3)]
        hoop = [(dth[0] - u[1]) * inv_r, (dth[1] + u[0]) * inv_r, dth[2] * inv_r]
        for f in range(3):
            uh, ul = split(u[f])
            both = dot3(uh, ul, grad_h[...], grad_l[...])
            hh, hl = split(hoop[f])
            g = (both[:, :LANES], dot(hh, mean_ref[...]) + dot(hl, mean_ref[...]), both[:, LANES:])
            for j in range(3):
                c = 3 * f + j
                proj[at, c * LANES : (c + 1) * LANES] = g[j]
        return carry

    lax.fori_loop(0, 4, grad_block, 0)

    groups = NODE_1D
    short = PLANES // groups

    def rolled(value, shift):
        return pltpu.roll(value, shift % LANES, 1) if shift % LANES else value

    def face_copy(slot, to):
        return pltpu.make_async_remote_copy(
            src_ref=face_out.at[slot],
            dst_ref=face_in.at[slot],
            send_sem=fs_sem.at[slot],
            recv_sem=fr_sem.at[slot],
            device_id={"mode": to},
            device_id_type=MESH,
        )

    faces = (face_copy(0, up), face_copy(1, down))
    for slot, start in ((0, NODE_1D - 1), (1, 0)):

        def pack(i, carry, slot=slot, start=start):
            at = pl.ds(pl.multiple_of(i * 64, 64), 64)
            total = jnp.zeros((64, LANES), F32)
            for c in range(groups):
                total = jnp.where(lane % groups == c, rolled(field(proj, c, at), c - start), total)
            face_out[slot, at, :] = total
            return carry

        lax.fori_loop(0, PLANES // 64, pack, 0)
        total = jnp.zeros((short, LANES), F32)
        for b in range(groups):
            moved = field(proj, 8, slice(b * short, (b + 1) * short))
            total = jnp.where(lane % groups == b, rolled(moved, b - start), total)
        face_out[slot, PLANES:, :] = total
        faces[slot].start()

    for face in faces:
        face.wait()
    every(lambda k, to: send_p(1, k, to, me).start())

    def wall_lanes(layer):
        lead, trail = lane // NODE_1D % NODE_1D, lane % NODE_1D
        code = jnp.where(lo, orient_ref[layer * CYCLES], orient_ref[layer * CYCLES + 1])
        flipped_a = jnp.where(code % 2 == 1, NODE_1D - 1 - lead, lead)
        flipped_b = jnp.where(code // 2 % 2 == 1, NODE_1D - 1 - trail, trail)
        x = jnp.where(code // 4 % 2 == 1, flipped_a, flipped_b)
        inner = jnp.logical_and(lo, x == 0)
        outer = jnp.logical_and(jnp.logical_not(lo), x == NODE_1D - 1)
        return inner, jnp.logical_or(inner, outer)

    top = lane % NODE_1D == NODE_1D - 1
    low_rows = lane % NODE_1D == 0

    def unpacked(from_down, from_up, c):
        below = rolled(from_down, -c)
        above = rolled(from_up, NODE_1D - 1 - c)
        return jnp.where(top, above, jnp.where(low_rows, below, 0.0))

    for b in range(groups):

        def face_block(i, carry, b=b):
            start = pl.multiple_of(b * short + i * ROWS, ROWS)
            at = pl.ds(start, ROWS)
            nine = pl.ds(pl.multiple_of(PLANES + i * ROWS, ROWS), ROWS)
            down_face, up_face = face_in[0, at, :], face_in[1, at, :]
            g = [field(proj, c, at) + unpacked(down_face, up_face, c) for c in range(8)]
            g.append(field(proj, 8, at) + unpacked(face_in[0, nine, :], face_in[1, nine, :], b))
            for c in range(9):
                proj[at, c * LANES : (c + 1) * LANES] = g[c]
            u = [field(vv, f, at) for f in range(3)]
            for f in range(3):
                total = g[3 * f] * u[0] + g[3 * f + 1] * u[1] + g[3 * f + 2] * u[2]
                conv[at, f * LANES : (f + 1) * LANES] = -total
            return carry

        lax.fori_loop(0, short // ROWS, face_block, 0)

    def put_rate(at, f, value):
        high, low = split(value)
        rh[at, f * LANES : (f + 1) * LANES] = high
        rl[at, f * LANES : (f + 1) * LANES] = low

    share = PLANES // 4
    per = share // modes
    quarter = me // per
    backs, outs = (back0, back1), (out0_ref, out1_ref)
    diag = (0, 3, 5)

    def give(c, to, slot):
        return pltpu.make_async_remote_copy(
            src_ref=backs[c].at[to],
            dst_ref=outs[c].at[slot],
            send_sem=bs_sem.at[c, to],
            recv_sem=br_sem.at[c, slot],
            device_id={"mode": to},
            device_id_type=MESH,
        )

    def quarters(value):
        return value.reshape(per, 4, modes // 4, LANES)

    def cycle_part(c):
        in_c = lo if c == 0 else jnp.logical_not(lo)
        o = orient_ref[me * CYCLES + c]
        place = stored_of_grid(o, lane) + lane // CELL * CELL
        cell_grid = jnp.where(place == stored, 1.0, 0.0).astype(BF)

        def conf_half(far):
            which = lax.rem(half_of + far, 2)
            rows = pl.ds(pl.multiple_of(which * half, half), half)
            for p in range(3):
                high, low = split(xp[c, pl.ds(which * side, side), p].reshape(half, LANES))
                at = slice(p * LANES, (p + 1) * LANES)
                ph[rows, at] = dot(high, cell_grid).astype(BF)
                pw[rows, at] = dot(low, cell_grid).astype(BF)

            def conf_block(i, carry):
                at = pl.ds(pl.multiple_of(i * half, half), half)
                total = dot3(fh_ref[at, rows], fl_ref[at, rows], ph[rows, :], pw[rows, :])
                vp[at, :] = vp[at, :] + total if far else total
                return carry

            lax.fori_loop(0, 4, conf_block, 0)

        def recv_half(far):
            def step(k, carry):
                frm = target(2 * k + far)
                send_p(c, 2 * k + far, frm, frm).wait_recv()
                return carry

            lax.fori_loop(1 - far, side, step, 0)

        own_p[c].wait()
        recv_half(0)
        conf_half(0)
        recv_half(1)
        conf_half(1)

        def deriv_block(i, carry):
            at = pl.ds(pl.multiple_of(i * half, half), half)
            for p in range(3):
                high, low = split(field(vp, p, at))
                dp[at, 2 * p * LANES : (2 * p + 2) * LANES] = dot3(high, low, both_h[...], both_l[...])
            return carry

        lax.fori_loop(0, 2, deriv_block, 0)

        def local_block(i, carry):
            at = pl.ds(pl.multiple_of(i * ROWS, ROWS), ROWS)
            dth_at = pl.ds(pl.multiple_of(PLANES + i * ROWS, ROWS), ROWS)
            u_r, u_t, u_z = [field(vv, f, at) for f in range(3)]
            spin = u_t * inv_r
            ur2, spin2, uz2 = [jnp.where(in_c, v, swap(v)) for v in (u_r, spin, u_z)]
            psi, advect = [], []
            for p in range(3):
                value = field(vp, p, at)
                other = swap(value)
                for h in range(2):
                    psi.append(jnp.where(in_c, value if h == c else other, 0.0))
                advect.append(
                    ur2 * field(dp, 2 * p, at) + spin2 * field(vp, p, dth_at) + uz2 * field(dp, 2 * p + 1, at)
                )
            conform, inverse = exponentials(psi)
            g = [field(proj, j, at) for j in range(9)]
            wa, wb, wc = 0.5 * (g[1] - g[3]), 0.5 * (g[2] - g[6]), 0.5 * (g[5] - g[7])
            wa2 = wa + spin
            r0 = [wa2 * psi[1] + wb * psi[2], wa2 * psi[3] + wb * psi[4], wa2 * psi[4] + wb * psi[5]]
            r1 = [wc * psi[2] - wa2 * psi[0], wc * psi[4] - wa2 * psi[1], wc * psi[5] - wa2 * psi[2]]
            r2 = [-(wb * psi[j] + wc * psi[k]) for j, k in ((0, 1), (1, 3), (2, 4))]
            rate = [
                2.0 * (r0[0] + g[0]),
                r0[1] + r1[0] + (g[1] + g[3]),
                r0[2] + r2[0] + (g[2] + g[6]),
                2.0 * (r1[1] + g[4]),
                r1[2] + r2[1] + (g[5] + g[7]),
                2.0 * (r2[2] + g[8]),
            ]
            for m in range(6):
                unit = 1.0 if m in diag else 0.0
                rate[m] = rate[m] - (1.0 / RELAX_TIME) * (
                    unit - inverse[m] + MOBILITY * (conform[m] - 2.0 * unit + inverse[m])
                )
            stress = [conform[m] - 1.0 if m in diag else conform[m] for m in range(6)]
            for f, (m, n) in enumerate(((0, 2), (1, 4), (2, 5))):
                high, low = split(pair_up(c, stress[m], stress[n]))
                sth[at, f * LANES : (f + 1) * LANES] = high
                stl[at, f * LANES : (f + 1) * LANES] = low
            hoop = [stress[m] * inv_r for m in (1, 3, 4)]
            base = [
                field(conv, 0, at) + (stress[0] - stress[3]) * inv_r,
                field(conv, 1, at) + 2.0 * hoop[0],
                field(conv, 2, at) + stress[2] * inv_r,
            ]
            mom[at, :LANES] = pair_up(c, base[0], base[1])
            mom[at, LANES:] = pair_up(c, base[2], rate[5]) - jnp.where(lo, 0.0, advect[2])
            put_rate(at, 2, pair_up(c, rate[0], rate[1]) - advect[0])
            put_rate(at, 3, pair_up(c, rate[2], rate[3]) - advect[1])
            first = rate[4] if c == 0 else swap(rate[4])
            put_rate(at, 4, jnp.where(lo, first - advect[2], 0.0))
            put_rate(at, 5, pair_up(c, hoop[0], hoop[1]))
            last = hoop[2] if c == 0 else swap(hoop[2])
            put_rate(at, 6, jnp.where(lo, last, 0.0))
            return carry

        lax.fori_loop(0, PLANES // ROWS, local_block, 0)
        if c == 0:
            loads[3].wait()

        def div_block(i, carry):
            at = pl.ds(pl.multiple_of(i * half, half), half)
            for f, cols in enumerate((slice(0, wide), slice(wide, 3 * LANES))):
                depth = cols.stop - cols.start
                total = dot3(
                    sth[at, cols], stl[at, cols], div_ref[:depth, :LANES], div_ref[:depth, LANES:]
                )
                put_rate(at, f, field(mom, f, at) + total)
            return carry

        lax.fori_loop(0, 2, div_block, 0)
        if c == 0:
            for load in loads[4:]:
                load.wait()

        def back_block(step, carry):
            pair = lax.rem(quarter // 2 + 1 + step // 2, 2)
            i = pair * 2 + lax.rem(quarter + step + step // 2, 2)
            at = pl.ds(pl.multiple_of(i * share, share), share)
            dst = pl.ds(i * per, per)
            cols, hoops = slice(0, wide), slice(5 * LANES, 7 * LANES)
            total = dot3(bh_ref[at, :PLANES], bl_ref[at, :PLANES], rh[:, cols], rl[:, cols])
            total += dot3(bh_ref[at, PLANES:], bl_ref[at, PLANES:], rh[:, hoops], rl[:, hoops])
            coefs = [total[:, :LANES], total[:, LANES:]]
            cols = slice(wide, 5 * LANES)
            total = dot3(bh_ref[at, :PLANES], bl_ref[at, :PLANES], rh[:, cols], rl[:, cols])
            coefs += [total[:, j * LANES : (j + 1) * LANES] for j in range(3)]
            if c == 0:
                blocks = [None] * 4
                for f in range(9):
                    b, inside, wall, width = first_cycle(f)
                    moved = rolled(coefs[f // 2], inside - wall - f % 2 * CELL)
                    blocks[b] = moved if inside == 0 else jnp.where(lane < inside, blocks[b], moved)
                    if inside + width > LANES:
                        blocks[b + 1] = moved
                for p in range(4):
                    if not fold:
                        back0[dst, p] = blocks[p].reshape(per, modes, LANES)
                    elif p < 3:
                        back0[dst, 4 * p : 4 * p + 4] = quarters(blocks[p])
                    else:
                        value = quarters(blocks[p])
                        for j in range(3):
                            extra = quarters(rolled(blocks[p], INSIDE - j * (LANES // 4)))[:, 3]
                            back0[dst, 12 + j] = jnp.where(lane < INSIDE, value[:, j], extra)
                for p in range(5):
                    kept[p, at, :] = coefs[p]
            else:
                for p in range(5):
                    face = rolled(kept[p, at, :], NODE_1D - CELL)
                    coefs[p] = jnp.where(lane % CELL < NODE_1D, 0.5 * (coefs[p] + face), coefs[p])
                for p in range(5):
                    if not fold:
                        back1[dst, p] = coefs[p].reshape(per, modes, LANES)
                    elif p < 4:
                        back1[dst, 4 * p : 4 * p + 4] = quarters(coefs[p])
                    else:
                        value, upper = quarters(coefs[p]), quarters(swap(coefs[p]))
                        for j in range(2):
                            back1[dst, 16 + j] = jnp.where(lo, value[:, j], upper[:, 2 + j])

            def give_start(j, inner):
                to = i * per + lax.rem(me + j, per)

                @pl.when(to != me)
                def _():
                    give(c, to, me).start()

                return inner

            lax.fori_loop(0, per, give_start, 0)
            return carry

        lax.fori_loop(0, 4, back_block, 0)

    cycle_part(0)
    cycle_part(1)
    own = [pltpu.make_async_copy(backs[c].at[me], outs[c].at[me], local_sem.at[c]) for c in range(2)]
    for copy in own:
        copy.start()
    load_v.wait()
    mode_ids = me * modes + lax.broadcasted_iota(jnp.int32, (modes, 1), 0)
    speed = jnp.where(mode_ids == 0, wall_ref[0], 0.0)

    def set_walls(layer, carry):
        inner, on_wall = wall_lanes(layer)
        at = columns(layer)
        for c in range(3):
            wall = jnp.where(inner, speed, 0.0) if c == 1 else 0.0
            vel_out[c, :, at] = jnp.where(on_wall, wall, vel_out[c, :, at])
        return carry

    lax.fori_loop(0, n_dev, set_walls, 0)
    every(lambda k, to: send_v(k, to, me).wait_send())
    for c in range(2):
        every(lambda k, to, c=c: send_p(c, k, to, me).wait_send())
    for copy in own:
        copy.wait()

    edge = jnp.logical_or(top, low_rows)
    weight = jnp.where(edge, 0.5 * STEP_DT, STEP_DT)
    joined = jnp.logical_and(lane >= CELL, lane < CELL + NODE_1D)

    def first_fields(at):
        if not fold:
            blocks = [out0_ref[at, p] for p in range(4)]
        else:
            blocks = [out0_ref[at, 4 * p : 4 * p + 4].reshape(modes, LANES) for p in range(3)]
            units = [out0_ref[at, 12 + j] for j in range(3)]
            piece = lane // (LANES // 4)
            outer = [rolled(units[j], (j + 1) * (LANES // 4)) for j in range(3)]
            units.append(jnp.where(piece == 0, outer[0], jnp.where(piece == 1, outer[1], outer[2])))
            blocks.append(jnp.concatenate(units, axis=0))
        fields = []
        for f in range(9):
            b, inside, wall, width = first_cycle(f)
            value = rolled(blocks[b], wall - inside)
            if inside + width > LANES:
                value = jnp.where(lane < wall + LANES - inside, value, rolled(blocks[b + 1], wall - inside))
            fields.append(value)
        return fields

    def second_fields(at):
        fields = []
        for f in range(9):
            p = f // 2
            if not fold:
                value = rolled(out1_ref[at, p], (f + 1) % 2 * CELL)
            elif p < 4:
                value = out1_ref[at, 4 * p : 4 * p + 4].reshape(modes, LANES)
                value = rolled(value, (f + 1) % 2 * CELL)
            else:
                value = out1_ref[at, 16:18].reshape(modes // 2, LANES)
                value = jnp.concatenate([rolled(value, CELL), value], axis=0)
            fields.append(value)
        return fields

    many = modes % 8 == 0

    def add_cycle(c):
        here = lane >= CELL if c else lane < KEPT

        def add_layer(order, carry):
            k = 2 * lax.rem(order, side) + order // side
            frm = target(k)

            @pl.when(k > 0)
            def _():
                give(c, frm, frm).wait_recv()
                give(c, frm, me).wait_send()

            fields = [weight * v for v in (second_fields if c else first_fields)(frm)]
            step = NODE_1D - 1
            cats = [jnp.concatenate(split(v), axis=1) for v in ([jnp.concatenate(fields, axis=0)] if many else fields)]
            layers = [lax.rem(frm + ahead, n_dev) for ahead in (0, 1, n_dev - 1)]
            hots = []
            for layer, shift, only in zip(layers, (0, -step, step), (None, top, low_rows)):
                valid = [v if only is None else jnp.logical_and(v, only) for v in (here, joined)]
                place = jnp.where(valid[0], stored_index(orient_ref, layer, lane + shift), -1)
                hit = place == stored
                if c:
                    twin = jnp.where(valid[1], stored_index(orient_ref, layer, lane + shift - NODE_1D), -1)
                    hit = jnp.logical_or(hit, twin == stored)
                hot = jnp.where(hit, 1.0, 0.0).astype(BF)
                hots.append(jnp.concatenate([hot, hot], axis=1))
            hots = jnp.concatenate(hots, axis=0)
            sums = [
                lax.dot_general(v, hots, (((1,), (1,)), ((), ())), preferred_element_type=F32) for v in cats
            ]
            for j, layer in enumerate(layers):
                _, on_wall = wall_lanes(layer)
                at = columns(layer)
                cols = slice(j * LANES, (j + 1) * LANES)
                for f in range(9):
                    total = sums[0][f * modes : (f + 1) * modes, cols] if many else sums[f][:, cols]
                    to = CHANNEL_OF[f]
                    if to < 3:
                        vel_out[to, :, at] += jnp.where(on_wall, 0.0, total)
                    else:
                        logc_out[to - 3, :, at] += total
            return carry

        lax.fori_loop(0, n_dev, add_layer, 0)

    add_cycle(0)
    add_cycle(1)


def store_kernel(vel_ref, logc_ref, vel_out, logc_out, sem):
    copies = [pltpu.make_async_copy(vel_ref.at[c], vel_out.at[c], sem.at[c]) for c in range(3)]
    copies += [pltpu.make_async_copy(logc_ref.at[c], logc_out.at[c], sem.at[3 + c]) for c in range(6)]
    for copy in copies:
        copy.start()
    for copy in copies:
        copy.wait()


def body(velocity, log_conf, orientation, wall_speed):
    n_dev = lax.axis_size("mode")
    modes = velocity.shape[1]
    fold = modes % 32 == 0
    head = (15, modes // 4, LANES) if fold else (4, modes, LANES)
    tail = (18, modes // 4, LANES) if fold else (5, modes, LANES)
    consts = [jnp.asarray(t) for t in tables()]
    hbm = pl.BlockSpec(memory_space=pltpu.HBM)
    vmem = pl.BlockSpec(memory_space=pltpu.VMEM)
    dma = pltpu.SemaphoreType.DMA
    face_rows = PLANES + PLANES * CYCLES * NODE_1D // LANES
    held = pl.pallas_call(
        functools.partial(main_kernel, n_dev, modes, fold),
        out_shape=(
            jax.ShapeDtypeStruct(velocity.shape, F32),
            jax.ShapeDtypeStruct(log_conf.shape, F32),
        ),
        in_specs=[hbm] * 3 + [pl.BlockSpec(memory_space=pltpu.SMEM)] + [hbm] * len(consts),
        out_specs=(vmem, vmem),
        scratch_shapes=[pltpu.VMEM(t.shape, t.dtype) for t in consts]
        + [
            pltpu.SMEM(orientation.shape, jnp.int32),
            pltpu.VMEM((n_dev, *head), F32),
            pltpu.VMEM((n_dev, *tail), F32),
            pltpu.VMEM((2, n_dev, 3, modes, LANES), F32),
            pltpu.VMEM((n_dev, 3, modes, LANES), F32),
            pltpu.VMEM((2, n_dev, 3, modes, LANES), F32),
            pltpu.VMEM((PLANES, 3 * LANES), BF),
            pltpu.VMEM((PLANES, 3 * LANES), BF),
            pltpu.VMEM((PLANES, 3 * LANES), BF),
            pltpu.VMEM((PLANES, 3 * LANES), BF),
            pltpu.VMEM((2 * PLANES, 3 * LANES), F32),
            pltpu.VMEM((2 * PLANES, 3 * LANES), F32),
            pltpu.VMEM((PLANES, 6 * LANES), F32),
            pltpu.VMEM((PLANES, 9 * LANES), F32),
            pltpu.VMEM((2, face_rows, LANES), F32),
            pltpu.VMEM((2, face_rows, LANES), F32),
            pltpu.VMEM((PLANES, 3 * LANES), F32),
            pltpu.VMEM((PLANES, 2 * LANES), F32),
            pltpu.VMEM((PLANES, 3 * LANES), BF),
            pltpu.VMEM((PLANES, 3 * LANES), BF),
            pltpu.VMEM((PLANES, 7 * LANES), BF),
            pltpu.VMEM((PLANES, 7 * LANES), BF),
            pltpu.VMEM((5, PLANES, LANES), F32),
            pltpu.VMEM((n_dev, *head), F32),
            pltpu.VMEM((n_dev, *tail), F32),
            dma((6,)),
            dma((len(consts),)),
            dma((n_dev,)),
            dma((n_dev,)),
            dma((2, n_dev)),
            dma((2, n_dev)),
            dma((2,)),
            dma((2,)),
            dma((2, n_dev)),
            dma((2, n_dev)),
        ],
        compiler_params=pltpu.CompilerParams(
            collective_id=0, has_side_effects=True, vmem_limit_bytes=36 * 2**20
        ),
        name="fields",
    )(
        *[pltpu.with_memory_space_constraint(v, pltpu.HBM) for v in (velocity, log_conf, orientation)],
        wall_speed,
        *[pltpu.with_memory_space_constraint(v, pltpu.HBM) for v in consts],
    )

    free = pl.BlockSpec(memory_space=pl.ANY)
    return pl.pallas_call(
        store_kernel,
        out_shape=(
            jax.ShapeDtypeStruct(velocity.shape, F32),
            jax.ShapeDtypeStruct(log_conf.shape, F32),
        ),
        in_specs=[vmem, vmem],
        out_specs=(free, free),
        scratch_shapes=[dma((9,))],
        compiler_params=pltpu.CompilerParams(vmem_limit_bytes=8 * 2**20),
        name="store",
    )(*held)


def solution(mesh):
    in_specs = (P("ens", "mode", None), P("ens", "mode", None), P(), P("ens"))
    out_specs = (P("ens", "mode", None), P("ens", "mode", None))
    return jax.shard_map(body, mesh=mesh, in_specs=in_specs, out_specs=out_specs, check_vma=False)
```

```python
import functools

import jax
import jax.numpy as jnp
import ml_dtypes
import numpy as np
from jax import lax
from jax.experimental import pallas as pl
from jax.experimental.pallas import tpu as pltpu
from jax.sharding import PartitionSpec as P

NODE_1D = 8
CYCLES = 2
PLANES = 512
CELL = NODE_1D * NODE_1D
LANES = CYCLES * CELL
KEPT = CELL - NODE_1D
INSIDE = LANES - LANES // 4
CHANNEL_OF = (0, 1, 2, 8, 3, 4, 5, 6, 7)
STEP_DT = 0.002
RELAX_TIME = 0.02
MOBILITY = 0.3
LAYER_HEIGHT = 0.25
R_INNER = 1.0
ROWS = 16
BF = jnp.bfloat16
F32 = jnp.float32
MESH = pl.DeviceIdType.MESH


def cheb_table(points):
    nodes_xi = -np.cos(np.pi * np.arange(points) / (points - 1))
    weights = np.ones(points)
    weights[0] = 2.0
    weights[-1] = 2.0
    weights = weights * (-1.0) ** np.arange(points)
    identity = np.eye(points)
    spacing = nodes_xi[:, None] - nodes_xi[None, :] + identity
    matrix = weights[:, None] / weights[None, :] / spacing
    matrix = matrix * (1.0 - identity)
    matrix = matrix - identity * matrix.sum(axis=1)[:, None]
    return (nodes_xi, matrix)


def halves(table):
    high = np.asarray(table, np.float32).astype(ml_dtypes.bfloat16)
    low = (np.asarray(table, np.float64) - high.astype(np.float64)).astype(ml_dtypes.bfloat16)
    return high, low


def tables():
    n = np.arange(PLANES)
    k = np.arange(PLANES // 2)
    angle = (n[:, None] * k[None, :] % PLANES) * (2.0 * np.pi / PLANES)
    cosine = np.cos(angle) * np.sqrt(2.0 / PLANES)
    sine = np.sin(angle) * np.sqrt(2.0 / PLANES)
    cosine[:, 0] = PLANES**-0.5
    sine[:, 0] = (-1.0) ** n * PLANES**-0.5
    basis = np.stack([cosine, sine], axis=2).reshape(PLANES, PLANES)
    dbasis = np.stack([-k * sine, k * cosine], axis=2).reshape(PLANES, PLANES)
    forward = np.concatenate([basis, dbasis], axis=0)
    backward = np.concatenate([basis.T, -dbasis.T], axis=1)

    xi, matrix = cheb_table(NODE_1D)
    eye, eyes = np.eye(NODE_1D), np.eye(CYCLES)
    cell_r = np.kron(matrix.T * (2.0 * CYCLES), eye)
    cell_z = np.kron(eye, matrix.T * (2.0 / LAYER_HEIGHT))
    d_r, d_z = np.kron(eyes, cell_r), np.kron(eyes, cell_z)
    mean = np.eye(CYCLES * NODE_1D)
    for c in range(1, CYCLES):
        i = c * NODE_1D
        mean[i - 1 : i + 1, i - 1 : i + 1] = 0.5
    mean = np.kron(mean, eye)
    weight = np.ones(NODE_1D)
    weight[0] = weight[-1] = 0.5
    weight = np.tile(weight, CYCLES * NODE_1D)
    mean_w = mean * weight[None, :]
    both = np.concatenate([d_r, d_z], axis=1)
    grad = np.concatenate([d_r @ mean_w, d_z @ mean_w], axis=1)
    div = np.kron(np.eye(2), np.concatenate([cell_r, cell_z], axis=0))
    return (
        *halves(forward),
        *halves(backward),
        np.concatenate([*halves(both), *halves(grad), mean_w.astype(ml_dtypes.bfloat16)], axis=1),
        np.concatenate(halves(div), axis=1),
    )


def inverse_radius(lane):
    xi, _ = cheb_table(NODE_1D)
    radius = R_INNER + (np.arange(CYCLES)[:, None] + (xi[None, :] + 1.0) / 2.0) / CYCLES
    total = jnp.zeros(lane.shape, F32)
    for i, r in enumerate(radius.reshape(-1)):
        total = jnp.where(lane // NODE_1D == i, float(1.0 / r), total)
    return total


def split(x):
    high = x.astype(BF)
    return high, (x - high.astype(F32)).astype(BF)


def dot(a, b):
    return jnp.dot(a, b, preferred_element_type=F32)


def dot3(ah, al, bh, bl):
    return dot(ah, bh) + (dot(ah, bl) + dot(al, bh))


def stored_of_grid(o, grid):
    side = NODE_1D
    y = grid % side
    x = grid // side % side
    swapped = o // 4 % 2 == 1
    a = jnp.where(swapped, x, y)
    b = jnp.where(swapped, y, x)
    a = jnp.where(o % 2 == 1, side - 1 - a, a)
    b = jnp.where(o // 2 % 2 == 1, side - 1 - b, b)
    return a * side + b


def stored_index(orient_ref, layer, grid):
    cycle = grid // CELL
    place = jnp.zeros_like(grid)
    for c in range(CYCLES):
        o = orient_ref[layer * CYCLES + c]
        place = jnp.where(cycle == c, c * CELL + stored_of_grid(o, grid), place)
    return place


def square(m):
    a, b, c, d, e, f = m
    bb, cc, ee = b * b, c * c, e * e
    return (
        a * a + bb + cc,
        b * (a + d) + c * e,
        c * (a + f) + b * e,
        bb + d * d + ee,
        e * (d + f) + b * c,
        cc + ee + f * f,
    )


def product(m, n):
    a, b, c, d, e, f = m
    p, q, r, s, t, u = n
    return (
        a * p + b * q + c * r,
        a * q + b * s + c * t,
        a * r + b * t + c * u,
        b * q + d * s + e * t,
        b * r + d * t + e * u,
        c * r + e * t + f * u,
    )


def exponentials(psi):
    x = tuple(v * 0.125 for v in psi)
    x2 = square(x)
    x3 = product(x, x2)
    x4 = square(x2)
    even = [x2[i] * 0.5 + x4[i] * (1.0 / 24.0) for i in range(6)]
    for i in (0, 3, 5):
        even[i] = even[i] + 1.0
    odd = [x[i] + x3[i] * (1.0 / 6.0) for i in range(6)]
    plus = tuple(even[i] + odd[i] for i in range(6))
    minus = tuple(even[i] - odd[i] for i in range(6))
    for _ in range(3):
        plus, minus = square(plus), square(minus)
    return plus, minus


def first_cycle(f):
    wall = NODE_1D if f < 3 else 0
    start = f * KEPT - min(f, 3) * NODE_1D
    return start // LANES, start % LANES, wall, KEPT - wall


def field(ref, f, rows=slice(None)):
    return ref[rows, f * LANES : (f + 1) * LANES]


def main_kernel(
    n_dev, modes, fold,
    vel_ref, logc_ref, orient_in, wall_ref, fh_in, fl_in, bh_in, bl_in, node_in, div_in,
    vel_out, logc_out,
    fh_ref, fl_ref, bh_ref, bl_ref, node_ref, div_ref,
    orient_ref, out0_ref, out1_ref, packed, xv, xp, xh, xl, ph, pw, vv, vp, dp, proj, face_out, face_in, conv, mom, sth, stl, rh, rl,
    kept, back0, back1,
    local_sem, const_sem, vs_sem, vr_sem, ps_sem, pr_sem, fs_sem, fr_sem, bs_sem, br_sem,
):
    me = lax.axis_index("mode")
    up = lax.rem(me + 1, n_dev)
    down = lax.rem(me + n_dev - 1, n_dev)

    barrier = pltpu.get_barrier_semaphore()

    def greet(k, carry):
        pl.semaphore_signal(
            barrier, inc=1, device_id={"mode": lax.rem(me + k, n_dev)}, device_id_type=MESH
        )
        return carry

    lax.fori_loop(1, n_dev, greet, 0)
    early = [
        pltpu.make_async_copy(a, b, local_sem.at[i])
        for i, (a, b) in ((0, (logc_ref, logc_out)), (4, (orient_in, orient_ref)))
    ]
    for copy in early:
        copy.start()
    pl.semaphore_wait(barrier, n_dev - 1)

    side = n_dev // 2
    half_of = me // side

    def target(k):
        j = k // 2
        return lax.rem(half_of + lax.rem(k, 2), 2) * side + lax.rem(me + j, side)

    def columns(d):
        return pl.ds(pl.multiple_of(d * LANES, LANES), LANES)

    def every(do):
        def step(k, carry):
            do(k, target(k))
            return carry

        lax.fori_loop(1, n_dev, step, 0)

    def send_v(k, to, slot):
        return pltpu.make_async_remote_copy(
            src_ref=vel_ref.at[:, :, columns(to)],
            dst_ref=xv.at[slot],
            send_sem=vs_sem.at[k],
            recv_sem=vr_sem.at[slot],
            device_id={"mode": to},
            device_id_type=MESH,
        )

    def send_p(c, k, to, slot):
        return pltpu.make_async_remote_copy(
            src_ref=packed.at[c, to],
            dst_ref=xp.at[c, slot],
            send_sem=ps_sem.at[c, k],
            recv_sem=pr_sem.at[c, slot],
            device_id={"mode": to},
            device_id_type=MESH,
        )

    every(lambda k, to: send_v(k, to, me).start())
    own_v = pltpu.make_async_copy(vel_ref.at[:, :, columns(me)], xv.at[me], local_sem.at[1])
    own_v.start()
    load_v = pltpu.make_async_copy(vel_ref, vel_out, local_sem.at[5])
    load_v.start()
    loads = [
        pltpu.make_async_copy(a, b, const_sem.at[i])
        for i, (a, b) in enumerate(
            (
                (node_in, node_ref), (fh_in, fh_ref), (fl_in, fl_ref),
                (div_in, div_ref), (bh_in, bh_ref), (bl_in, bl_ref),
            )
        )
    ]
    for load in loads:
        load.start()

    lane = lax.broadcasted_iota(jnp.int32, (1, LANES), 1)
    lo = lane < CELL

    def swap(value):
        return pltpu.roll(value, CELL, 1)

    def pair_up(c, a, b):
        return jnp.where(lo, a, swap(b)) if c == 0 else jnp.where(lo, swap(a), b)

    for copy in early:
        copy.wait()
    own_p = [
        pltpu.make_async_copy(packed.at[c, me], xp.at[c, me], local_sem.at[2 + c]) for c in range(2)
    ]
    for c in range(2):

        def pack_psi(to, carry, c=c):
            at = columns(to)
            for p in range(3):
                packed[c, to, p] = pair_up(c, logc_out[2 * p, :, at], logc_out[2 * p + 1, :, at])
            return carry

        lax.fori_loop(0, n_dev, pack_psi, 0)
        if c == 0:
            every(lambda k, to: send_p(0, k, to, me).start())
        own_p[c].start()

    stored = lax.broadcasted_iota(jnp.int32, (LANES, LANES), 0)
    to_grid = jnp.where(stored_index(orient_ref, me, lane) == stored, 1.0, 0.0).astype(BF)

    half = PLANES // 2
    inv_r = inverse_radius(lane)
    for load in loads[:3]:
        load.wait()
    wide = 2 * LANES
    both_h, both_l, grad_h, grad_l = [node_ref.at[:, i * wide : (i + 1) * wide] for i in range(4)]
    mean_ref = node_ref.at[:, 4 * wide : 4 * wide + LANES]

    def vel_half(far):
        def step(k, carry):
            frm = target(2 * k + far)
            send_v(2 * k + far, frm, frm).wait_recv()
            return carry

        lax.fori_loop(1 - far, side, step, 0)
        which = lax.rem(half_of + far, 2)
        rows = pl.ds(pl.multiple_of(which * half, half), half)
        for f in range(3):
            high, low = split(xv[pl.ds(which * side, side), f].reshape(half, LANES))
            at = slice(f * LANES, (f + 1) * LANES)
            xh[rows, at] = dot(high, to_grid).astype(BF)
            xl[rows, at] = dot(low, to_grid).astype(BF)

        def velocity_block(i, carry):
            at = pl.ds(pl.multiple_of(i * half, half), half)
            total = dot3(fh_ref[at, rows], fl_ref[at, rows], xh[rows, :], xl[rows, :])
            vv[at, :] = vv[at, :] + total if far else total
            return carry

        lax.fori_loop(0, 4, velocity_block, 0)

    own_v.wait()
    vel_half(0)
    vel_half(1)

    def grad_block(i, carry):
        block = half // 2
        at = pl.ds(pl.multiple_of(i * block, block), block)
        dth_at = pl.ds(pl.multiple_of(PLANES + i * block, block), block)
        u = [field(vv, f, at) for f in range(3)]
        dth = [field(vv, f, dth_at) for f in range(3)]
        hoop = [(dth[0] - u[1]) * inv_r, (dth[1] + u[0]) * inv_r, dth[2] * inv_r]
        for f in range(3):
            uh, ul = split(u[f])
            both = dot3(uh, ul, grad_h[...], grad_l[...])
            hh, hl = split(hoop[f])
            g = (both[:, :LANES], dot(hh, mean_ref[...]) + dot(hl, mean_ref[...]), both[:, LANES:])
            for j in range(3):
                c = 3 * f + j
                proj[at, c * LANES : (c + 1) * LANES] = g[j]
        return carry

    lax.fori_loop(0, 4, grad_block, 0)

    groups = NODE_1D
    short = PLANES // groups

    def rolled(value, shift):
        return pltpu.roll(value, shift % LANES, 1) if shift % LANES else value

    def face_copy(slot, to):
        return pltpu.make_async_remote_copy(
            src_ref=face_out.at[slot],
            dst_ref=face_in.at[slot],
            send_sem=fs_sem.at[slot],
            recv_sem=fr_sem.at[slot],
            device_id={"mode": to},
            device_id_type=MESH,
        )

    faces = (face_copy(0, up), face_copy(1, down))
    for slot, start in ((0, NODE_1D - 1), (1, 0)):

        def pack(i, carry, slot=slot, start=start):
            at = pl.ds(pl.multiple_of(i * 64, 64), 64)
            total = jnp.zeros((64, LANES), F32)
            for c in range(groups):
                total = jnp.where(lane % groups == c, rolled(field(proj, c, at), c - start), total)
            face_out[slot, at, :] = total
            return carry

        lax.fori_loop(0, PLANES // 64, pack, 0)
        total = jnp.zeros((short, LANES), F32)
        for b in range(groups):
            moved = field(proj, 8, slice(b * short, (b + 1) * short))
            total = jnp.where(lane % groups == b, rolled(moved, b - start), total)
        face_out[slot, PLANES:, :] = total
        faces[slot].start()

    for face in faces:
        face.wait()
    every(lambda k, to: send_p(1, k, to, me).start())

    def wall_lanes(layer):
        lead, trail = lane // NODE_1D % NODE_1D, lane % NODE_1D
        code = jnp.where(lo, orient_ref[layer * CYCLES], orient_ref[layer * CYCLES + 1])
        flipped_a = jnp.where(code % 2 == 1, NODE_1D - 1 - lead, lead)
        flipped_b = jnp.where(code // 2 % 2 == 1, NODE_1D - 1 - trail, trail)
        x = jnp.where(code // 4 % 2 == 1, flipped_a, flipped_b)
        inner = jnp.logical_and(lo, x == 0)
        outer = jnp.logical_and(jnp.logical_not(lo), x == NODE_1D - 1)
        return inner, jnp.logical_or(inner, outer)

    top = lane % NODE_1D == NODE_1D - 1
    low_rows = lane % NODE_1D == 0

    def unpacked(from_down, from_up, c):
        below = rolled(from_down, -c)
        above = rolled(from_up, NODE_1D - 1 - c)
        return jnp.where(top, above, jnp.where(low_rows, below, 0.0))

    for b in range(groups):

        def face_block(i, carry, b=b):
            start = pl.multiple_of(b * short + i * ROWS, ROWS)
            at = pl.ds(start, ROWS)
            nine = pl.ds(pl.multiple_of(PLANES + i * ROWS, ROWS), ROWS)
            down_face, up_face = face_in[0, at, :], face_in[1, at, :]
            g = [field(proj, c, at) + unpacked(down_face, up_face, c) for c in range(8)]
            g.append(field(proj, 8, at) + unpacked(face_in[0, nine, :], face_in[1, nine, :], b))
            for c in range(9):
                proj[at, c * LANES : (c + 1) * LANES] = g[c]
            u = [field(vv, f, at) for f in range(3)]
            for f in range(3):
                total = g[3 * f] * u[0] + g[3 * f + 1] * u[1] + g[3 * f + 2] * u[2]
                conv[at, f * LANES : (f + 1) * LANES] = -total
            return carry

        lax.fori_loop(0, short // ROWS, face_block, 0)

    def put_rate(at, f, value):
        high, low = split(value)
        rh[at, f * LANES : (f + 1) * LANES] = high
        rl[at, f * LANES : (f + 1) * LANES] = low

    share = PLANES // 4
    per = share // modes
    quarter = me // per
    backs, outs = (back0, back1), (out0_ref, out1_ref)
    diag = (0, 3, 5)

    def give(c, to, slot):
        return pltpu.make_async_remote_copy(
            src_ref=backs[c].at[to],
            dst_ref=outs[c].at[slot],
            send_sem=bs_sem.at[c, to],
            recv_sem=br_sem.at[c, slot],
            device_id={"mode": to},
            device_id_type=MESH,
        )

    def quarters(value):
        return value.reshape(per, 4, modes // 4, LANES)

    def cycle_part(c):
        in_c = lo if c == 0 else jnp.logical_not(lo)
        o = orient_ref[me * CYCLES + c]
        place = stored_of_grid(o, lane) + lane // CELL * CELL
        cell_grid = jnp.where(place == stored, 1.0, 0.0).astype(BF)

        def conf_half(far):
            which = lax.rem(half_of + far, 2)
            rows = pl.ds(pl.multiple_of(which * half, half), half)
            for p in range(3):
                high, low = split(xp[c, pl.ds(which * side, side), p].reshape(half, LANES))
                at = slice(p * LANES, (p + 1) * LANES)
                ph[rows, at] = dot(high, cell_grid).astype(BF)
                pw[rows, at] = dot(low, cell_grid).astype(BF)

            def conf_block(i, carry):
                at = pl.ds(pl.multiple_of(i * half, half), half)
                total = dot3(fh_ref[at, rows], fl_ref[at, rows], ph[rows, :], pw[rows, :])
                vp[at, :] = vp[at, :] + total if far else total
                return carry

            lax.fori_loop(0, 4, conf_block, 0)

        def recv_half(far):
            def step(k, carry):
                frm = target(2 * k + far)
                send_p(c, 2 * k + far, frm, frm).wait_recv()
                return carry

            lax.fori_loop(1 - far, side, step, 0)

        own_p[c].wait()
        recv_half(0)
        conf_half(0)
        recv_half(1)
        conf_half(1)

        def deriv_block(i, carry):
            at = pl.ds(pl.multiple_of(i * half, half), half)
            for p in range(3):
                high, low = split(field(vp, p, at))
                dp[at, 2 * p * LANES : (2 * p + 2) * LANES] = dot3(high, low, both_h[...], both_l[...])
            return carry

        lax.fori_loop(0, 2, deriv_block, 0)

        def local_block(i, carry):
            at = pl.ds(pl.multiple_of(i * ROWS, ROWS), ROWS)
            dth_at = pl.ds(pl.multiple_of(PLANES + i * ROWS, ROWS), ROWS)
            u_r, u_t, u_z = [field(vv, f, at) for f in range(3)]
            spin = u_t * inv_r
            ur2, spin2, uz2 = [jnp.where(in_c, v, swap(v)) for v in (u_r, spin, u_z)]
            psi, advect = [], []
            for p in range(3):
                value = field(vp, p, at)
                other = swap(value)
                for h in range(2):
                    psi.append(jnp.where(in_c, value if h == c else other, 0.0))
                advect.append(
                    ur2 * field(dp, 2 * p, at) + spin2 * field(vp, p, dth_at) + uz2 * field(dp, 2 * p + 1, at)
                )
            conform, inverse = exponentials(psi)
            g = [field(proj, j, at) for j in range(9)]
            wa, wb, wc = 0.5 * (g[1] - g[3]), 0.5 * (g[2] - g[6]), 0.5 * (g[5] - g[7])
            wa2 = wa + spin
            r0 = [wa2 * psi[1] + wb * psi[2], wa2 * psi[3] + wb * psi[4], wa2 * psi[4] + wb * psi[5]]
            r1 = [wc * psi[2] - wa2 * psi[0], wc * psi[4] - wa2 * psi[1], wc * psi[5] - wa2 * psi[2]]
            r2 = [-(wb * psi[j] + wc * psi[k]) for j, k in ((0, 1), (1, 3), (2, 4))]
            rate = [
                2.0 * (r0[0] + g[0]),
                r0[1] + r1[0] + (g[1] + g[3]),
                r0[2] + r2[0] + (g[2] + g[6]),
                2.0 * (r1[1] + g[4]),
                r1[2] + r2[1] + (g[5] + g[7]),
                2.0 * (r2[2] + g[8]),
            ]
            for m in range(6):
                unit = 1.0 if m in diag else 0.0
                rate[m] = rate[m] - (1.0 / RELAX_TIME) * (
                    unit - inverse[m] + MOBILITY * (conform[m] - 2.0 * unit + inverse[m])
                )
            stress = [conform[m] - 1.0 if m in diag else conform[m] for m in range(6)]
            for f, (m, n) in enumerate(((0, 2), (1, 4), (2, 5))):
                high, low = split(pair_up(c, stress[m], stress[n]))
                sth[at, f * LANES : (f + 1) * LANES] = high
                stl[at, f * LANES : (f + 1) * LANES] = low
            hoop = [stress[m] * inv_r for m in (1, 3, 4)]
            base = [
                field(conv, 0, at) + (stress[0] - stress[3]) * inv_r,
                field(conv, 1, at) + 2.0 * hoop[0],
                field(conv, 2, at) + stress[2] * inv_r,
            ]
            mom[at, :LANES] = pair_up(c, base[0], base[1])
            mom[at, LANES:] = pair_up(c, base[2], rate[5]) - jnp.where(lo, 0.0, advect[2])
            put_rate(at, 2, pair_up(c, rate[0], rate[1]) - advect[0])
            put_rate(at, 3, pair_up(c, rate[2], rate[3]) - advect[1])
            first = rate[4] if c == 0 else swap(rate[4])
            put_rate(at, 4, jnp.where(lo, first - advect[2], 0.0))
            put_rate(at, 5, pair_up(c, hoop[0], hoop[1]))
            last = hoop[2] if c == 0 else swap(hoop[2])
            put_rate(at, 6, jnp.where(lo, last, 0.0))
            return carry

        lax.fori_loop(0, PLANES // ROWS, local_block, 0)
        if c == 0:
            loads[3].wait()

        def div_block(i, carry):
            at = pl.ds(pl.multiple_of(i * half, half), half)
            for f, cols in enumerate((slice(0, wide), slice(wide, 3 * LANES))):
                depth = cols.stop - cols.start
                total = dot3(
                    sth[at, cols], stl[at, cols], div_ref[:depth, :LANES], div_ref[:depth, LANES:]
                )
                put_rate(at, f, field(mom, f, at) + total)
            return carry

        lax.fori_loop(0, 2, div_block, 0)
        if c == 0:
            for load in loads[4:]:
                load.wait()

        def back_block(step, carry):
            pair = lax.rem(quarter // 2 + 1 + step // 2, 2)
            i = pair * 2 + lax.rem(quarter + step + step // 2, 2)
            at = pl.ds(pl.multiple_of(i * share, share), share)
            dst = pl.ds(i * per, per)
            cols, hoops = slice(0, wide), slice(5 * LANES, 7 * LANES)
            total = dot3(bh_ref[at, :PLANES], bl_ref[at, :PLANES], rh[:, cols], rl[:, cols])
            total += dot3(bh_ref[at, PLANES:], bl_ref[at, PLANES:], rh[:, hoops], rl[:, hoops])
            coefs = [total[:, :LANES], total[:, LANES:]]
            cols = slice(wide, 5 * LANES)
            total = dot3(bh_ref[at, :PLANES], bl_ref[at, :PLANES], rh[:, cols], rl[:, cols])
            coefs += [total[:, j * LANES : (j + 1) * LANES] for j in range(3)]
            if c == 0:
                blocks = [None] * 4
                for f in range(9):
                    b, inside, wall, width = first_cycle(f)
                    moved = rolled(coefs[f // 2], inside - wall - f % 2 * CELL)
                    blocks[b] = moved if inside == 0 else jnp.where(lane < inside, blocks[b], moved)
                    if inside + width > LANES:
                        blocks[b + 1] = moved
                for p in range(4):
                    if not fold:
                        back0[dst, p] = blocks[p].reshape(per, modes, LANES)
                    elif p < 3:
                        back0[dst, 4 * p : 4 * p + 4] = quarters(blocks[p])
                    else:
                        value = quarters(blocks[p])
                        for j in range(3):
                            extra = quarters(rolled(blocks[p], INSIDE - j * (LANES // 4)))[:, 3]
                            back0[dst, 12 + j] = jnp.where(lane < INSIDE, value[:, j], extra)
                for p in range(5):
                    kept[p, at, :] = coefs[p]
            else:
                for p in range(5):
                    face = rolled(kept[p, at, :], NODE_1D - CELL)
                    coefs[p] = jnp.where(lane % CELL < NODE_1D, 0.5 * (coefs[p] + face), coefs[p])
                for p in range(5):
                    if not fold:
                        back1[dst, p] = coefs[p].reshape(per, modes, LANES)
                    elif p < 4:
                        back1[dst, 4 * p : 4 * p + 4] = quarters(coefs[p])
                    else:
                        value, upper = quarters(coefs[p]), quarters(swap(coefs[p]))
                        for j in range(2):
                            back1[dst, 16 + j] = jnp.where(lo, value[:, j], upper[:, 2 + j])

            def give_start(j, inner):
                to = i * per + lax.rem(me + j, per)

                @pl.when(to != me)
                def _():
                    give(c, to, me).start()

                return inner

            lax.fori_loop(0, per, give_start, 0)
            return carry

        lax.fori_loop(0, 4, back_block, 0)

    cycle_part(0)
    cycle_part(1)
    own = [pltpu.make_async_copy(backs[c].at[me], outs[c].at[me], local_sem.at[c]) for c in range(2)]
    for copy in own:
        copy.start()
    load_v.wait()
    mode_ids = me * modes + lax.broadcasted_iota(jnp.int32, (modes, 1), 0)
    speed = jnp.where(mode_ids == 0, wall_ref[0], 0.0)

    def set_walls(layer, carry):
        inner, on_wall = wall_lanes(layer)
        at = columns(layer)
        for c in range(3):
            wall = jnp.where(inner, speed, 0.0) if c == 1 else 0.0
            vel_out[c, :, at] = jnp.where(on_wall, wall, vel_out[c, :, at])
        return carry

    lax.fori_loop(0, n_dev, set_walls, 0)
    every(lambda k, to: send_v(k, to, me).wait_send())
    for c in range(2):
        every(lambda k, to, c=c: send_p(c, k, to, me).wait_send())
    for copy in own:
        copy.wait()

    edge = jnp.logical_or(top, low_rows)
    weight = jnp.where(edge, 0.5 * STEP_DT, STEP_DT)
    joined = jnp.logical_and(lane >= CELL, lane < CELL + NODE_1D)

    def first_fields(at):
        if not fold:
            blocks = [out0_ref[at, p] for p in range(4)]
        else:
            blocks = [out0_ref[at, 4 * p : 4 * p + 4].reshape(modes, LANES) for p in range(3)]
            units = [out0_ref[at, 12 + j] for j in range(3)]
            piece = lane // (LANES // 4)
            outer = [rolled(units[j], (j + 1) * (LANES // 4)) for j in range(3)]
            units.append(jnp.where(piece == 0, outer[0], jnp.where(piece == 1, outer[1], outer[2])))
            blocks.append(jnp.concatenate(units, axis=0))
        fields = []
        for f in range(9):
            b, inside, wall, width = first_cycle(f)
            value = rolled(blocks[b], wall - inside)
            if inside + width > LANES:
                value = jnp.where(lane < wall + LANES - inside, value, rolled(blocks[b + 1], wall - inside))
            fields.append(value)
        return fields

    def second_fields(at):
        fields = []
        for f in range(9):
            p = f // 2
            if not fold:
                value = rolled(out1_ref[at, p], (f + 1) % 2 * CELL)
            elif p < 4:
                value = out1_ref[at, 4 * p : 4 * p + 4].reshape(modes, LANES)
                value = rolled(value, (f + 1) % 2 * CELL)
            else:
                value = out1_ref[at, 16:18].reshape(modes // 2, LANES)
                value = jnp.concatenate([rolled(value, CELL), value], axis=0)
            fields.append(value)
        return fields

    many = modes % 8 == 0

    def add_cycle(c):
        here = lane >= CELL if c else lane < KEPT

        def add_layer(order, carry):
            far = order // side
            m = lax.rem(order, side)
            local = lax.rem(me, side)
            near_by = lax.rem(local // per + m // per, 2) * per + lax.rem(local + n_dev * per - m, per)
            frm = lax.rem(half_of + far, 2) * side + near_by

            @pl.when(order > 0)
            def _():
                give(c, frm, frm).wait_recv()
                give(c, frm, me).wait_send()

            fields = [weight * v for v in (second_fields if c else first_fields)(frm)]
            step = NODE_1D - 1
            cats = [jnp.concatenate(split(v), axis=1) for v in ([jnp.concatenate(fields, axis=0)] if many else fields)]
            layers = [lax.rem(frm + ahead, n_dev) for ahead in (0, 1, n_dev - 1)]
            hots = []
            for layer, shift, only in zip(layers, (0, -step, step), (None, top, low_rows)):
                valid = [v if only is None else jnp.logical_and(v, only) for v in (here, joined)]
                place = jnp.where(valid[0], stored_index(orient_ref, layer, lane + shift), -1)
                hit = place == stored
                if c:
                    twin = jnp.where(valid[1], stored_index(orient_ref, layer, lane + shift - NODE_1D), -1)
                    hit = jnp.logical_or(hit, twin == stored)
                hot = jnp.where(hit, 1.0, 0.0).astype(BF)
                hots.append(jnp.concatenate([hot, hot], axis=1))
            hots = jnp.concatenate(hots, axis=0)
            sums = [
                lax.dot_general(v, hots, (((1,), (1,)), ((), ())), preferred_element_type=F32) for v in cats
            ]
            for j, layer in enumerate(layers):
                _, on_wall = wall_lanes(layer)
                at = columns(layer)
                cols = slice(j * LANES, (j + 1) * LANES)
                for f in range(9):
                    total = sums[0][f * modes : (f + 1) * modes, cols] if many else sums[f][:, cols]
                    to = CHANNEL_OF[f]
                    if to < 3:
                        vel_out[to, :, at] += jnp.where(on_wall, 0.0, total)
                    else:
                        logc_out[to - 3, :, at] += total
            return carry

        lax.fori_loop(0, n_dev, add_layer, 0)

    add_cycle(0)
    add_cycle(1)


def store_kernel(vel_ref, logc_ref, vel_out, logc_out, sem):
    copies = [pltpu.make_async_copy(vel_ref.at[c], vel_out.at[c], sem.at[c]) for c in range(3)]
    copies += [pltpu.make_async_copy(logc_ref.at[c], logc_out.at[c], sem.at[3 + c]) for c in range(6)]
    for copy in copies:
        copy.start()
    for copy in copies:
        copy.wait()


def body(velocity, log_conf, orientation, wall_speed):
    n_dev = lax.axis_size("mode")
    modes = velocity.shape[1]
    fold = modes % 32 == 0
    head = (15, modes // 4, LANES) if fold else (4, modes, LANES)
    tail = (18, modes // 4, LANES) if fold else (5, modes, LANES)
    consts = [jnp.asarray(t) for t in tables()]
    hbm = pl.BlockSpec(memory_space=pltpu.HBM)
    vmem = pl.BlockSpec(memory_space=pltpu.VMEM)
    dma = pltpu.SemaphoreType.DMA
    face_rows = PLANES + PLANES * CYCLES * NODE_1D // LANES
    held = pl.pallas_call(
        functools.partial(main_kernel, n_dev, modes, fold),
        out_shape=(
            jax.ShapeDtypeStruct(velocity.shape, F32),
            jax.ShapeDtypeStruct(log_conf.shape, F32),
        ),
        in_specs=[hbm] * 3 + [pl.BlockSpec(memory_space=pltpu.SMEM)] + [hbm] * len(consts),
        out_specs=(vmem, vmem),
        scratch_shapes=[pltpu.VMEM(t.shape, t.dtype) for t in consts]
        + [
            pltpu.SMEM(orientation.shape, jnp.int32),
            pltpu.VMEM((n_dev, *head), F32),
            pltpu.VMEM((n_dev, *tail), F32),
            pltpu.VMEM((2, n_dev, 3, modes, LANES), F32),
            pltpu.VMEM((n_dev, 3, modes, LANES), F32),
            pltpu.VMEM((2, n_dev, 3, modes, LANES), F32),
            pltpu.VMEM((PLANES, 3 * LANES), BF),
            pltpu.VMEM((PLANES, 3 * LANES), BF),
            pltpu.VMEM((PLANES, 3 * LANES), BF),
            pltpu.VMEM((PLANES, 3 * LANES), BF),
            pltpu.VMEM((2 * PLANES, 3 * LANES), F32),
            pltpu.VMEM((2 * PLANES, 3 * LANES), F32),
            pltpu.VMEM((PLANES, 6 * LANES), F32),
            pltpu.VMEM((PLANES, 9 * LANES), F32),
            pltpu.VMEM((2, face_rows, LANES), F32),
            pltpu.VMEM((2, face_rows, LANES), F32),
            pltpu.VMEM((PLANES, 3 * LANES), F32),
            pltpu.VMEM((PLANES, 2 * LANES), F32),
            pltpu.VMEM((PLANES, 3 * LANES), BF),
            pltpu.VMEM((PLANES, 3 * LANES), BF),
            pltpu.VMEM((PLANES, 7 * LANES), BF),
            pltpu.VMEM((PLANES, 7 * LANES), BF),
            pltpu.VMEM((5, PLANES, LANES), F32),
            pltpu.VMEM((n_dev, *head), F32),
            pltpu.VMEM((n_dev, *tail), F32),
            dma((6,)),
            dma((len(consts),)),
            dma((n_dev,)),
            dma((n_dev,)),
            dma((2, n_dev)),
            dma((2, n_dev)),
            dma((2,)),
            dma((2,)),
            dma((2, n_dev)),
            dma((2, n_dev)),
        ],
        compiler_params=pltpu.CompilerParams(
            collective_id=0, has_side_effects=True, vmem_limit_bytes=36 * 2**20
        ),
        name="fields",
    )(
        *[pltpu.with_memory_space_constraint(v, pltpu.HBM) for v in (velocity, log_conf, orientation)],
        wall_speed,
        *[pltpu.with_memory_space_constraint(v, pltpu.HBM) for v in consts],
    )

    free = pl.BlockSpec(memory_space=pl.ANY)
    return pl.pallas_call(
        store_kernel,
        out_shape=(
            jax.ShapeDtypeStruct(velocity.shape, F32),
            jax.ShapeDtypeStruct(log_conf.shape, F32),
        ),
        in_specs=[vmem, vmem],
        out_specs=(free, free),
        scratch_shapes=[dma((9,))],
        compiler_params=pltpu.CompilerParams(vmem_limit_bytes=8 * 2**20),
        name="store",
    )(*held)


def solution(mesh):
    in_specs = (P("ens", "mode", None), P("ens", "mode", None), P(), P("ens"))
    out_specs = (P("ens", "mode", None), P("ens", "mode", None))
    return jax.shard_map(body, mesh=mesh, in_specs=in_specs, out_specs=out_specs, check_vma=False)
```

```python
import functools

import jax
import jax.numpy as jnp
import ml_dtypes
import numpy as np
from jax import lax
from jax.experimental import pallas as pl
from jax.experimental.pallas import tpu as pltpu
from jax.sharding import PartitionSpec as P

NODE_1D = 8
CYCLES = 2
PLANES = 512
CELL = NODE_1D * NODE_1D
LANES = CYCLES * CELL
KEPT = CELL - NODE_1D
INSIDE = LANES - LANES // 4
CHANNEL_OF = (0, 1, 2, 8, 3, 4, 5, 6, 7)
STEP_DT = 0.002
RELAX_TIME = 0.02
MOBILITY = 0.3
LAYER_HEIGHT = 0.25
R_INNER = 1.0
ROWS = 16
BF = jnp.bfloat16
F32 = jnp.float32
MESH = pl.DeviceIdType.MESH


def cheb_table(points):
    nodes_xi = -np.cos(np.pi * np.arange(points) / (points - 1))
    weights = np.ones(points)
    weights[0] = 2.0
    weights[-1] = 2.0
    weights = weights * (-1.0) ** np.arange(points)
    identity = np.eye(points)
    spacing = nodes_xi[:, None] - nodes_xi[None, :] + identity
    matrix = weights[:, None] / weights[None, :] / spacing
    matrix = matrix * (1.0 - identity)
    matrix = matrix - identity * matrix.sum(axis=1)[:, None]
    return (nodes_xi, matrix)


def halves(table):
    high = np.asarray(table, np.float32).astype(ml_dtypes.bfloat16)
    low = (np.asarray(table, np.float64) - high.astype(np.float64)).astype(ml_dtypes.bfloat16)
    return high, low


def tables():
    n = np.arange(PLANES)
    k = np.arange(PLANES // 2)
    angle = (n[:, None] * k[None, :] % PLANES) * (2.0 * np.pi / PLANES)
    cosine = np.cos(angle) * np.sqrt(2.0 / PLANES)
    sine = np.sin(angle) * np.sqrt(2.0 / PLANES)
    cosine[:, 0] = PLANES**-0.5
    sine[:, 0] = (-1.0) ** n * PLANES**-0.5
    basis = np.stack([cosine, sine], axis=2).reshape(PLANES, PLANES)
    dbasis = np.stack([-k * sine, k * cosine], axis=2).reshape(PLANES, PLANES)
    forward = np.concatenate([basis, dbasis], axis=0)
    backward = np.concatenate([basis.T, -dbasis.T], axis=1)

    xi, matrix = cheb_table(NODE_1D)
    eye, eyes = np.eye(NODE_1D), np.eye(CYCLES)
    cell_r = np.kron(matrix.T * (2.0 * CYCLES), eye)
    cell_z = np.kron(eye, matrix.T * (2.0 / LAYER_HEIGHT))
    d_r, d_z = np.kron(eyes, cell_r), np.kron(eyes, cell_z)
    mean = np.eye(CYCLES * NODE_1D)
    for c in range(1, CYCLES):
        i = c * NODE_1D
        mean[i - 1 : i + 1, i - 1 : i + 1] = 0.5
    mean = np.kron(mean, eye)
    weight = np.ones(NODE_1D)
    weight[0] = weight[-1] = 0.5
    weight = np.tile(weight, CYCLES * NODE_1D)
    mean_w = mean * weight[None, :]
    both = np.concatenate([d_r, d_z], axis=1)
    grad = np.concatenate([d_r @ mean_w, d_z @ mean_w], axis=1)
    div = np.kron(np.eye(2), np.concatenate([cell_r, cell_z], axis=0))
    return (
        *halves(forward),
        *halves(backward),
        np.concatenate([*halves(both), *halves(grad), mean_w.astype(ml_dtypes.bfloat16)], axis=1),
        np.concatenate(halves(div), axis=1),
    )


def inverse_radius(lane):
    xi, _ = cheb_table(NODE_1D)
    radius = R_INNER + (np.arange(CYCLES)[:, None] + (xi[None, :] + 1.0) / 2.0) / CYCLES
    total = jnp.zeros(lane.shape, F32)
    for i, r in enumerate(radius.reshape(-1)):
        total = jnp.where(lane // NODE_1D == i, float(1.0 / r), total)
    return total


def split(x):
    high = x.astype(BF)
    return high, (x - high.astype(F32)).astype(BF)


def dot(a, b):
    return jnp.dot(a, b, preferred_element_type=F32)


def dot3(ah, al, bh, bl):
    return dot(ah, bh) + (dot(ah, bl) + dot(al, bh))


def stored_of_grid(o, grid):
    side = NODE_1D
    y = grid % side
    x = grid // side % side
    swapped = o // 4 % 2 == 1
    a = jnp.where(swapped, x, y)
    b = jnp.where(swapped, y, x)
    a = jnp.where(o % 2 == 1, side - 1 - a, a)
    b = jnp.where(o // 2 % 2 == 1, side - 1 - b, b)
    return a * side + b


def stored_index(orient_ref, layer, grid):
    cycle = grid // CELL
    place = jnp.zeros_like(grid)
    for c in range(CYCLES):
        o = orient_ref[layer * CYCLES + c]
        place = jnp.where(cycle == c, c * CELL + stored_of_grid(o, grid), place)
    return place


def square(m):
    a, b, c, d, e, f = m
    bb, cc, ee = b * b, c * c, e * e
    return (
        a * a + bb + cc,
        b * (a + d) + c * e,
        c * (a + f) + b * e,
        bb + d * d + ee,
        e * (d + f) + b * c,
        cc + ee + f * f,
    )


def product(m, n):
    a, b, c, d, e, f = m
    p, q, r, s, t, u = n
    return (
        a * p + b * q + c * r,
        a * q + b * s + c * t,
        a * r + b * t + c * u,
        b * q + d * s + e * t,
        b * r + d * t + e * u,
        c * r + e * t + f * u,
    )


def exponentials(psi):
    x = tuple(v * 0.125 for v in psi)
    x2 = square(x)
    x3 = product(x, x2)
    x4 = square(x2)
    even = [x2[i] * 0.5 + x4[i] * (1.0 / 24.0) for i in range(6)]
    for i in (0, 3, 5):
        even[i] = even[i] + 1.0
    odd = [x[i] + x3[i] * (1.0 / 6.0) for i in range(6)]
    plus = tuple(even[i] + odd[i] for i in range(6))
    minus = tuple(even[i] - odd[i] for i in range(6))
    for _ in range(3):
        plus, minus = square(plus), square(minus)
    return plus, minus


def first_cycle(f):
    wall = NODE_1D if f < 3 else 0
    start = f * KEPT - min(f, 3) * NODE_1D
    return start // LANES, start % LANES, wall, KEPT - wall


def field(ref, f, rows=slice(None)):
    return ref[rows, f * LANES : (f + 1) * LANES]


def main_kernel(
    n_dev, modes, fold,
    vel_ref, logc_ref, orient_in, wall_ref, fh_in, fl_in, bh_in, bl_in, node_in, div_in,
    vel_out, logc_out,
    fh_ref, fl_ref, bh_ref, bl_ref, node_ref, div_ref,
    orient_ref, out0_ref, out1_ref, packed, xv, xp, xh, xl, ph, pw, vv, vp, dp, proj, face_out, face_in, conv, mom, sth, stl, rh, rl,
    kept, back0, back1,
    local_sem, const_sem, vs_sem, vr_sem, ps_sem, pr_sem, fs_sem, fr_sem, bs_sem, br_sem,
):
    me = lax.axis_index("mode")
    up = lax.rem(me + 1, n_dev)
    down = lax.rem(me + n_dev - 1, n_dev)

    barrier = pltpu.get_barrier_semaphore()

    def greet(k, carry):
        pl.semaphore_signal(
            barrier, inc=1, device_id={"mode": lax.rem(me + k, n_dev)}, device_id_type=MESH
        )
        return carry

    lax.fori_loop(1, n_dev, greet, 0)
    early = [
        pltpu.make_async_copy(a, b, local_sem.at[i])
        for i, (a, b) in ((0, (logc_ref, logc_out)), (4, (orient_in, orient_ref)))
    ]
    for copy in early:
        copy.start()
    pl.semaphore_wait(barrier, n_dev - 1)

    side = n_dev // 2
    half_of = me // side

    def target(k):
        j = k // 2
        return lax.rem(half_of + lax.rem(k, 2), 2) * side + lax.rem(me + j, side)

    def columns(d):
        return pl.ds(pl.multiple_of(d * LANES, LANES), LANES)

    def every(do):
        def step(k, carry):
            do(k, target(k))
            return carry

        lax.fori_loop(1, n_dev, step, 0)

    def send_v(k, to, slot):
        return pltpu.make_async_remote_copy(
            src_ref=vel_ref.at[:, :, columns(to)],
            dst_ref=xv.at[slot],
            send_sem=vs_sem.at[k],
            recv_sem=vr_sem.at[slot],
            device_id={"mode": to},
            device_id_type=MESH,
        )

    def send_p(c, k, to, slot):
        return pltpu.make_async_remote_copy(
            src_ref=packed.at[c, to],
            dst_ref=xp.at[c, slot],
            send_sem=ps_sem.at[c, k],
            recv_sem=pr_sem.at[c, slot],
            device_id={"mode": to},
            device_id_type=MESH,
        )

    every(lambda k, to: send_v(k, to, me).start())
    own_v = pltpu.make_async_copy(vel_ref.at[:, :, columns(me)], xv.at[me], local_sem.at[1])
    own_v.start()
    load_v = pltpu.make_async_copy(vel_ref, vel_out, local_sem.at[5])
    load_v.start()
    loads = [
        pltpu.make_async_copy(a, b, const_sem.at[i])
        for i, (a, b) in enumerate(
            (
                (node_in, node_ref), (fh_in, fh_ref), (fl_in, fl_ref),
                (div_in, div_ref), (bh_in, bh_ref), (bl_in, bl_ref),
            )
        )
    ]
    for load in loads:
        load.start()

    lane = lax.broadcasted_iota(jnp.int32, (1, LANES), 1)
    lo = lane < CELL

    def swap(value):
        return pltpu.roll(value, CELL, 1)

    def pair_up(c, a, b):
        return jnp.where(lo, a, swap(b)) if c == 0 else jnp.where(lo, swap(a), b)

    for copy in early:
        copy.wait()
    own_p = [
        pltpu.make_async_copy(packed.at[c, me], xp.at[c, me], local_sem.at[2 + c]) for c in range(2)
    ]
    for c in range(2):

        def pack_psi(to, carry, c=c):
            at = columns(to)
            for p in range(3):
                packed[c, to, p] = pair_up(c, logc_out[2 * p, :, at], logc_out[2 * p + 1, :, at])
            return carry

        lax.fori_loop(0, n_dev, pack_psi, 0)
        if c == 0:
            every(lambda k, to: send_p(0, k, to, me).start())
        own_p[c].start()

    stored = lax.broadcasted_iota(jnp.int32, (LANES, LANES), 0)
    to_grid = jnp.where(stored_index(orient_ref, me, lane) == stored, 1.0, 0.0).astype(BF)

    half = PLANES // 2
    inv_r = inverse_radius(lane)
    for load in loads[:3]:
        load.wait()
    wide = 2 * LANES
    both_h, both_l, grad_h, grad_l = [node_ref.at[:, i * wide : (i + 1) * wide] for i in range(4)]
    mean_ref = node_ref.at[:, 4 * wide : 4 * wide + LANES]

    def vel_half(far):
        def step(k, carry):
            frm = target(2 * k + far)
            send_v(2 * k + far, frm, frm).wait_recv()
            return carry

        lax.fori_loop(1 - far, side, step, 0)
        which = lax.rem(half_of + far, 2)
        rows = pl.ds(pl.multiple_of(which * half, half), half)
        for f in range(3):
            high, low = split(xv[pl.ds(which * side, side), f].reshape(half, LANES))
            at = slice(f * LANES, (f + 1) * LANES)
            xh[rows, at] = dot(high, to_grid).astype(BF)
            xl[rows, at] = dot(low, to_grid).astype(BF)

        def velocity_block(i, carry):
            at = pl.ds(pl.multiple_of(i * half, half), half)
            total = dot3(fh_ref[at, rows], fl_ref[at, rows], xh[rows, :], xl[rows, :])
            vv[at, :] = vv[at, :] + total if far else total
            return carry

        lax.fori_loop(0, 4, velocity_block, 0)

    own_v.wait()
    vel_half(0)
    vel_half(1)

    def grad_block(i, carry):
        block = half // 2
        at = pl.ds(pl.multiple_of(i * block, block), block)
        dth_at = pl.ds(pl.multiple_of(PLANES + i * block, block), block)
        u = [field(vv, f, at) for f in range(3)]
        dth = [field(vv, f, dth_at) for f in range(3)]
        hoop = [(dth[0] - u[1]) * inv_r, (dth[1] + u[0]) * inv_r, dth[2] * inv_r]
        for f in range(3):
            uh, ul = split(u[f])
            both = dot3(uh, ul, grad_h[...], grad_l[...])
            hh, hl = split(hoop[f])
            g = (both[:, :LANES], dot(hh, mean_ref[...]) + dot(hl, mean_ref[...]), both[:, LANES:])
            for j in range(3):
                c = 3 * f + j
                proj[at, c * LANES : (c + 1) * LANES] = g[j]
        return carry

    lax.fori_loop(0, 4, grad_block, 0)

    groups = NODE_1D
    short = PLANES // groups

    def rolled(value, shift):
        return pltpu.roll(value, shift % LANES, 1) if shift % LANES else value

    def face_copy(slot, to):
        return pltpu.make_async_remote_copy(
            src_ref=face_out.at[slot],
            dst_ref=face_in.at[slot],
            send_sem=fs_sem.at[slot],
            recv_sem=fr_sem.at[slot],
            device_id={"mode": to},
            device_id_type=MESH,
        )

    faces = (face_copy(0, up), face_copy(1, down))
    for slot, start in ((0, NODE_1D - 1), (1, 0)):

        def pack(i, carry, slot=slot, start=start):
            at = pl.ds(pl.multiple_of(i * 64, 64), 64)
            total = jnp.zeros((64, LANES), F32)
            for c in range(groups):
                total = jnp.where(lane % groups == c, rolled(field(proj, c, at), c - start), total)
            face_out[slot, at, :] = total
            return carry

        lax.fori_loop(0, PLANES // 64, pack, 0)
        total = jnp.zeros((short, LANES), F32)
        for b in range(groups):
            moved = field(proj, 8, slice(b * short, (b + 1) * short))
            total = jnp.where(lane % groups == b, rolled(moved, b - start), total)
        face_out[slot, PLANES:, :] = total
        faces[slot].start()

    for face in faces:
        face.wait()
    def far_or_near(far):
        def step(k, carry):
            send_p(1, 2 * k + far, target(2 * k + far), me).start()
            return carry

        lax.fori_loop(1 - far, side, step, 0)

    far_or_near(1)

    def wall_lanes(layer):
        lead, trail = lane // NODE_1D % NODE_1D, lane % NODE_1D
        code = jnp.where(lo, orient_ref[layer * CYCLES], orient_ref[layer * CYCLES + 1])
        flipped_a = jnp.where(code % 2 == 1, NODE_1D - 1 - lead, lead)
        flipped_b = jnp.where(code // 2 % 2 == 1, NODE_1D - 1 - trail, trail)
        x = jnp.where(code // 4 % 2 == 1, flipped_a, flipped_b)
        inner = jnp.logical_and(lo, x == 0)
        outer = jnp.logical_and(jnp.logical_not(lo), x == NODE_1D - 1)
        return inner, jnp.logical_or(inner, outer)

    top = lane % NODE_1D == NODE_1D - 1
    low_rows = lane % NODE_1D == 0

    def unpacked(from_down, from_up, c):
        below = rolled(from_down, -c)
        above = rolled(from_up, NODE_1D - 1 - c)
        return jnp.where(top, above, jnp.where(low_rows, below, 0.0))

    for b in range(groups):

        def face_block(i, carry, b=b):
            start = pl.multiple_of(b * short + i * ROWS, ROWS)
            at = pl.ds(start, ROWS)
            nine = pl.ds(pl.multiple_of(PLANES + i * ROWS, ROWS), ROWS)
            down_face, up_face = face_in[0, at, :], face_in[1, at, :]
            g = [field(proj, c, at) + unpacked(down_face, up_face, c) for c in range(8)]
            g.append(field(proj, 8, at) + unpacked(face_in[0, nine, :], face_in[1, nine, :], b))
            for c in range(9):
                proj[at, c * LANES : (c + 1) * LANES] = g[c]
            u = [field(vv, f, at) for f in range(3)]
            for f in range(3):
                total = g[3 * f] * u[0] + g[3 * f + 1] * u[1] + g[3 * f + 2] * u[2]
                conv[at, f * LANES : (f + 1) * LANES] = -total
            return carry

        lax.fori_loop(0, short // ROWS, face_block, 0)

    def put_rate(at, f, value):
        high, low = split(value)
        rh[at, f * LANES : (f + 1) * LANES] = high
        rl[at, f * LANES : (f + 1) * LANES] = low

    share = PLANES // 4
    per = share // modes
    quarter = me // per
    backs, outs = (back0, back1), (out0_ref, out1_ref)
    diag = (0, 3, 5)

    def give(c, to, slot):
        return pltpu.make_async_remote_copy(
            src_ref=backs[c].at[to],
            dst_ref=outs[c].at[slot],
            send_sem=bs_sem.at[c, to],
            recv_sem=br_sem.at[c, slot],
            device_id={"mode": to},
            device_id_type=MESH,
        )

    def quarters(value):
        return value.reshape(per, 4, modes // 4, LANES)

    def cycle_part(c):
        in_c = lo if c == 0 else jnp.logical_not(lo)
        o = orient_ref[me * CYCLES + c]
        place = stored_of_grid(o, lane) + lane // CELL * CELL
        cell_grid = jnp.where(place == stored, 1.0, 0.0).astype(BF)

        def conf_half(far):
            which = lax.rem(half_of + far, 2)
            rows = pl.ds(pl.multiple_of(which * half, half), half)
            for p in range(3):
                high, low = split(xp[c, pl.ds(which * side, side), p].reshape(half, LANES))
                at = slice(p * LANES, (p + 1) * LANES)
                ph[rows, at] = dot(high, cell_grid).astype(BF)
                pw[rows, at] = dot(low, cell_grid).astype(BF)

            def conf_block(i, carry):
                at = pl.ds(pl.multiple_of(i * half, half), half)
                total = dot3(fh_ref[at, rows], fl_ref[at, rows], ph[rows, :], pw[rows, :])
                vp[at, :] = vp[at, :] + total if far else total
                return carry

            lax.fori_loop(0, 4, conf_block, 0)

        def recv_half(far):
            def step(k, carry):
                frm = target(2 * k + far)
                send_p(c, 2 * k + far, frm, frm).wait_recv()
                return carry

            lax.fori_loop(1 - far, side, step, 0)

        own_p[c].wait()
        recv_half(0)
        conf_half(0)
        if c == 0:
            far_or_near(0)
        recv_half(1)
        conf_half(1)

        def deriv_block(i, carry):
            at = pl.ds(pl.multiple_of(i * half, half), half)
            for p in range(3):
                high, low = split(field(vp, p, at))
                dp[at, 2 * p * LANES : (2 * p + 2) * LANES] = dot3(high, low, both_h[...], both_l[...])
            return carry

        lax.fori_loop(0, 2, deriv_block, 0)

        def local_block(i, carry):
            at = pl.ds(pl.multiple_of(i * ROWS, ROWS), ROWS)
            dth_at = pl.ds(pl.multiple_of(PLANES + i * ROWS, ROWS), ROWS)
            u_r, u_t, u_z = [field(vv, f, at) for f in range(3)]
            spin = u_t * inv_r
            ur2, spin2, uz2 = [jnp.where(in_c, v, swap(v)) for v in (u_r, spin, u_z)]
            psi, advect = [], []
            for p in range(3):
                value = field(vp, p, at)
                other = swap(value)
                for h in range(2):
                    psi.append(jnp.where(in_c, value if h == c else other, 0.0))
                advect.append(
                    ur2 * field(dp, 2 * p, at) + spin2 * field(vp, p, dth_at) + uz2 * field(dp, 2 * p + 1, at)
                )
            conform, inverse = exponentials(psi)
            g = [field(proj, j, at) for j in range(9)]
            wa, wb, wc = 0.5 * (g[1] - g[3]), 0.5 * (g[2] - g[6]), 0.5 * (g[5] - g[7])
            wa2 = wa + spin
            r0 = [wa2 * psi[1] + wb * psi[2], wa2 * psi[3] + wb * psi[4], wa2 * psi[4] + wb * psi[5]]
            r1 = [wc * psi[2] - wa2 * psi[0], wc * psi[4] - wa2 * psi[1], wc * psi[5] - wa2 * psi[2]]
            r2 = [-(wb * psi[j] + wc * psi[k]) for j, k in ((0, 1), (1, 3), (2, 4))]
            rate = [
                2.0 * (r0[0] + g[0]),
                r0[1] + r1[0] + (g[1] + g[3]),
                r0[2] + r2[0] + (g[2] + g[6]),
                2.0 * (r1[1] + g[4]),
                r1[2] + r2[1] + (g[5] + g[7]),
                2.0 * (r2[2] + g[8]),
            ]
            for m in range(6):
                unit = 1.0 if m in diag else 0.0
                rate[m] = rate[m] - (1.0 / RELAX_TIME) * (
                    unit - inverse[m] + MOBILITY * (conform[m] - 2.0 * unit + inverse[m])
                )
            stress = [conform[m] - 1.0 if m in diag else conform[m] for m in range(6)]
            for f, (m, n) in enumerate(((0, 2), (1, 4), (2, 5))):
                high, low = split(pair_up(c, stress[m], stress[n]))
                sth[at, f * LANES : (f + 1) * LANES] = high
                stl[at, f * LANES : (f + 1) * LANES] = low
            hoop = [stress[m] * inv_r for m in (1, 3, 4)]
            base = [
                field(conv, 0, at) + (stress[0] - stress[3]) * inv_r,
                field(conv, 1, at) + 2.0 * hoop[0],
                field(conv, 2, at) + stress[2] * inv_r,
            ]
            mom[at, :LANES] = pair_up(c, base[0], base[1])
            mom[at, LANES:] = pair_up(c, base[2], rate[5]) - jnp.where(lo, 0.0, advect[2])
            put_rate(at, 2, pair_up(c, rate[0], rate[1]) - advect[0])
            put_rate(at, 3, pair_up(c, rate[2], rate[3]) - advect[1])
            first = rate[4] if c == 0 else swap(rate[4])
            put_rate(at, 4, jnp.where(lo, first - advect[2], 0.0))
            put_rate(at, 5, pair_up(c, hoop[0], hoop[1]))
            last = hoop[2] if c == 0 else swap(hoop[2])
            put_rate(at, 6, jnp.where(lo, last, 0.0))
            return carry

        lax.fori_loop(0, PLANES // ROWS, local_block, 0)
        if c == 0:
            loads[3].wait()

        def div_block(i, carry):
            at = pl.ds(pl.multiple_of(i * half, half), half)
            for f, cols in enumerate((slice(0, wide), slice(wide, 3 * LANES))):
                depth = cols.stop - cols.start
                total = dot3(
                    sth[at, cols], stl[at, cols], div_ref[:depth, :LANES], div_ref[:depth, LANES:]
                )
                put_rate(at, f, field(mom, f, at) + total)
            return carry

        lax.fori_loop(0, 2, div_block, 0)
        if c == 0:
            for load in loads[4:]:
                load.wait()

        def back_block(step, carry):
            pair = lax.rem(quarter // 2 + 1 + step // 2, 2)
            i = pair * 2 + lax.rem(quarter + step + step // 2, 2)
            at = pl.ds(pl.multiple_of(i * share, share), share)
            dst = pl.ds(i * per, per)
            cols, hoops = slice(0, wide), slice(5 * LANES, 7 * LANES)
            total = dot3(bh_ref[at, :PLANES], bl_ref[at, :PLANES], rh[:, cols], rl[:, cols])
            total += dot3(bh_ref[at, PLANES:], bl_ref[at, PLANES:], rh[:, hoops], rl[:, hoops])
            coefs = [total[:, :LANES], total[:, LANES:]]
            cols = slice(wide, 5 * LANES)
            total = dot3(bh_ref[at, :PLANES], bl_ref[at, :PLANES], rh[:, cols], rl[:, cols])
            coefs += [total[:, j * LANES : (j + 1) * LANES] for j in range(3)]
            if c == 0:
                blocks = [None] * 4
                for f in range(9):
                    b, inside, wall, width = first_cycle(f)
                    moved = rolled(coefs[f // 2], inside - wall - f % 2 * CELL)
                    blocks[b] = moved if inside == 0 else jnp.where(lane < inside, blocks[b], moved)
                    if inside + width > LANES:
                        blocks[b + 1] = moved
                for p in range(4):
                    if not fold:
                        back0[dst, p] = blocks[p].reshape(per, modes, LANES)
                    elif p < 3:
                        back0[dst, 4 * p : 4 * p + 4] = quarters(blocks[p])
                    else:
                        value = quarters(blocks[p])
                        for j in range(3):
                            extra = quarters(rolled(blocks[p], INSIDE - j * (LANES // 4)))[:, 3]
                            back0[dst, 12 + j] = jnp.where(lane < INSIDE, value[:, j], extra)
                for p in range(5):
                    kept[p, at, :] = coefs[p]
            else:
                for p in range(5):
                    face = rolled(kept[p, at, :], NODE_1D - CELL)
                    coefs[p] = jnp.where(lane % CELL < NODE_1D, 0.5 * (coefs[p] + face), coefs[p])
                for p in range(5):
                    if not fold:
                        back1[dst, p] = coefs[p].reshape(per, modes, LANES)
                    elif p < 4:
                        back1[dst, 4 * p : 4 * p + 4] = quarters(coefs[p])
                    else:
                        value, upper = quarters(coefs[p]), quarters(swap(coefs[p]))
                        for j in range(2):
                            back1[dst, 16 + j] = jnp.where(lo, value[:, j], upper[:, 2 + j])

            def give_start(j, inner):
                to = i * per + lax.rem(me + j, per)

                @pl.when(to != me)
                def _():
                    give(c, to, me).start()

                return inner

            lax.fori_loop(0, per, give_start, 0)
            return carry

        lax.fori_loop(0, 4, back_block, 0)

    cycle_part(0)
    cycle_part(1)
    own = [pltpu.make_async_copy(backs[c].at[me], outs[c].at[me], local_sem.at[c]) for c in range(2)]
    for copy in own:
        copy.start()
    load_v.wait()
    mode_ids = me * modes + lax.broadcasted_iota(jnp.int32, (modes, 1), 0)
    speed = jnp.where(mode_ids == 0, wall_ref[0], 0.0)

    def set_walls(layer, carry):
        inner, on_wall = wall_lanes(layer)
        at = columns(layer)
        for c in range(3):
            wall = jnp.where(inner, speed, 0.0) if c == 1 else 0.0
            vel_out[c, :, at] = jnp.where(on_wall, wall, vel_out[c, :, at])
        return carry

    lax.fori_loop(0, n_dev, set_walls, 0)
    every(lambda k, to: send_v(k, to, me).wait_send())
    for c in range(2):
        every(lambda k, to, c=c: send_p(c, k, to, me).wait_send())
    for copy in own:
        copy.wait()

    edge = jnp.logical_or(top, low_rows)
    weight = jnp.where(edge, 0.5 * STEP_DT, STEP_DT)
    joined = jnp.logical_and(lane >= CELL, lane < CELL + NODE_1D)

    def first_fields(at):
        if not fold:
            blocks = [out0_ref[at, p] for p in range(4)]
        else:
            blocks = [out0_ref[at, 4 * p : 4 * p + 4].reshape(modes, LANES) for p in range(3)]
            units = [out0_ref[at, 12 + j] for j in range(3)]
            piece = lane // (LANES // 4)
            outer = [rolled(units[j], (j + 1) * (LANES // 4)) for j in range(3)]
            units.append(jnp.where(piece == 0, outer[0], jnp.where(piece == 1, outer[1], outer[2])))
            blocks.append(jnp.concatenate(units, axis=0))
        fields = []
        for f in range(9):
            b, inside, wall, width = first_cycle(f)
            value = rolled(blocks[b], wall - inside)
            if inside + width > LANES:
                value = jnp.where(lane < wall + LANES - inside, value, rolled(blocks[b + 1], wall - inside))
            fields.append(value)
        return fields

    def second_fields(at):
        fields = []
        for f in range(9):
            p = f // 2
            if not fold:
                value = rolled(out1_ref[at, p], (f + 1) % 2 * CELL)
            elif p < 4:
                value = out1_ref[at, 4 * p : 4 * p + 4].reshape(modes, LANES)
                value = rolled(value, (f + 1) % 2 * CELL)
            else:
                value = out1_ref[at, 16:18].reshape(modes // 2, LANES)
                value = jnp.concatenate([rolled(value, CELL), value], axis=0)
            fields.append(value)
        return fields

    many = modes % 8 == 0

    def add_cycle(c):
        here = lane >= CELL if c else lane < KEPT

        def add_layer(order, carry):
            far = order // side
            m = lax.rem(order, side)
            local = lax.rem(me, side)
            near_by = lax.rem(local // per + m // per, 2) * per + lax.rem(local + n_dev * per - m, per)
            frm = lax.rem(half_of + far, 2) * side + near_by

            @pl.when(order > 0)
            def _():
                give(c, frm, frm).wait_recv()
                give(c, frm, me).wait_send()

            fields = [weight * v for v in (second_fields if c else first_fields)(frm)]
            step = NODE_1D - 1
            cats = [jnp.concatenate(split(v), axis=1) for v in ([jnp.concatenate(fields, axis=0)] if many else fields)]
            layers = [lax.rem(frm + ahead, n_dev) for ahead in (0, 1, n_dev - 1)]
            hots = []
            for layer, shift, only in zip(layers, (0, -step, step), (None, top, low_rows)):
                valid = [v if only is None else jnp.logical_and(v, only) for v in (here, joined)]
                place = jnp.where(valid[0], stored_index(orient_ref, layer, lane + shift), -1)
                hit = place == stored
                if c:
                    twin = jnp.where(valid[1], stored_index(orient_ref, layer, lane + shift - NODE_1D), -1)
                    hit = jnp.logical_or(hit, twin == stored)
                hot = jnp.where(hit, 1.0, 0.0).astype(BF)
                hots.append(jnp.concatenate([hot, hot], axis=1))
            hots = jnp.concatenate(hots, axis=0)
            sums = [
                lax.dot_general(v, hots, (((1,), (1,)), ((), ())), preferred_element_type=F32) for v in cats
            ]
            for j, layer in enumerate(layers):
                _, on_wall = wall_lanes(layer)
                at = columns(layer)
                cols = slice(j * LANES, (j + 1) * LANES)
                for f in range(9):
                    total = sums[0][f * modes : (f + 1) * modes, cols] if many else sums[f][:, cols]
                    to = CHANNEL_OF[f]
                    if to < 3:
                        vel_out[to, :, at] += jnp.where(on_wall, 0.0, total)
                    else:
                        logc_out[to - 3, :, at] += total
            return carry

        lax.fori_loop(0, n_dev, add_layer, 0)

    add_cycle(0)
    add_cycle(1)


def store_kernel(vel_ref, logc_ref, vel_out, logc_out, sem):
    copies = [pltpu.make_async_copy(vel_ref.at[c], vel_out.at[c], sem.at[c]) for c in range(3)]
    copies += [pltpu.make_async_copy(logc_ref.at[c], logc_out.at[c], sem.at[3 + c]) for c in range(6)]
    for copy in copies:
        copy.start()
    for copy in copies:
        copy.wait()


def body(velocity, log_conf, orientation, wall_speed):
    n_dev = lax.axis_size("mode")
    modes = velocity.shape[1]
    fold = modes % 32 == 0
    head = (15, modes // 4, LANES) if fold else (4, modes, LANES)
    tail = (18, modes // 4, LANES) if fold else (5, modes, LANES)
    consts = [jnp.asarray(t) for t in tables()]
    hbm = pl.BlockSpec(memory_space=pltpu.HBM)
    vmem = pl.BlockSpec(memory_space=pltpu.VMEM)
    dma = pltpu.SemaphoreType.DMA
    face_rows = PLANES + PLANES * CYCLES * NODE_1D // LANES
    held = pl.pallas_call(
        functools.partial(main_kernel, n_dev, modes, fold),
        out_shape=(
            jax.ShapeDtypeStruct(velocity.shape, F32),
            jax.ShapeDtypeStruct(log_conf.shape, F32),
        ),
        in_specs=[hbm] * 3 + [pl.BlockSpec(memory_space=pltpu.SMEM)] + [hbm] * len(consts),
        out_specs=(vmem, vmem),
        scratch_shapes=[pltpu.VMEM(t.shape, t.dtype) for t in consts]
        + [
            pltpu.SMEM(orientation.shape, jnp.int32),
            pltpu.VMEM((n_dev, *head), F32),
            pltpu.VMEM((n_dev, *tail), F32),
            pltpu.VMEM((2, n_dev, 3, modes, LANES), F32),
            pltpu.VMEM((n_dev, 3, modes, LANES), F32),
            pltpu.VMEM((2, n_dev, 3, modes, LANES), F32),
            pltpu.VMEM((PLANES, 3 * LANES), BF),
            pltpu.VMEM((PLANES, 3 * LANES), BF),
            pltpu.VMEM((PLANES, 3 * LANES), BF),
            pltpu.VMEM((PLANES, 3 * LANES), BF),
            pltpu.VMEM((2 * PLANES, 3 * LANES), F32),
            pltpu.VMEM((2 * PLANES, 3 * LANES), F32),
            pltpu.VMEM((PLANES, 6 * LANES), F32),
            pltpu.VMEM((PLANES, 9 * LANES), F32),
            pltpu.VMEM((2, face_rows, LANES), F32),
            pltpu.VMEM((2, face_rows, LANES), F32),
            pltpu.VMEM((PLANES, 3 * LANES), F32),
            pltpu.VMEM((PLANES, 2 * LANES), F32),
            pltpu.VMEM((PLANES, 3 * LANES), BF),
            pltpu.VMEM((PLANES, 3 * LANES), BF),
            pltpu.VMEM((PLANES, 7 * LANES), BF),
            pltpu.VMEM((PLANES, 7 * LANES), BF),
            pltpu.VMEM((5, PLANES, LANES), F32),
            pltpu.VMEM((n_dev, *head), F32),
            pltpu.VMEM((n_dev, *tail), F32),
            dma((6,)),
            dma((len(consts),)),
            dma((n_dev,)),
            dma((n_dev,)),
            dma((2, n_dev)),
            dma((2, n_dev)),
            dma((2,)),
            dma((2,)),
            dma((2, n_dev)),
            dma((2, n_dev)),
        ],
        compiler_params=pltpu.CompilerParams(
            collective_id=0, has_side_effects=True, vmem_limit_bytes=36 * 2**20
        ),
        name="fields",
    )(
        *[pltpu.with_memory_space_constraint(v, pltpu.HBM) for v in (velocity, log_conf, orientation)],
        wall_speed,
        *[pltpu.with_memory_space_constraint(v, pltpu.HBM) for v in consts],
    )

    free = pl.BlockSpec(memory_space=pl.ANY)
    return pl.pallas_call(
        store_kernel,
        out_shape=(
            jax.ShapeDtypeStruct(velocity.shape, F32),
            jax.ShapeDtypeStruct(log_conf.shape, F32),
        ),
        in_specs=[vmem, vmem],
        out_specs=(free, free),
        scratch_shapes=[dma((9,))],
        compiler_params=pltpu.CompilerParams(vmem_limit_bytes=8 * 2**20),
        name="store",
    )(*held)


def solution(mesh):
    in_specs = (P("ens", "mode", None), P("ens", "mode", None), P(), P("ens"))
    out_specs = (P("ens", "mode", None), P("ens", "mode", None))
    return jax.shard_map(body, mesh=mesh, in_specs=in_specs, out_specs=out_specs, check_vma=False)
```

```python
import functools

import jax
import jax.numpy as jnp
import ml_dtypes
import numpy as np
from jax import lax
from jax.experimental import pallas as pl
from jax.experimental.pallas import tpu as pltpu
from jax.sharding import PartitionSpec as P

NODE_1D = 8
CYCLES = 2
PLANES = 512
CELL = NODE_1D * NODE_1D
LANES = CYCLES * CELL
KEPT = CELL - NODE_1D
INSIDE = LANES - LANES // 4
CHANNEL_OF = (0, 1, 2, 8, 3, 4, 5, 6, 7)
STEP_DT = 0.002
RELAX_TIME = 0.02
MOBILITY = 0.3
LAYER_HEIGHT = 0.25
R_INNER = 1.0
ROWS = 16
BF = jnp.bfloat16
F32 = jnp.float32
MESH = pl.DeviceIdType.MESH


def cheb_table(points):
    nodes_xi = -np.cos(np.pi * np.arange(points) / (points - 1))
    weights = np.ones(points)
    weights[0] = 2.0
    weights[-1] = 2.0
    weights = weights * (-1.0) ** np.arange(points)
    identity = np.eye(points)
    spacing = nodes_xi[:, None] - nodes_xi[None, :] + identity
    matrix = weights[:, None] / weights[None, :] / spacing
    matrix = matrix * (1.0 - identity)
    matrix = matrix - identity * matrix.sum(axis=1)[:, None]
    return (nodes_xi, matrix)


def halves(table):
    high = np.asarray(table, np.float32).astype(ml_dtypes.bfloat16)
    low = (np.asarray(table, np.float64) - high.astype(np.float64)).astype(ml_dtypes.bfloat16)
    return high, low


def tables():
    n = np.arange(PLANES)
    k = np.arange(PLANES // 2)
    angle = (n[:, None] * k[None, :] % PLANES) * (2.0 * np.pi / PLANES)
    cosine = np.cos(angle) * np.sqrt(2.0 / PLANES)
    sine = np.sin(angle) * np.sqrt(2.0 / PLANES)
    cosine[:, 0] = PLANES**-0.5
    sine[:, 0] = (-1.0) ** n * PLANES**-0.5
    basis = np.stack([cosine, sine], axis=2).reshape(PLANES, PLANES)
    dbasis = np.stack([-k * sine, k * cosine], axis=2).reshape(PLANES, PLANES)
    forward = np.concatenate([basis, dbasis], axis=0)
    backward = np.concatenate([basis.T, -dbasis.T], axis=1)

    xi, matrix = cheb_table(NODE_1D)
    eye, eyes = np.eye(NODE_1D), np.eye(CYCLES)
    cell_r = np.kron(matrix.T * (2.0 * CYCLES), eye)
    cell_z = np.kron(eye, matrix.T * (2.0 / LAYER_HEIGHT))
    d_r, d_z = np.kron(eyes, cell_r), np.kron(eyes, cell_z)
    mean = np.eye(CYCLES * NODE_1D)
    for c in range(1, CYCLES):
        i = c * NODE_1D
        mean[i - 1 : i + 1, i - 1 : i + 1] = 0.5
    mean = np.kron(mean, eye)
    weight = np.ones(NODE_1D)
    weight[0] = weight[-1] = 0.5
    weight = np.tile(weight, CYCLES * NODE_1D)
    mean_w = mean * weight[None, :]
    both = np.concatenate([d_r, d_z], axis=1)
    grad = np.concatenate([d_r @ mean_w, d_z @ mean_w], axis=1)
    div = np.kron(np.eye(2), np.concatenate([cell_r, cell_z], axis=0))
    return (
        *halves(forward),
        *halves(backward),
        np.concatenate([*halves(both), *halves(grad), mean_w.astype(ml_dtypes.bfloat16)], axis=1),
        np.concatenate(halves(div), axis=1),
    )


def inverse_radius(lane):
    xi, _ = cheb_table(NODE_1D)
    radius = R_INNER + (np.arange(CYCLES)[:, None] + (xi[None, :] + 1.0) / 2.0) / CYCLES
    total = jnp.zeros(lane.shape, F32)
    for i, r in enumerate(radius.reshape(-1)):
        total = jnp.where(lane // NODE_1D == i, float(1.0 / r), total)
    return total


def split(x):
    high = x.astype(BF)
    return high, (x - high.astype(F32)).astype(BF)


def dot(a, b):
    return jnp.dot(a, b, preferred_element_type=F32)


def dot3(ah, al, bh, bl):
    return dot(ah, bh) + (dot(ah, bl) + dot(al, bh))


def stored_of_grid(o, grid):
    side = NODE_1D
    y = grid % side
    x = grid // side % side
    swapped = o // 4 % 2 == 1
    a = jnp.where(swapped, x, y)
    b = jnp.where(swapped, y, x)
    a = jnp.where(o % 2 == 1, side - 1 - a, a)
    b = jnp.where(o // 2 % 2 == 1, side - 1 - b, b)
    return a * side + b


def stored_index(orient_ref, layer, grid):
    cycle = grid // CELL
    place = jnp.zeros_like(grid)
    for c in range(CYCLES):
        o = orient_ref[layer * CYCLES + c]
        place = jnp.where(cycle == c, c * CELL + stored_of_grid(o, grid), place)
    return place


def square(m):
    a, b, c, d, e, f = m
    bb, cc, ee = b * b, c * c, e * e
    return (
        a * a + bb + cc,
        b * (a + d) + c * e,
        c * (a + f) + b * e,
        bb + d * d + ee,
        e * (d + f) + b * c,
        cc + ee + f * f,
    )


def product(m, n):
    a, b, c, d, e, f = m
    p, q, r, s, t, u = n
    return (
        a * p + b * q + c * r,
        a * q + b * s + c * t,
        a * r + b * t + c * u,
        b * q + d * s + e * t,
        b * r + d * t + e * u,
        c * r + e * t + f * u,
    )


def exponentials(psi):
    x = tuple(v * 0.125 for v in psi)
    x2 = square(x)
    x3 = product(x, x2)
    x4 = square(x2)
    even = [x2[i] * 0.5 + x4[i] * (1.0 / 24.0) for i in range(6)]
    for i in (0, 3, 5):
        even[i] = even[i] + 1.0
    odd = [x[i] + x3[i] * (1.0 / 6.0) for i in range(6)]
    plus = tuple(even[i] + odd[i] for i in range(6))
    minus = tuple(even[i] - odd[i] for i in range(6))
    for _ in range(3):
        plus, minus = square(plus), square(minus)
    return plus, minus


def first_cycle(f):
    wall = NODE_1D if f < 3 else 0
    start = f * KEPT - min(f, 3) * NODE_1D
    return start // LANES, start % LANES, wall, KEPT - wall


def field(ref, f, rows=slice(None)):
    return ref[rows, f * LANES : (f + 1) * LANES]


def main_kernel(
    n_dev, modes, fold,
    vel_ref, logc_ref, orient_in, wall_ref, fh_in, fl_in, bh_in, bl_in, node_in, div_in,
    vel_out, logc_out,
    fh_ref, fl_ref, bh_ref, bl_ref, node_ref, div_ref,
    orient_ref, out0_ref, out1_ref, packed, xv, xp, xh, xl, ph, pw, vv, vp, dp, proj, face_out, face_in, conv, mom, sth, stl, rh, rl,
    kept, back0, back1,
    local_sem, const_sem, vs_sem, vr_sem, ps_sem, pr_sem, fs_sem, fr_sem, bs_sem, br_sem,
):
    me = lax.axis_index("mode")
    up = lax.rem(me + 1, n_dev)
    down = lax.rem(me + n_dev - 1, n_dev)

    barrier = pltpu.get_barrier_semaphore()

    def greet(k, carry):
        pl.semaphore_signal(
            barrier, inc=1, device_id={"mode": lax.rem(me + k, n_dev)}, device_id_type=MESH
        )
        return carry

    lax.fori_loop(1, n_dev, greet, 0)
    early = [
        pltpu.make_async_copy(a, b, local_sem.at[i])
        for i, (a, b) in ((0, (logc_ref, logc_out)), (4, (orient_in, orient_ref)))
    ]
    for copy in early:
        copy.start()
    pl.semaphore_wait(barrier, n_dev - 1)

    side = n_dev // 2
    half_of = me // side

    def target(k):
        j = k // 2
        return lax.rem(half_of + lax.rem(k, 2), 2) * side + lax.rem(me + j, side)

    def columns(d):
        return pl.ds(pl.multiple_of(d * LANES, LANES), LANES)

    def every(do):
        def step(k, carry):
            do(k, target(k))
            return carry

        lax.fori_loop(1, n_dev, step, 0)

    def send_v(k, to, slot):
        return pltpu.make_async_remote_copy(
            src_ref=vel_ref.at[:, :, columns(to)],
            dst_ref=xv.at[slot],
            send_sem=vs_sem.at[k],
            recv_sem=vr_sem.at[slot],
            device_id={"mode": to},
            device_id_type=MESH,
        )

    def send_p(c, k, to, slot):
        return pltpu.make_async_remote_copy(
            src_ref=packed.at[c, to],
            dst_ref=xp.at[c, slot],
            send_sem=ps_sem.at[c, k],
            recv_sem=pr_sem.at[c, slot],
            device_id={"mode": to},
            device_id_type=MESH,
        )

    every(lambda k, to: send_v(k, to, me).start())
    own_v = pltpu.make_async_copy(vel_ref.at[:, :, columns(me)], xv.at[me], local_sem.at[1])
    own_v.start()
    load_v = pltpu.make_async_copy(vel_ref, vel_out, local_sem.at[5])
    load_v.start()
    loads = [
        pltpu.make_async_copy(a, b, const_sem.at[i])
        for i, (a, b) in enumerate(
            (
                (node_in, node_ref), (fh_in, fh_ref), (fl_in, fl_ref),
                (div_in, div_ref), (bh_in, bh_ref), (bl_in, bl_ref),
            )
        )
    ]
    for load in loads:
        load.start()

    lane = lax.broadcasted_iota(jnp.int32, (1, LANES), 1)
    lo = lane < CELL

    def swap(value):
        return pltpu.roll(value, CELL, 1)

    def pair_up(c, a, b):
        return jnp.where(lo, a, swap(b)) if c == 0 else jnp.where(lo, swap(a), b)

    for copy in early:
        copy.wait()
    own_p = [
        pltpu.make_async_copy(packed.at[c, me], xp.at[c, me], local_sem.at[2 + c]) for c in range(2)
    ]
    for c in range(2):

        def pack_psi(to, carry, c=c):
            at = columns(to)
            for p in range(3):
                packed[c, to, p] = pair_up(c, logc_out[2 * p, :, at], logc_out[2 * p + 1, :, at])
            return carry

        lax.fori_loop(0, n_dev, pack_psi, 0)
        if c == 0:
            every(lambda k, to: send_p(0, k, to, me).start())
        own_p[c].start()

    stored = lax.broadcasted_iota(jnp.int32, (LANES, LANES), 0)
    to_grid = jnp.where(stored_index(orient_ref, me, lane) == stored, 1.0, 0.0).astype(BF)

    half = PLANES // 2
    inv_r = inverse_radius(lane)
    for load in loads[:3]:
        load.wait()
    wide = 2 * LANES
    both_h, both_l, grad_h, grad_l = [node_ref.at[:, i * wide : (i + 1) * wide] for i in range(4)]
    mean_ref = node_ref.at[:, 4 * wide : 4 * wide + LANES]

    def vel_half(far):
        def step(k, carry):
            frm = target(2 * k + far)
            send_v(2 * k + far, frm, frm).wait_recv()
            return carry

        lax.fori_loop(1 - far, side, step, 0)
        which = lax.rem(half_of + far, 2)
        rows = pl.ds(pl.multiple_of(which * half, half), half)
        for f in range(3):
            high, low = split(xv[pl.ds(which * side, side), f].reshape(half, LANES))
            at = slice(f * LANES, (f + 1) * LANES)
            xh[rows, at] = dot(high, to_grid).astype(BF)
            xl[rows, at] = dot(low, to_grid).astype(BF)

        def velocity_block(i, carry):
            at = pl.ds(pl.multiple_of(i * half, half), half)
            total = dot3(fh_ref[at, rows], fl_ref[at, rows], xh[rows, :], xl[rows, :])
            vv[at, :] = vv[at, :] + total if far else total
            return carry

        lax.fori_loop(0, 4, velocity_block, 0)

    own_v.wait()
    vel_half(0)
    vel_half(1)

    def grad_block(i, carry):
        block = half // 2
        at = pl.ds(pl.multiple_of(i * block, block), block)
        dth_at = pl.ds(pl.multiple_of(PLANES + i * block, block), block)
        u = [field(vv, f, at) for f in range(3)]
        dth = [field(vv, f, dth_at) for f in range(3)]
        hoop = [(dth[0] - u[1]) * inv_r, (dth[1] + u[0]) * inv_r, dth[2] * inv_r]
        for f in range(3):
            uh, ul = split(u[f])
            both = dot3(uh, ul, grad_h[...], grad_l[...])
            hh, hl = split(hoop[f])
            g = (both[:, :LANES], dot(hh, mean_ref[...]) + dot(hl, mean_ref[...]), both[:, LANES:])
            for j in range(3):
                c = 3 * f + j
                proj[at, c * LANES : (c + 1) * LANES] = g[j]
        return carry

    lax.fori_loop(0, 4, grad_block, 0)

    groups = NODE_1D
    short = PLANES // groups

    def rolled(value, shift):
        return pltpu.roll(value, shift % LANES, 1) if shift % LANES else value

    def face_copy(slot, to):
        return pltpu.make_async_remote_copy(
            src_ref=face_out.at[slot],
            dst_ref=face_in.at[slot],
            send_sem=fs_sem.at[slot],
            recv_sem=fr_sem.at[slot],
            device_id={"mode": to},
            device_id_type=MESH,
        )

    faces = (face_copy(0, up), face_copy(1, down))
    for slot, start in ((0, NODE_1D - 1), (1, 0)):

        def pack(i, carry, slot=slot, start=start):
            at = pl.ds(pl.multiple_of(i * 64, 64), 64)
            total = jnp.zeros((64, LANES), F32)
            for c in range(groups):
                total = jnp.where(lane % groups == c, rolled(field(proj, c, at), c - start), total)
            face_out[slot, at, :] = total
            return carry

        lax.fori_loop(0, PLANES // 64, pack, 0)
        total = jnp.zeros((short, LANES), F32)
        for b in range(groups):
            moved = field(proj, 8, slice(b * short, (b + 1) * short))
            total = jnp.where(lane % groups == b, rolled(moved, b - start), total)
        face_out[slot, PLANES:, :] = total
        faces[slot].start()

    for face in faces:
        face.wait()
    def far_or_near(far):
        def step(k, carry):
            send_p(1, 2 * k + far, target(2 * k + far), me).start()
            return carry

        lax.fori_loop(1 - far, side, step, 0)

    far_or_near(1)

    def wall_lanes(layer):
        lead, trail = lane // NODE_1D % NODE_1D, lane % NODE_1D
        code = jnp.where(lo, orient_ref[layer * CYCLES], orient_ref[layer * CYCLES + 1])
        flipped_a = jnp.where(code % 2 == 1, NODE_1D - 1 - lead, lead)
        flipped_b = jnp.where(code // 2 % 2 == 1, NODE_1D - 1 - trail, trail)
        x = jnp.where(code // 4 % 2 == 1, flipped_a, flipped_b)
        inner = jnp.logical_and(lo, x == 0)
        outer = jnp.logical_and(jnp.logical_not(lo), x == NODE_1D - 1)
        return inner, jnp.logical_or(inner, outer)

    top = lane % NODE_1D == NODE_1D - 1
    low_rows = lane % NODE_1D == 0

    def unpacked(from_down, from_up, c):
        below = rolled(from_down, -c)
        above = rolled(from_up, NODE_1D - 1 - c)
        return jnp.where(top, above, jnp.where(low_rows, below, 0.0))

    for b in range(groups):

        def face_block(i, carry, b=b):
            start = pl.multiple_of(b * short + i * ROWS, ROWS)
            at = pl.ds(start, ROWS)
            nine = pl.ds(pl.multiple_of(PLANES + i * ROWS, ROWS), ROWS)
            down_face, up_face = face_in[0, at, :], face_in[1, at, :]
            g = [field(proj, c, at) + unpacked(down_face, up_face, c) for c in range(8)]
            g.append(field(proj, 8, at) + unpacked(face_in[0, nine, :], face_in[1, nine, :], b))
            for c in range(9):
                proj[at, c * LANES : (c + 1) * LANES] = g[c]
            u = [field(vv, f, at) for f in range(3)]
            for f in range(3):
                total = g[3 * f] * u[0] + g[3 * f + 1] * u[1] + g[3 * f + 2] * u[2]
                conv[at, f * LANES : (f + 1) * LANES] = -total
            return carry

        lax.fori_loop(0, short // ROWS, face_block, 0)

    def put_rate(at, f, value):
        high, low = split(value)
        rh[at, f * LANES : (f + 1) * LANES] = high
        rl[at, f * LANES : (f + 1) * LANES] = low

    share = PLANES // 4
    per = share // modes
    quarter = me // per
    backs, outs = (back0, back1), (out0_ref, out1_ref)
    diag = (0, 3, 5)

    def give(c, to, slot):
        return pltpu.make_async_remote_copy(
            src_ref=backs[c].at[to],
            dst_ref=outs[c].at[slot],
            send_sem=bs_sem.at[c, to],
            recv_sem=br_sem.at[c, slot],
            device_id={"mode": to},
            device_id_type=MESH,
        )

    def quarters(value):
        return value.reshape(per, 4, modes // 4, LANES)

    def cycle_part(c):
        in_c = lo if c == 0 else jnp.logical_not(lo)
        o = orient_ref[me * CYCLES + c]
        place = stored_of_grid(o, lane) + lane // CELL * CELL
        cell_grid = jnp.where(place == stored, 1.0, 0.0).astype(BF)

        def conf_half(far):
            which = lax.rem(half_of + far, 2)
            rows = pl.ds(pl.multiple_of(which * half, half), half)
            for p in range(3):
                high, low = split(xp[c, pl.ds(which * side, side), p].reshape(half, LANES))
                at = slice(p * LANES, (p + 1) * LANES)
                ph[rows, at] = dot(high, cell_grid).astype(BF)
                pw[rows, at] = dot(low, cell_grid).astype(BF)

            def conf_block(i, carry):
                at = pl.ds(pl.multiple_of(i * half, half), half)
                total = dot3(fh_ref[at, rows], fl_ref[at, rows], ph[rows, :], pw[rows, :])
                vp[at, :] = vp[at, :] + total if far else total
                return carry

            lax.fori_loop(0, 4, conf_block, 0)

        def recv_half(far):
            def step(k, carry):
                frm = target(2 * k + far)
                send_p(c, 2 * k + far, frm, frm).wait_recv()
                return carry

            lax.fori_loop(1 - far, side, step, 0)

        own_p[c].wait()
        recv_half(0)
        conf_half(0)
        recv_half(1)
        if c == 0:
            far_or_near(0)
        conf_half(1)

        def deriv_block(i, carry):
            at = pl.ds(pl.multiple_of(i * half, half), half)
            for p in range(3):
                high, low = split(field(vp, p, at))
                dp[at, 2 * p * LANES : (2 * p + 2) * LANES] = dot3(high, low, both_h[...], both_l[...])
            return carry

        lax.fori_loop(0, 2, deriv_block, 0)

        def local_block(i, carry):
            at = pl.ds(pl.multiple_of(i * ROWS, ROWS), ROWS)
            dth_at = pl.ds(pl.multiple_of(PLANES + i * ROWS, ROWS), ROWS)
            u_r, u_t, u_z = [field(vv, f, at) for f in range(3)]
            spin = u_t * inv_r
            ur2, spin2, uz2 = [jnp.where(in_c, v, swap(v)) for v in (u_r, spin, u_z)]
            psi, advect = [], []
            for p in range(3):
                value = field(vp, p, at)
                other = swap(value)
                for h in range(2):
                    psi.append(jnp.where(in_c, value if h == c else other, 0.0))
                advect.append(
                    ur2 * field(dp, 2 * p, at) + spin2 * field(vp, p, dth_at) + uz2 * field(dp, 2 * p + 1, at)
                )
            conform, inverse = exponentials(psi)
            g = [field(proj, j, at) for j in range(9)]
            wa, wb, wc = 0.5 * (g[1] - g[3]), 0.5 * (g[2] - g[6]), 0.5 * (g[5] - g[7])
            wa2 = wa + spin
            r0 = [wa2 * psi[1] + wb * psi[2], wa2 * psi[3] + wb * psi[4], wa2 * psi[4] + wb * psi[5]]
            r1 = [wc * psi[2] - wa2 * psi[0], wc * psi[4] - wa2 * psi[1], wc * psi[5] - wa2 * psi[2]]
            r2 = [-(wb * psi[j] + wc * psi[k]) for j, k in ((0, 1), (1, 3), (2, 4))]
            rate = [
                2.0 * (r0[0] + g[0]),
                r0[1] + r1[0] + (g[1] + g[3]),
                r0[2] + r2[0] + (g[2] + g[6]),
                2.0 * (r1[1] + g[4]),
                r1[2] + r2[1] + (g[5] + g[7]),
                2.0 * (r2[2] + g[8]),
            ]
            for m in range(6):
                unit = 1.0 if m in diag else 0.0
                rate[m] = rate[m] - (1.0 / RELAX_TIME) * (
                    unit - inverse[m] + MOBILITY * (conform[m] - 2.0 * unit + inverse[m])
                )
            stress = [conform[m] - 1.0 if m in diag else conform[m] for m in range(6)]
            for f, (m, n) in enumerate(((0, 2), (1, 4), (2, 5))):
                high, low = split(pair_up(c, stress[m], stress[n]))
                sth[at, f * LANES : (f + 1) * LANES] = high
                stl[at, f * LANES : (f + 1) * LANES] = low
            hoop = [stress[m] * inv_r for m in (1, 3, 4)]
            base = [
                field(conv, 0, at) + (stress[0] - stress[3]) * inv_r,
                field(conv, 1, at) + 2.0 * hoop[0],
                field(conv, 2, at) + stress[2] * inv_r,
            ]
            mom[at, :LANES] = pair_up(c, base[0], base[1])
            mom[at, LANES:] = pair_up(c, base[2], rate[5]) - jnp.where(lo, 0.0, advect[2])
            put_rate(at, 2, pair_up(c, rate[0], rate[1]) - advect[0])
            put_rate(at, 3, pair_up(c, rate[2], rate[3]) - advect[1])
            first = rate[4] if c == 0 else swap(rate[4])
            put_rate(at, 4, jnp.where(lo, first - advect[2], 0.0))
            put_rate(at, 5, pair_up(c, hoop[0], hoop[1]))
            last = hoop[2] if c == 0 else swap(hoop[2])
            put_rate(at, 6, jnp.where(lo, last, 0.0))
            return carry

        lax.fori_loop(0, PLANES // ROWS, local_block, 0)
        if c == 0:
            loads[3].wait()

        def div_block(i, carry):
            at = pl.ds(pl.multiple_of(i * half, half), half)
            for f, cols in enumerate((slice(0, wide), slice(wide, 3 * LANES))):
                depth = cols.stop - cols.start
                total = dot3(
                    sth[at, cols], stl[at, cols], div_ref[:depth, :LANES], div_ref[:depth, LANES:]
                )
                put_rate(at, f, field(mom, f, at) + total)
            return carry

        lax.fori_loop(0, 2, div_block, 0)
        if c == 0:
            for load in loads[4:]:
                load.wait()

        def back_block(step, carry):
            pair = lax.rem(quarter // 2 + 1 + step // 2, 2)
            i = pair * 2 + lax.rem(quarter + step + step // 2, 2)
            at = pl.ds(pl.multiple_of(i * share, share), share)
            dst = pl.ds(i * per, per)
            cols, hoops = slice(0, wide), slice(5 * LANES, 7 * LANES)
            total = dot3(bh_ref[at, :PLANES], bl_ref[at, :PLANES], rh[:, cols], rl[:, cols])
            total += dot3(bh_ref[at, PLANES:], bl_ref[at, PLANES:], rh[:, hoops], rl[:, hoops])
            coefs = [total[:, :LANES], total[:, LANES:]]
            cols = slice(wide, 5 * LANES)
            total = dot3(bh_ref[at, :PLANES], bl_ref[at, :PLANES], rh[:, cols], rl[:, cols])
            coefs += [total[:, j * LANES : (j + 1) * LANES] for j in range(3)]
            if c == 0:
                blocks = [None] * 4
                for f in range(9):
                    b, inside, wall, width = first_cycle(f)
                    moved = rolled(coefs[f // 2], inside - wall - f % 2 * CELL)
                    blocks[b] = moved if inside == 0 else jnp.where(lane < inside, blocks[b], moved)
                    if inside + width > LANES:
                        blocks[b + 1] = moved
                for p in range(4):
                    if not fold:
                        back0[dst, p] = blocks[p].reshape(per, modes, LANES)
                    elif p < 3:
                        back0[dst, 4 * p : 4 * p + 4] = quarters(blocks[p])
                    else:
                        value = quarters(blocks[p])
                        for j in range(3):
                            extra = quarters(rolled(blocks[p], INSIDE - j * (LANES // 4)))[:, 3]
                            back0[dst, 12 + j] = jnp.where(lane < INSIDE, value[:, j], extra)
                for p in range(5):
                    kept[p, at, :] = coefs[p]
            else:
                for p in range(5):
                    face = rolled(kept[p, at, :], NODE_1D - CELL)
                    coefs[p] = jnp.where(lane % CELL < NODE_1D, 0.5 * (coefs[p] + face), coefs[p])
                for p in range(5):
                    if not fold:
                        back1[dst, p] = coefs[p].reshape(per, modes, LANES)
                    elif p < 4:
                        back1[dst, 4 * p : 4 * p + 4] = quarters(coefs[p])
                    else:
                        value, upper = quarters(coefs[p]), quarters(swap(coefs[p]))
                        for j in range(2):
                            back1[dst, 16 + j] = jnp.where(lo, value[:, j], upper[:, 2 + j])

            def give_start(j, inner):
                to = i * per + lax.rem(me + j, per)

                @pl.when(to != me)
                def _():
                    give(c, to, me).start()

                return inner

            lax.fori_loop(0, per, give_start, 0)
            return carry

        lax.fori_loop(0, 4, back_block, 0)

    cycle_part(0)
    cycle_part(1)
    own = [pltpu.make_async_copy(backs[c].at[me], outs[c].at[me], local_sem.at[c]) for c in range(2)]
    for copy in own:
        copy.start()
    load_v.wait()
    mode_ids = me * modes + lax.broadcasted_iota(jnp.int32, (modes, 1), 0)
    speed = jnp.where(mode_ids == 0, wall_ref[0], 0.0)

    def set_walls(layer, carry):
        inner, on_wall = wall_lanes(layer)
        at = columns(layer)
        for c in range(3):
            wall = jnp.where(inner, speed, 0.0) if c == 1 else 0.0
            vel_out[c, :, at] = jnp.where(on_wall, wall, vel_out[c, :, at])
        return carry

    lax.fori_loop(0, n_dev, set_walls, 0)
    every(lambda k, to: send_v(k, to, me).wait_send())
    for c in range(2):
        every(lambda k, to, c=c: send_p(c, k, to, me).wait_send())
    for copy in own:
        copy.wait()

    edge = jnp.logical_or(top, low_rows)
    weight = jnp.where(edge, 0.5 * STEP_DT, STEP_DT)
    joined = jnp.logical_and(lane >= CELL, lane < CELL + NODE_1D)

    def first_fields(at):
        if not fold:
            blocks = [out0_ref[at, p] for p in range(4)]
        else:
            blocks = [out0_ref[at, 4 * p : 4 * p + 4].reshape(modes, LANES) for p in range(3)]
            units = [out0_ref[at, 12 + j] for j in range(3)]
            piece = lane // (LANES // 4)
            outer = [rolled(units[j], (j + 1) * (LANES // 4)) for j in range(3)]
            units.append(jnp.where(piece == 0, outer[0], jnp.where(piece == 1, outer[1], outer[2])))
            blocks.append(jnp.concatenate(units, axis=0))
        fields = []
        for f in range(9):
            b, inside, wall, width = first_cycle(f)
            value = rolled(blocks[b], wall - inside)
            if inside + width > LANES:
                value = jnp.where(lane < wall + LANES - inside, value, rolled(blocks[b + 1], wall - inside))
            fields.append(value)
        return fields

    def second_fields(at):
        fields = []
        for f in range(9):
            p = f // 2
            if not fold:
                value = rolled(out1_ref[at, p], (f + 1) % 2 * CELL)
            elif p < 4:
                value = out1_ref[at, 4 * p : 4 * p + 4].reshape(modes, LANES)
                value = rolled(value, (f + 1) % 2 * CELL)
            else:
                value = out1_ref[at, 16:18].reshape(modes // 2, LANES)
                value = jnp.concatenate([rolled(value, CELL), value], axis=0)
            fields.append(value)
        return fields

    many = modes % 8 == 0

    def add_cycle(c):
        here = lane >= CELL if c else lane < KEPT

        def add_layer(order, carry):
            far = order // side
            m = lax.rem(order, side)
            local = lax.rem(me, side)
            near_by = lax.rem(local // per + m // per, 2) * per + lax.rem(local + n_dev * per - m, per)
            frm = lax.rem(half_of + far, 2) * side + near_by

            @pl.when(order > 0)
            def _():
                give(c, frm, frm).wait_recv()
                give(c, frm, me).wait_send()

            fields = [weight * v for v in (second_fields if c else first_fields)(frm)]
            step = NODE_1D - 1
            cats = [jnp.concatenate(split(v), axis=1) for v in ([jnp.concatenate(fields, axis=0)] if many else fields)]
            layers = [lax.rem(frm + ahead, n_dev) for ahead in (0, 1, n_dev - 1)]
            hots = []
            for layer, shift, only in zip(layers, (0, -step, step), (None, top, low_rows)):
                valid = [v if only is None else jnp.logical_and(v, only) for v in (here, joined)]
                place = jnp.where(valid[0], stored_index(orient_ref, layer, lane + shift), -1)
                hit = place == stored
                if c:
                    twin = jnp.where(valid[1], stored_index(orient_ref, layer, lane + shift - NODE_1D), -1)
                    hit = jnp.logical_or(hit, twin == stored)
                hot = jnp.where(hit, 1.0, 0.0).astype(BF)
                hots.append(jnp.concatenate([hot, hot], axis=1))
            hots = jnp.concatenate(hots, axis=0)
            sums = [
                lax.dot_general(v, hots, (((1,), (1,)), ((), ())), preferred_element_type=F32) for v in cats
            ]
            for j, layer in enumerate(layers):
                _, on_wall = wall_lanes(layer)
                at = columns(layer)
                cols = slice(j * LANES, (j + 1) * LANES)
                for f in range(9):
                    total = sums[0][f * modes : (f + 1) * modes, cols] if many else sums[f][:, cols]
                    to = CHANNEL_OF[f]
                    if to < 3:
                        vel_out[to, :, at] += jnp.where(on_wall, 0.0, total)
                    else:
                        logc_out[to - 3, :, at] += total
            return carry

        lax.fori_loop(0, n_dev, add_layer, 0)

    add_cycle(0)
    add_cycle(1)


def store_kernel(vel_ref, logc_ref, vel_out, logc_out, sem):
    copies = [pltpu.make_async_copy(vel_ref.at[c], vel_out.at[c], sem.at[c]) for c in range(3)]
    copies += [pltpu.make_async_copy(logc_ref.at[c], logc_out.at[c], sem.at[3 + c]) for c in range(6)]
    for copy in copies:
        copy.start()
    for copy in copies:
        copy.wait()


def body(velocity, log_conf, orientation, wall_speed):
    n_dev = lax.axis_size("mode")
    modes = velocity.shape[1]
    fold = modes % 32 == 0
    head = (15, modes // 4, LANES) if fold else (4, modes, LANES)
    tail = (18, modes // 4, LANES) if fold else (5, modes, LANES)
    consts = [jnp.asarray(t) for t in tables()]
    hbm = pl.BlockSpec(memory_space=pltpu.HBM)
    vmem = pl.BlockSpec(memory_space=pltpu.VMEM)
    dma = pltpu.SemaphoreType.DMA
    face_rows = PLANES + PLANES * CYCLES * NODE_1D // LANES
    held = pl.pallas_call(
        functools.partial(main_kernel, n_dev, modes, fold),
        out_shape=(
            jax.ShapeDtypeStruct(velocity.shape, F32),
            jax.ShapeDtypeStruct(log_conf.shape, F32),
        ),
        in_specs=[hbm] * 3 + [pl.BlockSpec(memory_space=pltpu.SMEM)] + [hbm] * len(consts),
        out_specs=(vmem, vmem),
        scratch_shapes=[pltpu.VMEM(t.shape, t.dtype) for t in consts]
        + [
            pltpu.SMEM(orientation.shape, jnp.int32),
            pltpu.VMEM((n_dev, *head), F32),
            pltpu.VMEM((n_dev, *tail), F32),
            pltpu.VMEM((2, n_dev, 3, modes, LANES), F32),
            pltpu.VMEM((n_dev, 3, modes, LANES), F32),
            pltpu.VMEM((2, n_dev, 3, modes, LANES), F32),
            pltpu.VMEM((PLANES, 3 * LANES), BF),
            pltpu.VMEM((PLANES, 3 * LANES), BF),
            pltpu.VMEM((PLANES, 3 * LANES), BF),
            pltpu.VMEM((PLANES, 3 * LANES), BF),
            pltpu.VMEM((2 * PLANES, 3 * LANES), F32),
            pltpu.VMEM((2 * PLANES, 3 * LANES), F32),
            pltpu.VMEM((PLANES, 6 * LANES), F32),
            pltpu.VMEM((PLANES, 9 * LANES), F32),
            pltpu.VMEM((2, face_rows, LANES), F32),
            pltpu.VMEM((2, face_rows, LANES), F32),
            pltpu.VMEM((PLANES, 3 * LANES), F32),
            pltpu.VMEM((PLANES, 2 * LANES), F32),
            pltpu.VMEM((PLANES, 3 * LANES), BF),
            pltpu.VMEM((PLANES, 3 * LANES), BF),
            pltpu.VMEM((PLANES, 7 * LANES), BF),
            pltpu.VMEM((PLANES, 7 * LANES), BF),
            pltpu.VMEM((5, PLANES, LANES), F32),
            pltpu.VMEM((n_dev, *head), F32),
            pltpu.VMEM((n_dev, *tail), F32),
            dma((6,)),
            dma((len(consts),)),
            dma((n_dev,)),
            dma((n_dev,)),
            dma((2, n_dev)),
            dma((2, n_dev)),
            dma((2,)),
            dma((2,)),
            dma((2, n_dev)),
            dma((2, n_dev)),
        ],
        compiler_params=pltpu.CompilerParams(
            collective_id=0, has_side_effects=True, vmem_limit_bytes=36 * 2**20
        ),
        name="fields",
    )(
        *[pltpu.with_memory_space_constraint(v, pltpu.HBM) for v in (velocity, log_conf, orientation)],
        wall_speed,
        *[pltpu.with_memory_space_constraint(v, pltpu.HBM) for v in consts],
    )

    free = pl.BlockSpec(memory_space=pl.ANY)
    return pl.pallas_call(
        store_kernel,
        out_shape=(
            jax.ShapeDtypeStruct(velocity.shape, F32),
            jax.ShapeDtypeStruct(log_conf.shape, F32),
        ),
        in_specs=[vmem, vmem],
        out_specs=(free, free),
        scratch_shapes=[dma((9,))],
        compiler_params=pltpu.CompilerParams(vmem_limit_bytes=8 * 2**20),
        name="store",
    )(*held)


def solution(mesh):
    in_specs = (P("ens", "mode", None), P("ens", "mode", None), P(), P("ens"))
    out_specs = (P("ens", "mode", None), P("ens", "mode", None))
    return jax.shard_map(body, mesh=mesh, in_specs=in_specs, out_specs=out_specs, check_vma=False)
```
